32 devices in a mesh: segment: 4 (over y, x), patch: 8 (over z, core).
Axes of the slice: x: 2, y: 2, z: 4, core: 2. Of those that a mesh axis runs over, the one named last changes fastest.
Arguments:
- features: bfloat16 [4, 2, 320, 32, 128], P('segment', None, None, 'patch'), may hold values from -48 to 48, as said below
- latent: float32 [2, 4, 32, 128], P(None, None, 'patch'), may hold values from -48 to 48
- plan_pos: int32 [2], replicated, may hold values from 0 to 9
- blocks_used: int32 [4], P('segment'), may hold values from 1 to 2, as said below
- conv1_w: bfloat16 [4, 2, 9, 320, 320], P('segment'), may hold values from -0.109375 to 0.109375
- conv2_w: bfloat16 [4, 2, 9, 320, 320], P('segment'), may hold values from -0.109375 to 0.109375
- norm_gain: float32 [4, 2, 2, 320], P('segment'), may hold values from 0.25 to 1.75
- norm_shift: float32 [4, 2, 2, 320], P('segment'), may hold values from -3 to 3
- in_w: bfloat16 [9, 320, 4], replicated, may hold values from -1 to 1
- head_w: bfloat16 [9, 4, 320], replicated, may hold values from -0.109375 to 0.109375
- head_gain: float32 [320], replicated, may hold values from 0.25 to 1.75
- head_shift: float32 [320], replicated, may hold values from -3 to 3
Outputs:
- latent_out: float32 [2, 4, 32, 128], P(None, None, 'patch', 'segment')
- features_out: bfloat16 [4, 2, 320, 32, 128], P('segment', None, None, 'patch')
The draws below stay inside these ranges and needn't reach their ends.
Inputs may be any that keep to these rules, and one draw needn't show every extreme that they name: `features`: every entry lies within the range; row magnitudes vary over the rows. `blocks_used`: each section holds 1 or 2 blocks; both counts occur.
All inputs are finite; a program needn't handle non-finite values.
Results may differ from the reference program's by a relative error of at most 0.0075.
Values may be sent and summed in bfloat16 or wider, within the bound.
No kernel may reach another device: no remote copies, remote signals or barrier semaphores. Data moves between devices by JAX's collectives and lax.ppermute only.
A program may use at most 64 MiB of HBM per device.

```python
import jax
import jax.numpy as jnp
from jax import lax

C = 320
GROUPS = 32
LAT = 4
BLOCKS = 2
STEPS = 2
SCHED = 12
COLS = 128
MB = 2
SEGMENTS = 4
NR = 32


def ramp_field(key, lead_shape, chan_count):
    full_shape = lead_shape + (chan_count, NR, COLS)
    row_pos = jnp.arange(NR, dtype=jnp.float32) / max(NR - 1, 1)
    row_scale = 0.3 * jnp.exp(jnp.log(10.0) * row_pos)
    chan_scale = jnp.exp(jax.random.uniform(jax.random.fold_in(key, 1), lead_shape + (chan_count, 1, 1), minval=-0.69, maxval=0.69))
    col_scale = jnp.exp(jax.random.uniform(jax.random.fold_in(key, 2), (COLS,), minval=-0.69, maxval=0.69))
    base_draw = jnp.clip(jax.random.normal(jax.random.fold_in(key, 3), full_shape), -4.0, 4.0)
    return base_draw * chan_scale * row_scale[:, None] * col_scale


def draw_features(key, part):
    return ramp_field(key, (SEGMENTS, MB), C).astype(jnp.bfloat16)


def draw_latent(key, part):
    return ramp_field(key, (MB,), LAT).astype(jnp.float32)


def draw_blocks_used(key, part):
    counts_run = jax.random.randint(jax.random.fold_in(key, 11), (SEGMENTS,), 1, 3)
    first_pos = jax.random.randint(jax.random.fold_in(key, 12), (), 0, SEGMENTS)
    second_pos = (first_pos + 1 + jax.random.randint(jax.random.fold_in(key, 13), (), 0, SEGMENTS - 1)) % SEGMENTS
    counts_run = counts_run.at[first_pos].set(2)
    counts_run = counts_run.at[second_pos].set(1)
    return counts_run.astype(jnp.int32)


def levels(rng, dims, split, low, largest):
    level = 1.0
    for dim, blocks in split:
        draws = jax.random.uniform(jax.random.fold_in(jax.random.fold_in(rng, 6), dim), (blocks,), jnp.float32, low / len(split), largest / len(split))
        level = level * jnp.repeat(jnp.exp(draws), dims[dim] // blocks).reshape((-1,) + (1,) * (len(dims) - 1 - dim))
    return level


def normal_values(rng, dims, width, limit, split=(), kind=jnp.bfloat16):
    result = width * jax.random.normal(rng, dims, jnp.float32)
    if split:
        result = result * levels(rng, dims, split, -0.22, 0.18)
    return jnp.clip(result, -limit, limit).astype(kind)


def setup_inputs(seed: int = 0) -> dict:
    streams_of = jax.random.split(jax.random.key(seed), 13)
    return {
        "features": draw_features(jax.random.fold_in(streams_of[12], 71), 0),
        "latent": draw_latent(jax.random.fold_in(streams_of[12], 71), 0),
        "plan_pos": jax.random.randint(streams_of[2], (MB,), 0, SCHED - 2).astype(jnp.int32),
        "blocks_used": draw_blocks_used(jax.random.fold_in(streams_of[12], 71), 0),
        "conv1_w": normal_values(streams_of[4], (SEGMENTS, BLOCKS, 9, C, C), (9 * C) ** -0.5, 0.109375, ((0, 4),)),
        "conv2_w": normal_values(streams_of[5], (SEGMENTS, BLOCKS, 9, C, C), (9 * C) ** -0.5, 0.109375, ((0, 4),)),
        "norm_gain": jnp.clip(1.0 + 0.15 * jax.random.normal(streams_of[6], (SEGMENTS, BLOCKS, 2, C), jnp.float32), 0.25, 1.75),
        "norm_shift": normal_values(streams_of[7], (SEGMENTS, BLOCKS, 2, C), 0.5, 3.0, ((0, 4),), jnp.float32),
        "in_w": normal_values(streams_of[8], (9, C, LAT), (9 * LAT) ** -0.5, 1.0),
        "head_w": normal_values(streams_of[9], (9, LAT, C), (9 * C) ** -0.5, 0.109375),
        "head_gain": jnp.clip(1.0 + 0.15 * jax.random.normal(streams_of[10], (C,), jnp.float32), 0.25, 1.75),
        "head_shift": normal_values(streams_of[11], (C,), 0.5, 3.0, (), jnp.float32),
    }


epsilon = 1e-05
sigma_top = 3.0
sigma_low = 0.1
rho_power = 7.0

def sigma_at(position):
    fraction = position.astype(jnp.float32) / (SCHED - 1)
    top_root = sigma_top ** (1.0 / rho_power)
    low_root = sigma_low ** (1.0 / rho_power)
    return (top_root + fraction * (low_root - top_root)) ** rho_power

def group_norm_silu(values, gain, shift):
    batch_size, chan_count, height, col_count = values.shape
    grouped = values.reshape(batch_size, GROUPS, chan_count // GROUPS, height, col_count)
    center = lax.optimization_barrier(jnp.mean(grouped, axis=(2, 3, 4), keepdims=True))
    spread = lax.optimization_barrier(jnp.mean(jnp.square(grouped - center), axis=(2, 3, 4), keepdims=True))
    normed = ((grouped - center) / jnp.sqrt(spread + epsilon)).reshape(values.shape)
    normed = normed * gain[None, :, None, None] + shift[None, :, None, None]
    return jax.nn.silu(normed).astype(jnp.bfloat16)

def conv_same(inputs, kernel):
    padded = jnp.pad(inputs.astype(jnp.float32), ((0, 0), (0, 0), (1, 1), (1, 1)))
    kernel_wide = kernel.astype(jnp.float32)
    height, col_count = (inputs.shape[2], inputs.shape[3])
    accum = jnp.zeros((inputs.shape[0], kernel.shape[1], height, col_count), jnp.float32)
    for tap_no in range(9):
        row_off, col_off = (tap_no // 3, tap_no % 3)
        window = padded[:, :, row_off:row_off + height, col_off:col_off + col_count]
        accum = accum + jnp.einsum('oi,bihw->bohw', kernel_wide[tap_no], window)
    return accum

def resnet_unit(hidden, kern_one, kern_two, gain_pair, shift_pair):
    first_act = group_norm_silu(hidden.astype(jnp.float32), gain_pair[0], shift_pair[0])
    middle = conv_same(first_act, kern_one)
    second = group_norm_silu(middle, gain_pair[1], shift_pair[1])
    return (hidden.astype(jnp.float32) + conv_same(second, kern_two)).astype(jnp.bfloat16)

def reference(features, latent, plan_pos, blocks_used, conv1_w, conv2_w, norm_gain, norm_shift, in_w, head_w, head_gain, head_shift):
    for step_no in range(STEPS):
        head_input = group_norm_silu(features[SEGMENTS - 1].astype(jnp.float32), head_gain, head_shift)
        noise_pred = conv_same(head_input, head_w)
        position = (plan_pos + step_no).astype(jnp.int32)
        sigma_now = sigma_at(position)
        sigma_next = sigma_at(position + 1)
        latent = latent + (sigma_next - sigma_now)[:, None, None, None] * noise_pred
        scaled = (latent / jnp.sqrt(sigma_next * sigma_next + 1.0)[:, None, None, None]).astype(jnp.bfloat16)
        entry_rows = conv_same(scaled, in_w).astype(jnp.bfloat16)
        outputs = []
        for segment_no in range(SEGMENTS):
            source = entry_rows if segment_no == 0 else features[segment_no - 1]
            after_one = resnet_unit(source, conv1_w[segment_no, 0], conv2_w[segment_no, 0], norm_gain[segment_no, 0], norm_shift[segment_no, 0])
            after_two = resnet_unit(after_one, conv1_w[segment_no, 1], conv2_w[segment_no, 1], norm_gain[segment_no, 1], norm_shift[segment_no, 1])
            outputs.append(jnp.where(blocks_used[segment_no] >= 2, after_two, after_one))
        features = jnp.stack(outputs)
    return (latent, features)
```

```python
import functools

import jax
import jax.numpy as jnp
from jax import lax
from jax.experimental import pallas as pl
from jax.experimental.pallas import tpu as pltpu
from jax.sharding import PartitionSpec as P

GROUPS = 32
STEPS = 2
SCHED = 12
CORES = 2

epsilon = 1e-05
sigma_top = 3.0
sigma_low = 0.1
rho_power = 7.0

F32 = jnp.float32
BF16 = jnp.bfloat16
VMEM_LIMIT = 48 * 1024 * 1024


def sigma_at(position):
    fraction = position.astype(F32) / (SCHED - 1)
    top_root = sigma_top ** (1.0 / rho_power)
    low_root = sigma_low ** (1.0 / rho_power)
    return (top_root + fraction * (low_root - top_root)) ** rho_power


def dot(a, b):
    return lax.dot_general(a, b, (((1,), (0,)), ((), ())), preferred_element_type=F32)


def split3(x):
    hi = x.astype(BF16)
    rest = x - hi.astype(F32)
    mid = rest.astype(BF16)
    lo = (rest - mid.astype(F32)).astype(BF16)
    return hi, mid, lo


def group_sum(x, gather):
    parts = jnp.concatenate(split3(x), axis=0)
    return jnp.sum(dot(gather, parts), axis=1, keepdims=True)


def expand(x, spread):
    return dot(spread, jnp.concatenate(split3(x), axis=0))


def local_stats(tiles, gather, spread, count):
    total = tiles[0]()
    for tile in tiles[1:]:
        total = total + tile()
    mean = group_sum(total, gather) / count
    center = expand(jnp.broadcast_to(mean, (GROUPS, 128)), spread)
    square = None
    for tile in tiles:
        dev = tile() - center
        square = dev * dev if square is None else square + dev * dev
    return mean, group_sum(square, gather)


def encode_stats(mean, square):
    lane = lax.broadcasted_iota(jnp.int32, (GROUPS, 128), 1) // 16
    out = jnp.zeros((GROUPS, 128), F32)
    for slot, part in enumerate(split3(mean) + split3(square)):
        out = jnp.where(lane == slot, part.astype(F32), out)
    return out.astype(BF16)


def decode_stats(message):
    wide = message.astype(F32)
    take = [wide[:, 16 * k : 16 * k + 1] for k in range(6)]
    return take[0] + take[1] + take[2], take[3] + take[4] + take[5]


def combine_stats(messages, count):
    pairs = [decode_stats(m) for m in messages]
    mean = sum(p[0] for p in pairs) / len(pairs)
    square = sum(p[1] for p in pairs)
    for p in pairs:
        square = square + count * (p[0] - mean) * (p[0] - mean)
    return mean, lax.rsqrt(square / (count * len(pairs)) + epsilon)


def channel_moments(mean, scale, spread):
    both = jnp.concatenate(
        [jnp.broadcast_to(mean, (GROUPS, 128)), jnp.broadcast_to(scale, (GROUPS, 128))], axis=1
    )
    wide = expand(both, spread)
    return wide[:, :128], wide[:, 128:]


def silu(v):
    half = 0.5 * v
    return half + half * jnp.tanh(half)


def shift_cols(t):
    lane = lax.broadcasted_iota(jnp.int32, t.shape, 1)
    before = jnp.where(lane == 0, 0.0, pltpu.roll(t, 1, 1))
    after = jnp.where(lane == 127, 0.0, pltpu.roll(t, 127, 1))
    return before, after


def fill_patches(tiles, center, scale, shift, flags, patches):
    chans = center.shape[0]
    for r, tile in enumerate(tiles):
        t = silu((tile() - center) * scale + shift)
        if r == 0:
            t = jnp.where(flags[0] > 0, t, 0.0)
        if r == len(tiles) - 1:
            t = jnp.where(flags[1] > 0, t, 0.0)
        before, after = shift_cols(t)
        lanes = pl.ds(r * 128, 128)
        patches[pl.ds(0, chans), lanes] = before.astype(BF16)
        patches[pl.ds(chans, chans), lanes] = t.astype(BF16)
        patches[pl.ds(2 * chans, chans), lanes] = after.astype(BF16)


def conv_patches(patches, weight, rows):
    depth = patches.shape[0]
    acc = None
    for i in range(3):
        part = dot(weight[:, pl.ds(i * depth, depth)], patches[:, pl.ds(i * 128, rows * 128)])
        acc = part if acc is None else acc + part
    return acc


def write_messages(out, gather, spread, top_msg, bot_msg, st_msg, as_rows):
    chans, cells = out.shape
    rows = cells // 128
    tiles = [
        functools.partial(lambda r: out[:, pl.ds(r * 128, 128)].astype(F32), r) for r in range(rows)
    ]
    stats = encode_stats(*local_stats(tiles, gather, spread, count_of(chans, cells)))
    st_msg[...] = stats
    if as_rows:
        for ref, r in ((top_msg, 0), (bot_msg, rows - 1)):
            ref[pl.ds(0, chans), :] = out[:, pl.ds(r * 128, 128)].astype(BF16)
            ref[pl.ds(chans, GROUPS), :] = stats


def count_of(chans, cells):
    return float(chans // GROUPS * cells)


def row_tile(ref, r):
    return lambda: ref[:, pl.ds(r * 128, 128)].astype(F32)


def stats_kernel(rim, mid, gather, spread, st_msg):
    rows = mid.shape[1] // 128 + 2
    tiles = [row_tile(rim, 0)]
    tiles += [row_tile(mid, r) for r in range(rows - 2)]
    tiles += [row_tile(rim, 1)]
    st_msg[...] = encode_stats(
        *local_stats(tiles, gather[...], spread[...], count_of(mid.shape[0], rows * 128))
    )


def head_kernel(rim, mid, stats, gain, shift, weight, spread, latent, out):
    chans = mid.shape[0]
    rows = mid.shape[1] // 128 + 2
    messages = [stats[pl.ds(k * GROUPS, GROUPS), :] for k in range(stats.shape[0] // GROUPS)]
    mean, root = combine_stats(messages, count_of(chans, rows * 128))
    center, scale = channel_moments(mean, root, spread[...])
    scale = scale * gain[...]
    tiles = [row_tile(rim, 0)]
    tiles += [row_tile(mid, r) for r in range(rows - 2)]
    tiles += [row_tile(rim, 1)]
    sums = []
    for tile in tiles:
        act = silu((tile() - center) * scale + shift[...]).astype(BF16)
        y = dot(weight[...], act)
        before, _ = shift_cols(y[0:24])
        _, after = shift_cols(y[48:72])
        sums.append(before + y[24:48] + after)
    for r in range(-1, rows + 1):
        acc = jnp.zeros((8, 128), F32)
        for i in range(3):
            if 0 <= r + i - 1 < rows:
                acc = acc + sums[r + i - 1][8 * i : 8 * i + 8]
        if 0 <= r < rows:
            acc = acc + latent[:, pl.ds(r * 128, 128)]
        out[:, pl.ds((r + 1) * 128, 128)] = acc


def first_kernel(
    first_step,
    ints,
    floats,
    parts,
    latent_in,
    in_weight,
    rim,
    mid,
    up,
    down,
    stats,
    gain,
    shift,
    weight_hbm,
    gather,
    spread,
    out,
    source,
    latent_out,
    top_msg,
    bot_msg,
    st_msg,
    weight,
    patches,
    wide,
    moments,
    noise,
    field,
    entry,
    sem,
):
    copy = pltpu.make_async_copy(weight_hbm, weight, sem)
    copy.start()
    chans = mid.shape[0]
    rows = mid.shape[1] // 128 + 2
    cells = rows * 128
    chips = parts.shape[0]
    full = chips * rows
    flags = (ints[0], ints[1])
    section, place = ints[2], ints[3]

    @pl.when(section == 0)
    def _():
        noise[...] = jnp.zeros_like(noise)
        for d in range(chips):
            owner = lax.rem(place - d + chips, chips)
            lanes = pl.ds(pl.multiple_of(owner * cells, 128), cells + 256)
            noise[:, lanes] = noise[:, lanes] + parts[d]
        change, root = floats[0], floats[1]
        field[...] = jnp.zeros_like(field)
        for r in range(full):
            piece = noise[:, pl.ds((r + 1) * 128, 128)]
            if first_step:
                old = pltpu.roll(piece, 4, 0)
            else:
                old = latent_in[:, pl.ds(r * 128, 128)]
            new = old + change * piece
            latent_out[:, pl.ds(r * 128, 128)] = new
            scaled = (new / root).astype(BF16).astype(F32)
            before, after = shift_cols(scaled)
            lanes = pl.ds((r + 1) * 128, 128)
            field[pl.ds(0, 8), lanes] = before
            field[pl.ds(8, 8), lanes] = scaled
            field[pl.ds(16, 8), lanes] = after
        total = jnp.zeros((chans, 128), F32)
        for z in range(chips):
            taps = [
                field[:, pl.ds((z * rows + i) * 128, cells)] for i in range(3)
            ]
            rows_out = dot(in_weight[...], jnp.concatenate(taps, axis=0).astype(BF16)).astype(BF16)
            entry[:, pl.ds(z * cells + 128, cells)] = rows_out
            for r in range(rows):
                total = total + rows_out[:, r * 128 : (r + 1) * 128].astype(F32)
        entry[:, pl.ds(0, 128)] = jnp.zeros((chans, 128), BF16)
        entry[:, pl.ds(full * 128 + 128, 128)] = jnp.zeros((chans, 128), BF16)
        count = count_of(chans, full * 128)
        mean = group_sum(total, gather[...]) / count
        center = expand(jnp.broadcast_to(mean, (GROUPS, 128)), spread[...])
        square = jnp.zeros((chans, 128), F32)
        for r in range(full):
            dev = entry[:, pl.ds((r + 1) * 128, 128)].astype(F32) - center
            square = square + dev * dev
        scale = lax.rsqrt(group_sum(square, gather[...]) / count + epsilon)
        moments[:, 0:128], moments[:, 128:256] = channel_moments(mean, scale, spread[...])
        wide[...] = entry[:, pl.ds(pl.multiple_of(place * cells, 128), cells + 256)]

    @pl.when(section != 0)
    def _():
        latent_out[...] = jnp.zeros_like(latent_out)
        messages = [stats[pl.ds(k * GROUPS, GROUPS), :] for k in range(chips)]
        mean, scale = combine_stats(messages, count_of(chans, cells))
        moments[:, 0:128], moments[:, 128:256] = channel_moments(mean, scale, spread[...])
        wide[:, pl.ds(0, 128)] = up[...]
        wide[:, pl.ds(128, 128)] = rim[:, pl.ds(0, 128)]
        wide[:, pl.ds(256, cells - 256)] = mid[...]
        wide[:, pl.ds(cells, 128)] = rim[:, pl.ds(128, 128)]
        wide[:, pl.ds(cells + 128, 128)] = down[...]

    source[...] = wide[:, pl.ds(128, cells)]
    tiles = [row_tile(wide, r) for r in range(rows + 2)]
    fill_patches(
        tiles, moments[:, 0:128], moments[:, 128:256] * gain[...], shift[...], flags, patches
    )
    copy.wait()
    out[...] = conv_patches(patches, weight, rows)
    write_messages(out, gather[...], spread[...], top_msg, bot_msg, st_msg, True)


def conv_kernel(
    residual,
    last,
    ints,
    own,
    up,
    down,
    stats,
    gain,
    shift,
    weight_hbm,
    gather,
    spread,
    *rest,
):
    rest = list(rest)
    base = rest.pop(0) if residual else None
    if last:
        rim, mid, st_msg = rest[:3]
        rest = rest[3:]
    else:
        out, top_msg, bot_msg, st_msg = rest[:4]
        rest = rest[4:]
    weight, patches, sem = rest[:3]
    final = rest[3] if last else None
    copy = pltpu.make_async_copy(weight_hbm, weight, sem)
    copy.start()
    chans, cells = own.shape
    rows = cells // 128
    messages = [up[pl.ds(chans, GROUPS), :], down[pl.ds(chans, GROUPS), :]]
    messages += [stats[pl.ds(k * GROUPS, GROUPS), :] for k in range(stats.shape[0] // GROUPS)]
    mean, root = combine_stats(messages, count_of(chans, cells))
    center, scale = channel_moments(mean, root, spread[...])
    tiles = [lambda: up[pl.ds(0, chans), :].astype(F32)]
    tiles += [row_tile(own, r) for r in range(rows)]
    tiles += [lambda: down[pl.ds(0, chans), :].astype(F32)]
    fill_patches(tiles, center, scale * gain[...], shift[...], (ints[0], ints[1]), patches)
    copy.wait()
    acc = conv_patches(patches, weight, rows)
    if residual:
        acc = (base[...].astype(F32) + acc).astype(BF16)
    if last:
        acc = jnp.where(ints[4] >= 2, acc.astype(F32), base[...].astype(F32)).astype(BF16)
        final[...] = acc
        rim[:, pl.ds(0, 128)] = final[:, pl.ds(0, 128)]
        rim[:, pl.ds(128, 128)] = final[:, pl.ds(cells - 128, 128)]
        mid[...] = final[:, pl.ds(128, cells - 256)]
        write_messages(final, gather[...], spread[...], None, None, st_msg, False)
    else:
        out[...] = acc
        write_messages(out, gather[...], spread[...], top_msg, bot_msg, st_msg, True)


VM = pl.BlockSpec(memory_space=pltpu.VMEM)
SM = pl.BlockSpec(memory_space=pltpu.SMEM)
HB = pl.BlockSpec(memory_space=pl.ANY)


def call(kernel, outs, in_specs, scratch, flops):
    return pl.pallas_call(
        kernel,
        out_shape=outs,
        in_specs=in_specs,
        out_specs=jax.tree.map(lambda _: VM, outs),
        scratch_shapes=scratch,
        compiler_params=pltpu.CompilerParams(vmem_limit_bytes=VMEM_LIMIT),
        cost_estimate=pl.CostEstimate(flops=flops, bytes_accessed=4_000_000, transcendentals=0),
    )


def sds(shape, dtype):
    return jax.ShapeDtypeStruct(shape, dtype)


def per_device(
    features,
    latent,
    plan_pos,
    blocks_used,
    conv1_w,
    conv2_w,
    norm_gain,
    norm_shift,
    in_w,
    head_w,
    head_gain,
    head_shift,
):
    sections = lax.axis_size("segment")
    patches = lax.axis_size("patch")
    chips = patches // CORES
    section = lax.axis_index("segment")
    core = lax.rem(lax.axis_index("patch"), CORES)
    place = lax.axis_index("patch") // CORES
    _, batch, chans, own_rows, cols = features.shape
    rows = CORES * own_rows
    half = own_rows * cols
    cells = rows * cols
    joint = ("segment", "patch")

    swap_pairs = [(p, p ^ 1) for p in range(patches)]

    def swap(x):
        return lax.ppermute(x, "patch", swap_pairs)

    def around(x, by):
        pairs = [
            (CORES * z + c, CORES * ((z + by) % chips) + c)
            for z in range(chips)
            for c in range(CORES)
        ]
        return lax.ppermute(x, "patch", pairs)

    def onward(x, by=0):
        pairs = []
        for s in range(sections):
            for z in range(chips):
                for c in range(CORES):
                    here = s * patches + CORES * z + c
                    there = (s + 1) % sections * patches + CORES * ((z + by) % chips) + c
                    pairs.append((here, there))
        return lax.ppermute(x, joint, pairs)

    group_of = jnp.arange(chans) // (chans // GROUPS)
    member = (jnp.arange(GROUPS)[:, None] == group_of[None, :]).astype(BF16)
    gather = jnp.tile(member, (1, 3))
    spread = jnp.tile(member.T, (1, 3))

    def packed(w):
        return jnp.transpose(w, (1, 0, 2)).reshape(chans, 9 * chans)

    kernels = [packed(w[0, k]) for k in range(2) for w in (conv1_w, conv2_w)]
    gains = [norm_gain[0, k, q][:, None] for k in range(2) for q in range(2)]
    shifts = [norm_shift[0, k, q][:, None] for k in range(2) for q in range(2)]
    lat = latent.shape[1]
    head_packed = jnp.zeros((3, 3, 8, chans), BF16)
    head_packed = head_packed.at[:, :, :lat].set(
        jnp.transpose(head_w.reshape(3, 3, lat, chans), (1, 0, 2, 3))
    ).reshape(72, chans)
    in_packed = jnp.zeros((chans, 3, 3, 8), BF16)
    in_packed = in_packed.at[:, :, :, :lat].set(
        jnp.transpose(in_w.reshape(3, 3, chans, lat), (2, 0, 1, 3))
    ).reshape(chans, 72)

    ints = jnp.stack(
        [
            (place > 0).astype(jnp.int32),
            (place < chips - 1).astype(jnp.int32),
            section.astype(jnp.int32),
            place.astype(jnp.int32),
            blocks_used[0],
        ]
    )

    def pick(x, which):
        return lax.dynamic_index_in_dim(x, which, 0, keepdims=False)

    def gather_rows(x):
        mine = pick(x, core)
        other = swap(pick(x, 1 - core))
        low = jnp.where(core == 0, mine, other).reshape(x.shape[1], half)
        high = jnp.where(core == 0, other, mine).reshape(x.shape[1], half)
        return low, high

    low, high = gather_rows(features[0])
    rim = jnp.concatenate([low[:, :cols], high[:, half - cols :]], axis=1)
    mid = jnp.concatenate([low[:, cols:], high[:, : half - cols]], axis=1)
    latent_rows = jnp.concatenate(gather_rows(latent), axis=1)
    latent_rows = jnp.concatenate([jnp.zeros((8 - lat, cells), F32), latent_rows], axis=0)
    no_latent = jnp.zeros((8, cells), F32)
    position = pick(plan_pos, core)

    stats_shape = sds((GROUPS, 128), BF16)
    rows_shape = sds((chans + GROUPS, 128), BF16)
    wide_shape = sds((chans, cells), F32)
    half_shape = sds((chans, cells), BF16)
    conv_flops = 2 * 9 * chans * chans * cells
    conv_scratch = [
        pltpu.VMEM((chans, 9 * chans), BF16),
        pltpu.VMEM((3 * chans, cells + 256), BF16),
    ]

    st_msg = call(stats_kernel, stats_shape, [VM] * 4, [], 10_000_000)(rim, mid, gather, spread)
    full_latent = None

    def exchange(top_msg, bot_msg, st_msg):
        far = [around(st_msg, d) for d in range(2, chips - 1)]
        up = around(bot_msg, 1)
        down = around(top_msg, chips - 1)
        return up, down, jnp.concatenate([st_msg] + far, axis=0)

    for step in range(STEPS):
        first_step = step == 0
        rim_next = onward(rim)
        all_stats = jnp.concatenate(
            [st_msg] + [around(st_msg, d) for d in range(1, chips)], axis=0
        )
        mid_next = onward(mid)
        noise = call(head_kernel, sds((8, cells + 256), F32), [VM] * 8, [], 300_000_000)(
            rim,
            mid,
            all_stats,
            head_gain[:, None],
            head_shift[:, None],
            head_packed,
            spread,
            latent_rows if first_step else no_latent,
        )
        parts = jnp.stack([onward(noise, d) for d in range(chips)])
        stats_next = onward(all_stats)
        up_next = around(rim_next[:, cols:], 1)
        down_next = around(rim_next[:, :cols], chips - 1)
        sigma_now = sigma_at(position + step)
        sigma_next = sigma_at(position + step + 1)
        floats = jnp.stack([sigma_next - sigma_now, jnp.sqrt(sigma_next * sigma_next + 1.0)])
        if first_step:
            full_latent = jnp.zeros((8, 128), F32)
        middle, source, full_latent, top_msg, bot_msg, st_msg = call(
            functools.partial(first_kernel, first_step),
            (
                wide_shape,
                half_shape,
                sds((8, chips * cells), F32),
                rows_shape,
                rows_shape,
                stats_shape,
            ),
            [SM, SM] + [VM] * 10 + [HB] + [VM] * 2,
            conv_scratch
            + [
                pltpu.VMEM((chans, cells + 256), BF16),
                pltpu.VMEM((chans, 256), F32),
                pltpu.VMEM((8, chips * cells + 256), F32),
                pltpu.VMEM((24, chips * cells + 256), F32),
                pltpu.VMEM((chans, chips * cells + 256), BF16),
                pltpu.SemaphoreType.DMA(()),
            ],
            conv_flops,
        )(
            ints,
            floats,
            parts,
            full_latent,
            in_packed,
            rim_next,
            mid_next,
            up_next,
            down_next,
            stats_next,
            gains[0],
            shifts[0],
            kernels[0],
            gather,
            spread,
        )

        def conv(index, own, messages, base, last=False):
            up, down, stats = exchange(*messages)
            outs = (
                (sds((chans, 2 * cols), BF16), sds((chans, cells - 2 * cols), BF16), stats_shape)
                if last
                else (
                    wide_shape if base is None else half_shape,
                    rows_shape,
                    rows_shape,
                    stats_shape,
                )
            )
            extra = [] if base is None else [base]
            return call(
                functools.partial(conv_kernel, base is not None, last),
                outs,
                [SM] + [VM] * 6 + [HB] + [VM] * (2 + len(extra)),
                conv_scratch
                + [pltpu.SemaphoreType.DMA(())]
                + ([pltpu.VMEM((chans, cells), BF16)] if last else []),
                conv_flops,
            )(
                ints,
                own,
                up,
                down,
                stats,
                gains[index],
                shifts[index],
                kernels[index],
                gather,
                spread,
                *extra,
            )

        one, *messages = conv(1, middle, (top_msg, bot_msg, st_msg), source)
        middle, *messages = conv(2, one, messages, None)
        rim, mid, st_msg = conv(3, middle, messages, one, True)

    low = jnp.concatenate([rim[:, :cols], mid[:, : half - cols]], axis=1)
    high = jnp.concatenate([mid[:, half - cols :], rim[:, cols:]], axis=1)

    def both(low, high):
        mine = jnp.where(core == 0, low, high)
        other = swap(jnp.where(core == 0, high, low))
        pair = jnp.where(core == 0, jnp.stack([mine, other]), jnp.stack([other, mine]))
        return pair.reshape(batch, low.shape[0], own_rows, cols)

    features_out = both(low, high)[None]
    rows_here = lax.dynamic_slice_in_dim(full_latent, place * cells, cells, 1)[:lat]
    latent_all = both(rows_here[:, :half], rows_here[:, half:])
    share = cols // sections
    latent_out = jnp.zeros((batch, lat, own_rows, share), F32)
    for s in range(sections):
        if s == 0:
            piece = latent_all[..., :share]
        else:
            piece = lax.ppermute(
                latent_all[..., s * share : (s + 1) * share],
                "segment",
                [(q, (q + s) % sections) for q in range(sections)],
            )
        latent_out = jnp.where(section == s, piece, latent_out)
    return (latent_out, features_out)


def solution(mesh):
    placed = (
        P("segment", None, None, "patch", None),
        P(None, None, "patch", None),
        P(),
        P("segment"),
        P("segment", None, None, None, None),
        P("segment", None, None, None, None),
        P("segment", None, None, None),
        P("segment", None, None, None),
        P(),
        P(),
        P(),
        P(),
    )
    return jax.shard_map(
        per_device,
        mesh=mesh,
        in_specs=placed,
        out_specs=(P(None, None, "patch", "segment"), P("segment", None, None, "patch", None)),
        check_vma=False,
    )
```

```python
import functools

import jax
import jax.numpy as jnp
from jax import lax
from jax.experimental import pallas as pl
from jax.experimental.pallas import tpu as pltpu
from jax.sharding import PartitionSpec as P

GROUPS = 32
STEPS = 2
SCHED = 12
CORES = 2

epsilon = 1e-05
sigma_top = 3.0
sigma_low = 0.1
rho_power = 7.0

F32 = jnp.float32
BF16 = jnp.bfloat16
VMEM_LIMIT = 24 * 1024 * 1024


def sigma_at(position):
    fraction = position.astype(F32) / (SCHED - 1)
    top_root = sigma_top ** (1.0 / rho_power)
    low_root = sigma_low ** (1.0 / rho_power)
    return (top_root + fraction * (low_root - top_root)) ** rho_power


def dot(a, b):
    return lax.dot_general(a, b, (((1,), (0,)), ((), ())), preferred_element_type=F32)


def split3(x):
    hi = x.astype(BF16)
    rest = x - hi.astype(F32)
    mid = rest.astype(BF16)
    lo = (rest - mid.astype(F32)).astype(BF16)
    return hi, mid, lo


def group_sum(x, gather):
    parts = jnp.concatenate(split3(x), axis=0)
    return jnp.sum(dot(gather, parts), axis=1, keepdims=True)


def expand(x, spread):
    return dot(spread, jnp.concatenate(split3(x), axis=0))


def tile_sum(tiles):
    total = tiles[0]
    for tile in tiles[1:]:
        total = total + tile
    return total


def pivot_of(tiles, gather, spread, count):
    mean = group_sum(tile_sum(tiles), gather) / (count * len(tiles))
    return mean, expand(jnp.broadcast_to(mean, (GROUPS, 128)), spread)


def add_deviations(sums, tiles, center):
    first, second = sums
    for tile in tiles:
        dev = tile - center
        first = dev if first is None else first + dev
        second = dev * dev if second is None else second + dev * dev
    return first, second


def finish_stats(pivot, sums, gather, count):
    wide = dot(gather, jnp.concatenate(split3(jnp.concatenate(sums, axis=1)), axis=0))
    first = jnp.sum(wide[:, :128], axis=1, keepdims=True)
    second = jnp.sum(wide[:, 128:], axis=1, keepdims=True)
    return pivot + first / count, jnp.maximum(second - first * first / count, 0.0)


def encode_stats(mean, square):
    lane = lax.broadcasted_iota(jnp.int32, (GROUPS, 128), 1) // 16
    out = jnp.zeros((GROUPS, 128), F32)
    for slot, part in enumerate(split3(mean) + split3(square)):
        out = jnp.where(lane == slot, part.astype(F32), out)
    return out.astype(BF16)


def decode_stats(message):
    wide = message.astype(F32)
    take = [wide[:, 16 * k : 16 * k + 1] for k in range(6)]
    return take[0] + take[1] + take[2], take[3] + take[4] + take[5]


def combine_stats(messages, count):
    pairs = [decode_stats(m) for m in messages]
    mean = sum(p[0] for p in pairs) / len(pairs)
    square = sum(p[1] for p in pairs)
    for p in pairs:
        square = square + count * (p[0] - mean) * (p[0] - mean)
    return mean, lax.rsqrt(square / (count * len(pairs)) + epsilon)


def channel_moments(mean, scale, spread):
    both = jnp.concatenate(
        [jnp.broadcast_to(mean, (GROUPS, 128)), jnp.broadcast_to(scale, (GROUPS, 128))], axis=1
    )
    wide = expand(both, spread)
    return wide[:, :128], wide[:, 128:]


def silu(v):
    half = 0.5 * v
    return half + half * jnp.tanh(half)


def shift_cols(t):
    lane = lax.broadcasted_iota(jnp.int32, t.shape, 1)
    before = jnp.where(lane == 0, 0.0, pltpu.roll(t, 1, 1))
    after = jnp.where(lane == 127, 0.0, pltpu.roll(t, 127, 1))
    return before, after


def fill_row(r, last, tile, moments, flags, patches):
    center, scale, shift = moments
    chans = center.shape[0]
    main = chans // 128 * 128
    tail = chans - main
    t = silu((tile - center) * scale + shift)
    if r == 0:
        t = jnp.where(flags[0] > 0, t, 0.0)
    if r == last:
        t = jnp.where(flags[1] > 0, t, 0.0)
    before, after = shift_cols(t)
    lanes = pl.ds(r * 128, 128)
    for j, piece in enumerate((before, t, after)):
        piece = piece.astype(BF16)
        patches[pl.ds(j * main, main), lanes] = piece[:main]
        patches[pl.ds(3 * main + j * tail, tail), lanes] = piece[main:]


def conv_rows(patches, weight, start, rows):
    depth = weight.shape[1] // 9
    main = depth // 128 * 128
    parts = ((0, 3 * main), (3 * main, 3 * (depth - main)))
    pieces = [
        patches[pl.ds(low, size), pl.ds((start + i) * 128, rows * 128)]
        for low, size in parts
        for i in range(3)
    ]
    return dot(weight[...], jnp.concatenate(pieces, axis=0))


CHUNK = 4


def conv_all(tiles, moments, flags, patches, weight, store, gather, spread):
    rows = len(tiles) - 2
    chans = weight.shape[0]
    filled = 0
    per_row = count_of(chans, 128)
    sums = (None, None)
    for start in range(0, rows, CHUNK):
        while filled < start + CHUNK + 2:
            fill_row(filled, rows + 1, tiles[filled](), moments, flags, patches)
            filled += 1
        kept = store(start, CHUNK, conv_rows(patches, weight, start, CHUNK))
        kept = [kept[:, r * 128 : (r + 1) * 128] for r in range(CHUNK)]
        if start == 0:
            pivot, center = pivot_of(kept, gather, spread, per_row)
        sums = add_deviations(sums, kept, center)
    return encode_stats(*finish_stats(pivot, sums, gather, per_row * rows))


def write_messages(out, stats, top_msg, bot_msg, st_msg):
    chans, cells = out.shape
    st_msg[...] = stats
    for ref, start in ((top_msg, 0), (bot_msg, cells - 128)):
        ref[pl.ds(0, chans), :] = out[:, pl.ds(start, 128)].astype(BF16)
        ref[pl.ds(chans, GROUPS), :] = stats


def pack_kernel(first_hbm, second_hbm, *rest):
    outs, (loaded, sems) = rest[:4], rest[4:]
    chans = loaded.shape[2]
    main = chans // 128 * 128
    tail = chans - main
    copies = []
    for n in range(4):
        source = (first_hbm, second_hbm)[n % 2]
        copies.append(pltpu.make_async_copy(source.at[0, n // 2], loaded.at[n], sems.at[n]))
        copies[-1].start()
    for n in range(4):
        copies[n].wait()
        pieces = []
        for t in range(9):
            tap = loaded[n, t]
            outs[n][:, pl.ds(t * main, main)] = tap[:, :main]
            pieces.append(tap[:, main:])
        outs[n][:, pl.ds(9 * main, 9 * tail)] = jnp.concatenate(pieces, axis=1)


def count_of(chans, cells):
    return float(chans // GROUPS * cells)


def row_tile(ref, r):
    return lambda: ref[:, pl.ds(r * 128, 128)].astype(F32)


def stats_kernel(rim, mid, gather, spread, st_msg):
    rows = mid.shape[1] // 128 + 2
    tiles = [row_tile(rim, 0)]
    tiles += [row_tile(mid, r) for r in range(rows - 2)]
    tiles += [row_tile(rim, 1)]
    tiles = [tile() for tile in tiles]
    per_row = count_of(mid.shape[0], 128)
    pivot, center = pivot_of(tiles[:2], gather[...], spread[...], per_row)
    sums = add_deviations((None, None), tiles, center)
    st_msg[...] = encode_stats(*finish_stats(pivot, sums, gather[...], per_row * rows))


def head_kernel(rim, mid, stats, gain, shift, weight, spread, latent, out):
    chans = mid.shape[0]
    rows = mid.shape[1] // 128 + 2
    messages = [stats[pl.ds(k * GROUPS, GROUPS), :] for k in range(stats.shape[0] // GROUPS)]
    mean, root = combine_stats(messages, count_of(chans, rows * 128))
    center, scale = channel_moments(mean, root, spread[...])
    scale = scale * gain[...]
    tiles = [row_tile(rim, 0)]
    tiles += [row_tile(mid, r) for r in range(rows - 2)]
    tiles += [row_tile(rim, 1)]
    sums = []
    for tile in tiles:
        act = silu((tile() - center) * scale + shift[...]).astype(BF16)
        y = dot(weight[...], act)
        before, _ = shift_cols(y[0:24])
        _, after = shift_cols(y[48:72])
        sums.append(before + y[24:48] + after)
    for r in range(-1, rows + 1):
        acc = jnp.zeros((8, 128), F32)
        for i in range(3):
            if 0 <= r + i - 1 < rows:
                acc = acc + sums[r + i - 1][8 * i : 8 * i + 8]
        if 0 <= r < rows:
            acc = acc + latent[:, pl.ds(r * 128, 128)]
        out[:, pl.ds((r + 1) * 128, 128)] = acc


def first_kernel(
    first_step,
    ints,
    floats,
    parts,
    latent_in,
    in_weight,
    rim,
    mid,
    up,
    down,
    stats,
    gain,
    shift,
    weight,
    gather,
    spread,
    out,
    source,
    latent_out,
    top_msg,
    bot_msg,
    st_msg,
    patches,
    wide,
    moments,
    noise,
    field,
    entry,
):
    chans = mid.shape[0]
    rows = mid.shape[1] // 128 + 2
    cells = rows * 128
    chips = parts.shape[0]
    full = chips * rows
    flags = (ints[0], ints[1])
    section, place = ints[2], ints[3]

    @pl.when(section == 0)
    def _():
        noise[...] = jnp.zeros_like(noise)
        for d in range(chips):
            owner = lax.rem(place - d + chips, chips)
            lanes = pl.ds(pl.multiple_of(owner * cells, 128), cells + 256)
            noise[:, lanes] = noise[:, lanes] + parts[d]
        change, root = floats[0], floats[1]
        field[...] = jnp.zeros_like(field)
        for r in range(full):
            piece = noise[:, pl.ds((r + 1) * 128, 128)]
            if first_step:
                old = pltpu.roll(piece, 4, 0)
            else:
                old = latent_in[:, pl.ds(r * 128, 128)]
            new = old + change * piece
            latent_out[:, pl.ds(r * 128, 128)] = new
            scaled = (new / root).astype(BF16).astype(F32)
            before, after = shift_cols(scaled)
            lanes = pl.ds((r + 1) * 128, 128)
            field[pl.ds(0, 8), lanes] = before
            field[pl.ds(8, 8), lanes] = scaled
            field[pl.ds(16, 8), lanes] = after
        sums = (None, None)
        per_row = count_of(chans, 128)
        for z in range(chips):
            taps = [field[:, pl.ds((z * rows + i) * 128, cells)] for i in range(3)]
            rows_out = dot(in_weight[...], jnp.concatenate(taps, axis=0).astype(BF16)).astype(BF16)
            entry[:, pl.ds(z * cells + 128, cells)] = rows_out
            kept = [rows_out[:, r * 128 : (r + 1) * 128].astype(F32) for r in range(rows)]
            if z == 0:
                pivot, center = pivot_of(kept, gather[...], spread[...], per_row)
            sums = add_deviations(sums, kept, center)
        entry[:, pl.ds(0, 128)] = jnp.zeros((chans, 128), BF16)
        entry[:, pl.ds(full * 128 + 128, 128)] = jnp.zeros((chans, 128), BF16)
        count = per_row * full
        mean, square = finish_stats(pivot, sums, gather[...], count)
        scale = lax.rsqrt(square / count + epsilon)
        moments[:, 0:128], moments[:, 128:256] = channel_moments(mean, scale, spread[...])
        wide[...] = entry[:, pl.ds(pl.multiple_of(place * cells, 128), cells + 256)]

    @pl.when(section != 0)
    def _():
        latent_out[...] = jnp.zeros_like(latent_out)
        messages = [stats[pl.ds(k * GROUPS, GROUPS), :] for k in range(chips)]
        mean, scale = combine_stats(messages, count_of(chans, cells))
        moments[:, 0:128], moments[:, 128:256] = channel_moments(mean, scale, spread[...])
        wide[:, pl.ds(0, 128)] = up[...]
        wide[:, pl.ds(128, 128)] = rim[:, pl.ds(0, 128)]
        wide[:, pl.ds(256, cells - 256)] = mid[...]
        wide[:, pl.ds(cells, 128)] = rim[:, pl.ds(128, 128)]
        wide[:, pl.ds(cells + 128, 128)] = down[...]

    source[...] = wide[:, pl.ds(128, cells)]
    tiles = [row_tile(wide, r) for r in range(rows + 2)]
    known = (moments[:, 0:128], moments[:, 128:256] * gain[...], shift[...])

    def store(start, count, acc):
        out[:, pl.ds(start * 128, count * 128)] = acc
        return acc

    stats_out = conv_all(tiles, known, flags, patches, weight, store, gather[...], spread[...])
    write_messages(out, stats_out, top_msg, bot_msg, st_msg)


def conv_kernel(
    residual,
    last,
    ints,
    own,
    up,
    down,
    stats,
    gain,
    shift,
    weight,
    gather,
    spread,
    *rest,
):
    rest = list(rest)
    base = rest.pop(0) if residual else None
    if last:
        rim, mid, st_msg = rest[:3]
        rest = rest[3:]
    else:
        out, top_msg, bot_msg, st_msg = rest[:4]
        rest = rest[4:]
    patches = rest[0]
    chans, cells = own.shape
    rows = cells // 128
    messages = [up[pl.ds(chans, GROUPS), :], down[pl.ds(chans, GROUPS), :]]
    messages += [stats[pl.ds(k * GROUPS, GROUPS), :] for k in range(stats.shape[0] // GROUPS)]
    mean, root = combine_stats(messages, count_of(chans, cells))
    center, scale = channel_moments(mean, root, spread[...])
    tiles = [lambda: up[pl.ds(0, chans), :].astype(F32)]
    tiles += [row_tile(own, r) for r in range(rows)]
    tiles += [lambda: down[pl.ds(0, chans), :].astype(F32)]
    known = (center, scale * gain[...], shift[...])

    def store(start, count, acc):
        lanes = pl.ds(start * 128, count * 128)
        if residual:
            old = base[:, lanes].astype(F32)
            acc = (old + acc).astype(BF16).astype(F32)
        if not last:
            out[:, lanes] = acc.astype(out.dtype)
            return acc
        acc = jnp.where(ints[4] >= 2, acc, old)
        for r in range(count):
            row = acc[:, r * 128 : (r + 1) * 128].astype(BF16)
            if start + r == 0:
                rim[:, pl.ds(0, 128)] = row
            elif start + r == rows - 1:
                rim[:, pl.ds(128, 128)] = row
            else:
                mid[:, pl.ds((start + r - 1) * 128, 128)] = row
        return acc

    stats_out = conv_all(
        tiles, known, (ints[0], ints[1]), patches, weight, store, gather[...], spread[...]
    )
    if last:
        st_msg[...] = stats_out
    else:
        write_messages(out, stats_out, top_msg, bot_msg, st_msg)


VM = pl.BlockSpec(memory_space=pltpu.VMEM)
SM = pl.BlockSpec(memory_space=pltpu.SMEM)
HB = pl.BlockSpec(memory_space=pl.ANY)


def call(kernel, outs, in_specs, scratch, flops):
    return pl.pallas_call(
        kernel,
        out_shape=outs,
        in_specs=in_specs,
        out_specs=jax.tree.map(lambda _: VM, outs),
        scratch_shapes=scratch,
        compiler_params=pltpu.CompilerParams(vmem_limit_bytes=VMEM_LIMIT),
        cost_estimate=pl.CostEstimate(flops=flops, bytes_accessed=4_000_000, transcendentals=0),
    )


def sds(shape, dtype):
    return jax.ShapeDtypeStruct(shape, dtype)


def per_device(
    features,
    latent,
    plan_pos,
    blocks_used,
    conv1_w,
    conv2_w,
    norm_gain,
    norm_shift,
    in_w,
    head_w,
    head_gain,
    head_shift,
):
    sections = lax.axis_size("segment")
    patches = lax.axis_size("patch")
    chips = patches // CORES
    section = lax.axis_index("segment")
    core = lax.rem(lax.axis_index("patch"), CORES)
    place = lax.axis_index("patch") // CORES
    _, batch, chans, own_rows, cols = features.shape
    rows = CORES * own_rows
    half = own_rows * cols
    cells = rows * cols
    joint = ("segment", "patch")

    swap_pairs = [(p, p ^ 1) for p in range(patches)]

    def swap(x):
        return lax.ppermute(x, "patch", swap_pairs)

    def around(x, by):
        pairs = [
            (CORES * z + c, CORES * ((z + by) % chips) + c)
            for z in range(chips)
            for c in range(CORES)
        ]
        return lax.ppermute(x, "patch", pairs)

    def onward(x, by=0):
        pairs = []
        for s in range(sections):
            for z in range(chips):
                for c in range(CORES):
                    here = s * patches + CORES * z + c
                    there = (s + 1) % sections * patches + CORES * ((z + by) % chips) + c
                    pairs.append((here, there))
        return lax.ppermute(x, joint, pairs)

    group_of = jnp.arange(chans) // (chans // GROUPS)
    member = (jnp.arange(GROUPS)[:, None] == group_of[None, :]).astype(BF16)
    gather = jnp.tile(member, (1, 3))
    spread = jnp.tile(member.T, (1, 3))

    packed = sds((chans, 9 * chans), BF16)
    kernels = call(
        pack_kernel,
        (packed,) * 4,
        [HB, HB],
        [pltpu.VMEM((4,) + conv1_w.shape[2:], BF16), pltpu.SemaphoreType.DMA((4,))],
        10_000_000,
    )(conv1_w, conv2_w)
    gains = [norm_gain[0, k, q][:, None] for k in range(2) for q in range(2)]
    shifts = [norm_shift[0, k, q][:, None] for k in range(2) for q in range(2)]
    lat = latent.shape[1]
    head_packed = jnp.zeros((3, 3, 8, chans), BF16)
    head_packed = head_packed.at[:, :, :lat].set(
        jnp.transpose(head_w.reshape(3, 3, lat, chans), (1, 0, 2, 3))
    ).reshape(72, chans)
    in_packed = jnp.zeros((chans, 3, 3, 8), BF16)
    in_packed = in_packed.at[:, :, :, :lat].set(
        jnp.transpose(in_w.reshape(3, 3, chans, lat), (2, 0, 1, 3))
    ).reshape(chans, 72)

    ints = jnp.stack(
        [
            (place > 0).astype(jnp.int32),
            (place < chips - 1).astype(jnp.int32),
            section.astype(jnp.int32),
            place.astype(jnp.int32),
            blocks_used[0],
        ]
    )

    def pick(x, which):
        return lax.dynamic_index_in_dim(x, which, 0, keepdims=False)

    def gather_rows(x):
        mine = pick(x, core)
        other = swap(pick(x, 1 - core))
        low = jnp.where(core == 0, mine, other).reshape(x.shape[1], half)
        high = jnp.where(core == 0, other, mine).reshape(x.shape[1], half)
        return low, high

    low, high = gather_rows(features[0])
    rim = jnp.concatenate([low[:, :cols], high[:, half - cols :]], axis=1)
    mid = jnp.concatenate([low[:, cols:], high[:, : half - cols]], axis=1)
    latent_rows = jnp.concatenate(gather_rows(latent), axis=1)
    latent_rows = jnp.concatenate([jnp.zeros((8 - lat, cells), F32), latent_rows], axis=0)
    no_latent = jnp.zeros((8, cells), F32)
    position = pick(plan_pos, core)

    stats_shape = sds((GROUPS, 128), BF16)
    rows_shape = sds((chans + GROUPS, 128), BF16)
    wide_shape = sds((chans, cells), F32)
    half_shape = sds((chans, cells), BF16)
    conv_flops = 2 * 9 * chans * chans * cells
    conv_scratch = [pltpu.VMEM((3 * chans, cells + 256), BF16)]

    st_msg = call(stats_kernel, stats_shape, [VM] * 4, [], 10_000_000)(rim, mid, gather, spread)
    full_latent = None

    def exchange(top_msg, bot_msg, st_msg):
        far = [around(st_msg, d) for d in range(2, chips - 1)]
        up = around(bot_msg, 1)
        down = around(top_msg, chips - 1)
        return up, down, jnp.concatenate([st_msg] + far, axis=0)

    for step in range(STEPS):
        first_step = step == 0
        rim_next = onward(rim)
        all_stats = jnp.concatenate(
            [st_msg] + [around(st_msg, d) for d in range(1, chips)], axis=0
        )
        mid_next = onward(mid)
        noise = call(head_kernel, sds((8, cells + 256), F32), [VM] * 8, [], 300_000_000)(
            rim,
            mid,
            all_stats,
            head_gain[:, None],
            head_shift[:, None],
            head_packed,
            spread,
            latent_rows if first_step else no_latent,
        )
        parts = jnp.stack([onward(noise, d) for d in range(chips)])
        stats_next = onward(all_stats)
        up_next = around(rim_next[:, cols:], 1)
        down_next = around(rim_next[:, :cols], chips - 1)
        sigma_now = sigma_at(position + step)
        sigma_next = sigma_at(position + step + 1)
        floats = jnp.stack([sigma_next - sigma_now, jnp.sqrt(sigma_next * sigma_next + 1.0)])
        if first_step:
            full_latent = jnp.zeros((8, 128), F32)
        middle, source, full_latent, top_msg, bot_msg, st_msg = call(
            functools.partial(first_kernel, first_step),
            (
                wide_shape,
                half_shape,
                sds((8, chips * cells), F32),
                rows_shape,
                rows_shape,
                stats_shape,
            ),
            [SM, SM] + [VM] * 13,
            conv_scratch
            + [
                pltpu.VMEM((chans, cells + 256), BF16),
                pltpu.VMEM((chans, 256), F32),
                pltpu.VMEM((8, chips * cells + 256), F32),
                pltpu.VMEM((24, chips * cells + 256), F32),
                pltpu.VMEM((chans, chips * cells + 256), BF16),
            ],
            conv_flops,
        )(
            ints,
            floats,
            parts,
            full_latent,
            in_packed,
            rim_next,
            mid_next,
            up_next,
            down_next,
            stats_next,
            gains[0],
            shifts[0],
            kernels[0],
            gather,
            spread,
        )

        def conv(index, own, messages, base, last=False):
            up, down, stats = exchange(*messages)
            outs = (
                (sds((chans, 2 * cols), BF16), sds((chans, cells - 2 * cols), BF16), stats_shape)
                if last
                else (
                    wide_shape if base is None else half_shape,
                    rows_shape,
                    rows_shape,
                    stats_shape,
                )
            )
            extra = [] if base is None else [base]
            return call(
                functools.partial(conv_kernel, base is not None, last),
                outs,
                [SM] + [VM] * (9 + len(extra)),
                conv_scratch,
                conv_flops,
            )(
                ints,
                own,
                up,
                down,
                stats,
                gains[index],
                shifts[index],
                kernels[index],
                gather,
                spread,
                *extra,
            )

        one, *messages = conv(1, middle, (top_msg, bot_msg, st_msg), source)
        middle, *messages = conv(2, one, messages, None)
        rim, mid, st_msg = conv(3, middle, messages, one, True)

    low = jnp.concatenate([rim[:, :cols], mid[:, : half - cols]], axis=1)
    high = jnp.concatenate([mid[:, half - cols :], rim[:, cols:]], axis=1)

    def both(low, high):
        mine = jnp.where(core == 0, low, high)
        other = swap(jnp.where(core == 0, high, low))
        pair = jnp.where(core == 0, jnp.stack([mine, other]), jnp.stack([other, mine]))
        return pair.reshape(batch, low.shape[0], own_rows, cols)

    features_out = both(low, high)[None]
    rows_here = lax.dynamic_slice_in_dim(full_latent, place * cells, cells, 1)[:lat]
    latent_all = both(rows_here[:, :half], rows_here[:, half:])
    share = cols // sections
    latent_out = jnp.zeros((batch, lat, own_rows, share), F32)
    for s in range(sections):
        if s == 0:
            piece = latent_all[..., :share]
        else:
            piece = lax.ppermute(
                latent_all[..., s * share : (s + 1) * share],
                "segment",
                [(q, (q + s) % sections) for q in range(sections)],
            )
        latent_out = jnp.where(section == s, piece, latent_out)
    return (latent_out, features_out)


def solution(mesh):
    placed = (
        P("segment", None, None, "patch", None),
        P(None, None, "patch", None),
        P(),
        P("segment"),
        P("segment", None, None, None, None),
        P("segment", None, None, None, None),
        P("segment", None, None, None),
        P("segment", None, None, None),
        P(),
        P(),
        P(),
        P(),
    )
    return jax.shard_map(
        per_device,
        mesh=mesh,
        in_specs=placed,
        out_specs=(P(None, None, "patch", "segment"), P("segment", None, None, "patch", None)),
        check_vma=False,
    )
```

```python
import functools

import jax
import jax.numpy as jnp
from jax import lax
from jax.experimental import pallas as pl
from jax.experimental.pallas import tpu as pltpu
from jax.sharding import PartitionSpec as P

GROUPS = 32
STEPS = 2
SCHED = 12
CORES = 2

epsilon = 1e-05
sigma_top = 3.0
sigma_low = 0.1
rho_power = 7.0

F32 = jnp.float32
BF16 = jnp.bfloat16
VMEM_LIMIT = 24 * 1024 * 1024


def sigma_at(position):
    fraction = position.astype(F32) / (SCHED - 1)
    top_root = sigma_top ** (1.0 / rho_power)
    low_root = sigma_low ** (1.0 / rho_power)
    return (top_root + fraction * (low_root - top_root)) ** rho_power


def dot(a, b):
    return lax.dot_general(a, b, (((1,), (0,)), ((), ())), preferred_element_type=F32)


def split3(x):
    hi = x.astype(BF16)
    rest = x - hi.astype(F32)
    mid = rest.astype(BF16)
    lo = (rest - mid.astype(F32)).astype(BF16)
    return hi, mid, lo


def group_sum(x, gather):
    parts = jnp.concatenate(split3(x), axis=0)
    return jnp.sum(dot(gather, parts), axis=1, keepdims=True)


def expand(x, spread):
    return dot(spread, jnp.concatenate(split3(x), axis=0))


def tile_sum(tiles):
    total = tiles[0]
    for tile in tiles[1:]:
        total = total + tile
    return total


def pivot_of(tiles, gather, spread, count):
    mean = group_sum(tile_sum(tiles), gather) / (count * len(tiles))
    return mean, expand(jnp.broadcast_to(mean, (GROUPS, 128)), spread)


def add_deviations(sums, tiles, center):
    first, second = sums
    for tile in tiles:
        dev = tile - center
        first = dev if first is None else first + dev
        second = dev * dev if second is None else second + dev * dev
    return first, second


def finish_stats(pivot, sums, gather, count):
    wide = dot(gather, jnp.concatenate(split3(jnp.concatenate(sums, axis=1)), axis=0))
    first = jnp.sum(wide[:, :128], axis=1, keepdims=True)
    second = jnp.sum(wide[:, 128:], axis=1, keepdims=True)
    return pivot + first / count, jnp.maximum(second - first * first / count, 0.0)


def encode_stats(mean, square):
    lane = lax.broadcasted_iota(jnp.int32, (GROUPS, 128), 1) // 16
    out = jnp.zeros((GROUPS, 128), F32)
    for slot, part in enumerate(split3(mean) + split3(square)):
        out = jnp.where(lane == slot, part.astype(F32), out)
    return out.astype(BF16)


def decode_stats(message):
    wide = message.astype(F32)
    take = [wide[:, 16 * k : 16 * k + 1] for k in range(6)]
    return take[0] + take[1] + take[2], take[3] + take[4] + take[5]


def combine_stats(messages, count):
    pairs = [decode_stats(m) for m in messages]
    mean = sum(p[0] for p in pairs) / len(pairs)
    square = sum(p[1] for p in pairs)
    for p in pairs:
        square = square + count * (p[0] - mean) * (p[0] - mean)
    return mean, lax.rsqrt(square / (count * len(pairs)) + epsilon)


def channel_moments(mean, scale, spread):
    both = jnp.concatenate(
        [jnp.broadcast_to(mean, (GROUPS, 128)), jnp.broadcast_to(scale, (GROUPS, 128))], axis=1
    )
    wide = expand(both, spread)
    return wide[:, :128], wide[:, 128:]


def silu(v):
    half = 0.5 * v
    return half + half * jnp.tanh(half)


def shift_cols(t):
    lane = lax.broadcasted_iota(jnp.int32, t.shape, 1)
    before = jnp.where(lane == 0, 0.0, pltpu.roll(t, 1, 1))
    after = jnp.where(lane == 127, 0.0, pltpu.roll(t, 127, 1))
    return before, after


def fill_row(r, last, tile, moments, flags, patches):
    center, scale, shift = moments
    chans = center.shape[0]
    main = chans // 128 * 128
    tail = chans - main
    t = silu((tile - center) * scale + shift)
    if r == 0:
        t = jnp.where(flags[0] > 0, t, 0.0)
    if r == last:
        t = jnp.where(flags[1] > 0, t, 0.0)
    before, after = shift_cols(t)
    lanes = pl.ds(r * 128, 128)
    for j, piece in enumerate((before, t, after)):
        piece = piece.astype(BF16)
        patches[pl.ds(j * main, main), lanes] = piece[:main]
        patches[pl.ds(3 * main + j * tail, tail), lanes] = piece[main:]


def conv_rows(patches, weight, start, rows):
    depth = weight.shape[1] // 9
    main = depth // 128 * 128
    parts = ((0, 3 * main), (3 * main, 3 * (depth - main)))
    pieces = [
        patches[pl.ds(low, size), pl.ds((start + i) * 128, rows * 128)]
        for low, size in parts
        for i in range(3)
    ]
    return dot(weight[...], jnp.concatenate(pieces, axis=0))


CHUNK = 4


def conv_all(tiles, moments, flags, patches, weight, store, gather, spread):
    rows = len(tiles) - 2
    chans = weight.shape[0]
    filled = 0
    per_row = count_of(chans, 128)
    sums = (None, None)
    for start in range(0, rows, CHUNK):
        while filled < start + CHUNK + 2:
            fill_row(filled, rows + 1, tiles[filled](), moments, flags, patches)
            filled += 1
        kept = store(start, CHUNK, conv_rows(patches, weight, start, CHUNK))
        kept = [kept[:, r * 128 : (r + 1) * 128] for r in range(CHUNK)]
        if start == 0:
            pivot, center = pivot_of(kept, gather, spread, per_row)
        sums = add_deviations(sums, kept, center)
    return encode_stats(*finish_stats(pivot, sums, gather, per_row * rows))


def write_messages(out, stats, top_msg, bot_msg, st_msg):
    chans, cells = out.shape
    st_msg[...] = stats
    for ref, start in ((top_msg, 0), (bot_msg, cells - 128)):
        ref[pl.ds(0, chans), :] = out[:, pl.ds(start, 128)].astype(BF16)
        ref[pl.ds(chans, GROUPS), :] = stats


def pack_kernel(first, second, *outs):
    chans = first.shape[3]
    main = chans // 128 * 128
    tail = chans - main
    for n in range(4):
        pieces = []
        for t in range(9):
            tap = (first, second)[n % 2][0, n // 2, t]
            outs[n][:, pl.ds(t * main, main)] = tap[:, :main]
            pieces.append(tap[:, main:])
        outs[n][:, pl.ds(9 * main, 9 * tail)] = jnp.concatenate(pieces, axis=1)


def count_of(chans, cells):
    return float(chans // GROUPS * cells)


def row_tile(ref, r):
    return lambda: ref[:, pl.ds(r * 128, 128)].astype(F32)


def enter_kernel(ints, features, other, gather, spread, out, top_msg, bot_msg, st_msg):
    core = ints[5]
    own_rows = other.shape[1]
    tiles = []
    for part in range(CORES):
        for r in range(own_rows):
            row = jnp.where(core == part, features[core, :, r, :].astype(F32), other[:, r, :].astype(F32))
            out[:, pl.ds((part * own_rows + r) * 128, 128)] = row.astype(BF16)
            tiles.append(row)
    per_row = count_of(other.shape[0], 128)
    pivot, center = pivot_of(tiles[:2], gather[...], spread[...], per_row)
    sums = add_deviations((None, None), tiles, center)
    stats = encode_stats(*finish_stats(pivot, sums, gather[...], per_row * len(tiles)))
    write_messages(out, stats, top_msg, bot_msg, st_msg)


def column(params, k):
    return params[:, k : k + 1]


def gathered(up, down, others, count):
    chans = up.shape[0] - GROUPS
    messages = [up[pl.ds(chans, GROUPS), :], down[pl.ds(chans, GROUPS), :]]
    return combine_stats(messages + [ref[...] for ref in others], count)


def head_kernel(params, own, up, down, weight, spread, *rest):
    others, (out, forward) = rest[:-2], rest[-2:]
    latent = None
    if out.shape[0] == 8:
        others, latent = others[:-1], others[-1]
    chans, cells = own.shape
    rows = cells // 128
    mean, root = gathered(up, down, others, count_of(chans, cells))
    stats = encode_stats(mean, root)
    for ref, low in ((up, 0), (down, 128)):
        forward[pl.ds(0, chans), pl.ds(low, 128)] = ref[pl.ds(0, chans), :]
        forward[pl.ds(chans, GROUPS), pl.ds(low, 128)] = stats
    center, scale = channel_moments(mean, root, spread[...])
    scale = scale * column(params, 8)
    shift = column(params, 9)
    tiles = [row_tile(own, r) for r in range(rows)]
    sums = []
    for tile in tiles:
        act = silu((tile() - center) * scale + shift).astype(BF16)
        y = dot(weight[...], act)
        before, _ = shift_cols(y[0:24])
        _, after = shift_cols(y[48:72])
        sums.append(before + y[24:48] + after)
    for r in range(-1, rows + 1):
        acc = jnp.zeros((8, 128), F32)
        for i in range(3):
            if 0 <= r + i - 1 < rows:
                acc = acc + sums[r + i - 1][8 * i : 8 * i + 8]
        if latent is not None and 0 <= r < rows:
            acc = acc + latent[:, pl.ds(r * 128, 128)]
        out[:, pl.ds((r + 1) * 128, 128)] = acc[: out.shape[0]]


def first_kernel(first_step, chips, ints, floats, params, *rest):
    parts, rest = rest[:chips], rest[chips:]
    if not first_step:
        latent_in, rest = rest[0], rest[1:]
    in_weight, own, forward, weight, gather, spread = rest[:6]
    out, source, latent_out, top_msg, bot_msg, st_msg = rest[6:12]
    patches, wide, moments, noise, field, entry = rest[12:]
    chans, cells = own.shape
    rows = cells // 128
    full = chips * rows
    flags = (ints[0], ints[1])
    section, place = ints[2], ints[3]

    @pl.when(section == 0)
    def _():
        noise[...] = jnp.zeros_like(noise)
        for d in range(chips):
            owner = lax.rem(place - d + chips, chips)
            lanes = pl.ds(pl.multiple_of(owner * cells, 128), cells + 256)
            height = parts[d].shape[0]
            noise[:height, lanes] = noise[:height, lanes] + parts[d][...]
        change, root = floats[0], floats[1]
        field[...] = jnp.zeros_like(field)
        for r in range(full):
            piece = noise[:, pl.ds((r + 1) * 128, 128)]
            if first_step:
                old = pltpu.roll(piece, 4, 0)
            else:
                old = latent_in[:, pl.ds(r * 128, 128)]
            new = old + change * piece
            latent_out[:, pl.ds(r * 128, 128)] = new
            scaled = (new / root).astype(BF16).astype(F32)
            before, after = shift_cols(scaled)
            lanes = pl.ds((r + 1) * 128, 128)
            field[pl.ds(0, 8), lanes] = before
            field[pl.ds(8, 8), lanes] = scaled
            field[pl.ds(16, 8), lanes] = after
        sums = (None, None)
        per_row = count_of(chans, 128)
        for z in range(chips):
            taps = [field[:, pl.ds((z * rows + i) * 128, cells)] for i in range(3)]
            rows_out = dot(in_weight[...], jnp.concatenate(taps, axis=0).astype(BF16)).astype(BF16)
            entry[:, pl.ds(z * cells + 128, cells)] = rows_out
            kept = [rows_out[:, r * 128 : (r + 1) * 128].astype(F32) for r in range(rows)]
            if z == 0:
                pivot, center = pivot_of(kept, gather[...], spread[...], per_row)
            sums = add_deviations(sums, kept, center)
        entry[:, pl.ds(0, 128)] = jnp.zeros((chans, 128), BF16)
        entry[:, pl.ds(full * 128 + 128, 128)] = jnp.zeros((chans, 128), BF16)
        count = per_row * full
        mean, square = finish_stats(pivot, sums, gather[...], count)
        scale = lax.rsqrt(square / count + epsilon)
        moments[:, 0:128], moments[:, 128:256] = channel_moments(mean, scale, spread[...])
        wide[...] = entry[:, pl.ds(pl.multiple_of(place * cells, 128), cells + 256)]

    @pl.when(section != 0)
    def _():
        latent_out[...] = jnp.zeros_like(latent_out)
        mean, scale = decode_stats(forward[pl.ds(chans, GROUPS), pl.ds(0, 128)])
        moments[:, 0:128], moments[:, 128:256] = channel_moments(mean, scale, spread[...])
        wide[:, pl.ds(0, 128)] = forward[pl.ds(0, chans), pl.ds(0, 128)]
        wide[:, pl.ds(128, cells)] = own[...]
        wide[:, pl.ds(cells + 128, 128)] = forward[pl.ds(0, chans), pl.ds(128, 128)]

    source[...] = wide[:, pl.ds(128, cells)]
    tiles = [row_tile(wide, r) for r in range(rows + 2)]
    known = (moments[:, 0:128], moments[:, 128:256] * column(params, 0), column(params, 1))

    def store(start, count, acc):
        out[:, pl.ds(start * 128, count * 128)] = acc
        return acc

    stats_out = conv_all(tiles, known, flags, patches, weight, store, gather[...], spread[...])
    write_messages(out, stats_out, top_msg, bot_msg, st_msg)


def conv_kernel(index, residual, last, ints, params, own, up, down, weight, gather, spread, *rest):
    rest = list(rest)
    base = rest.pop(0) if residual else None
    patches = rest.pop()
    others, (out, top_msg, bot_msg, st_msg) = rest[:-4], rest[-4:]
    chans, cells = own.shape
    rows = cells // 128
    mean, root = gathered(up, down, others, count_of(chans, cells))
    center, scale = channel_moments(mean, root, spread[...])
    tiles = [lambda: up[pl.ds(0, chans), :].astype(F32)]
    tiles += [row_tile(own, r) for r in range(rows)]
    tiles += [lambda: down[pl.ds(0, chans), :].astype(F32)]
    known = (center, scale * column(params, 2 * index), column(params, 2 * index + 1))

    def store(start, count, acc):
        lanes = pl.ds(start * 128, count * 128)
        if residual:
            old = base[:, lanes].astype(F32)
            acc = (old + acc).astype(BF16).astype(F32)
        if last:
            acc = jnp.where(ints[4] >= 2, acc, old)
        out[:, lanes] = acc.astype(out.dtype)
        return acc

    stats_out = conv_all(
        tiles, known, (ints[0], ints[1]), patches, weight, store, gather[...], spread[...]
    )
    write_messages(out, stats_out, top_msg, bot_msg, st_msg)


VM = pl.BlockSpec(memory_space=pltpu.VMEM)
SM = pl.BlockSpec(memory_space=pltpu.SMEM)
HB = pl.BlockSpec(memory_space=pl.ANY)


def call(kernel, outs, in_specs, scratch, flops):
    return pl.pallas_call(
        kernel,
        out_shape=outs,
        in_specs=in_specs,
        out_specs=jax.tree.map(lambda _: VM, outs),
        scratch_shapes=scratch,
        compiler_params=pltpu.CompilerParams(vmem_limit_bytes=VMEM_LIMIT),
        cost_estimate=pl.CostEstimate(flops=flops, bytes_accessed=4_000_000, transcendentals=0),
    )


def sds(shape, dtype):
    return jax.ShapeDtypeStruct(shape, dtype)


def per_device(
    features,
    latent,
    plan_pos,
    blocks_used,
    conv1_w,
    conv2_w,
    norm_gain,
    norm_shift,
    in_w,
    head_w,
    head_gain,
    head_shift,
):
    sections = lax.axis_size("segment")
    patches = lax.axis_size("patch")
    chips = patches // CORES
    section = lax.axis_index("segment")
    core = lax.rem(lax.axis_index("patch"), CORES)
    place = lax.axis_index("patch") // CORES
    _, batch, chans, own_rows, cols = features.shape
    rows = CORES * own_rows
    half = own_rows * cols
    cells = rows * cols
    joint = ("segment", "patch")

    swap_pairs = [(p, p ^ 1) for p in range(patches)]

    def swap(x):
        return lax.ppermute(x, "patch", swap_pairs)

    def around(x, by):
        pairs = [
            (CORES * z + c, CORES * ((z + by) % chips) + c)
            for z in range(chips)
            for c in range(CORES)
        ]
        return lax.ppermute(x, "patch", pairs)

    def device(s, z, c):
        return s * patches + CORES * (z % chips) + c

    def every(shift_section):
        return [
            (s, z, c) for s in shift_section for z in range(chips) for c in range(CORES)
        ]

    def onward(x):
        pairs = [(device(s, z, c), device(s + 1, z, c)) for s, z, c in every(range(sections - 1))]
        return lax.ppermute(x, joint, pairs)

    def to_first(x, by):
        pairs = [
            (device(s, z, c), device(0, z + by, c)) for s, z, c in every([sections - 1])
        ]
        return lax.ppermute(x, joint, pairs)

    group_of = jnp.arange(chans) // (chans // GROUPS)
    member = (jnp.arange(GROUPS)[:, None] == group_of[None, :]).astype(BF16)
    gather = jnp.tile(member, (1, 3))
    spread = jnp.tile(member.T, (1, 3))

    lat = latent.shape[1]
    ints = jnp.stack(
        [
            (place > 0).astype(jnp.int32),
            (place < chips - 1).astype(jnp.int32),
            section.astype(jnp.int32),
            place.astype(jnp.int32),
            blocks_used[0],
            core.astype(jnp.int32),
        ]
    )

    def pick(x, which):
        return lax.dynamic_index_in_dim(x, which, 0, keepdims=False)

    stats_shape = sds((GROUPS, 128), BF16)
    rows_shape = sds((chans + GROUPS, 128), BF16)
    wide_shape = sds((chans, cells), F32)
    half_shape = sds((chans, cells), BF16)
    conv_flops = 2 * 9 * chans * chans * cells
    conv_scratch = [pltpu.VMEM((3 * chans, cells + 256), BF16)]

    own, *messages = call(
        enter_kernel,
        (half_shape, rows_shape, rows_shape, stats_shape),
        [SM] + [VM] * 4,
        [],
        10_000_000,
    )(ints, features[0], swap(pick(features[0], 1 - core)), gather, spread)

    conv1_w, conv2_w, norm_gain, norm_shift, in_w, head_w, latent, _ = lax.optimization_barrier(
        (conv1_w, conv2_w, norm_gain, norm_shift, in_w, head_w, latent, messages[2])
    )
    params = jnp.stack(
        [x[0, k, q] for k in range(2) for q in range(2) for x in (norm_gain, norm_shift)]
        + [head_gain, head_shift]
        + [jnp.zeros((chans,), F32)] * 6
    ).T
    kernels = call(
        pack_kernel, (sds((chans, 9 * chans), BF16),) * 4, [VM, VM], [], 10_000_000
    )(conv1_w, conv2_w)
    head_packed = jnp.zeros((3, 3, 8, chans), BF16)
    head_packed = head_packed.at[:, :, :lat].set(
        jnp.transpose(head_w.reshape(3, 3, lat, chans), (1, 0, 2, 3))
    ).reshape(72, chans)
    in_packed = jnp.zeros((chans, 3, 3, 8), BF16)
    in_packed = in_packed.at[:, :, :, :lat].set(
        jnp.transpose(in_w.reshape(3, 3, chans, lat), (2, 0, 1, 3))
    ).reshape(chans, 72)
    mine = pick(latent, core)
    other = swap(pick(latent, 1 - core))
    latent_rows = jnp.concatenate(
        [jnp.where(core == 0, mine, other), jnp.where(core == 0, other, mine)], axis=1
    ).reshape(lat, cells)
    latent_rows = jnp.concatenate([jnp.zeros((8 - lat, cells), F32), latent_rows], axis=0)
    position = pick(plan_pos, core)
    sigmas = [sigma_at(position + step) for step in range(STEPS + 1)]
    floats = [
        jnp.stack([sigmas[step + 1] - sigmas[step], jnp.sqrt(sigmas[step + 1] ** 2 + 1.0)])
        for step in range(STEPS)
    ]
    full_latent = None

    def exchange(top_msg, bot_msg, st_msg):
        up = around(bot_msg, 1)
        down = around(top_msg, chips - 1)
        return up, down, [st_msg] + [around(st_msg, d) for d in range(2, chips - 1)]

    for step in range(STEPS):
        first_step = step == 0
        own_next = onward(own)
        up, down, others = exchange(*messages)
        height = 8 if first_step else lat
        extra = [latent_rows] if first_step else []
        noise, forward = call(
            head_kernel,
            (sds((height, cells + 256), F32), sds((chans + GROUPS, 256), BF16)),
            [VM] * (6 + len(others) + len(extra)),
            [],
            300_000_000,
        )(params, own, up, down, head_packed, spread, *others, *extra)
        parts = [to_first(noise, d) for d in range(chips)]
        forward_next = onward(forward)
        extra = [] if first_step else [full_latent]
        middle, source, full_latent, *messages = call(
            functools.partial(first_kernel, first_step, chips),
            (
                wide_shape,
                half_shape,
                sds((8, chips * cells), F32),
                rows_shape,
                rows_shape,
                stats_shape,
            ),
            [SM, SM] + [VM] * (7 + chips + len(extra)),
            conv_scratch
            + [
                pltpu.VMEM((chans, cells + 256), BF16),
                pltpu.VMEM((chans, 256), F32),
                pltpu.VMEM((8, chips * cells + 256), F32),
                pltpu.VMEM((24, chips * cells + 256), F32),
                pltpu.VMEM((chans, chips * cells + 256), BF16),
            ],
            conv_flops,
        )(
            ints,
            floats[step],
            params,
            *parts,
            *extra,
            in_packed,
            own_next,
            forward_next,
            kernels[0],
            gather,
            spread,
        )

        def conv(index, own, messages, base, last=False):
            up, down, others = exchange(*messages)
            extra = [] if base is None else [base]
            return call(
                functools.partial(conv_kernel, index, base is not None, last),
                (wide_shape if base is None else half_shape, rows_shape, rows_shape, stats_shape),
                [SM] + [VM] * (7 + len(extra) + len(others)),
                conv_scratch,
                conv_flops,
            )(ints, params, own, up, down, kernels[index], gather, spread, *extra, *others)

        one, *messages = conv(1, middle, messages, source)
        middle, *messages = conv(2, one, messages, None)
        own, *messages = conv(3, middle, messages, one, True)

    def both(low, high):
        mine = jnp.where(core == 0, low, high)
        other = swap(jnp.where(core == 0, high, low))
        pair = jnp.where(core == 0, jnp.stack([mine, other]), jnp.stack([other, mine]))
        return pair.reshape(batch, low.shape[0], own_rows, cols)

    features_out = both(own[:, :half], own[:, half:])[None]
    rows_here = lax.dynamic_slice_in_dim(full_latent, place * cells, cells, 1)[:lat]
    latent_all = both(rows_here[:, :half], rows_here[:, half:])
    share = cols // sections
    latent_out = jnp.zeros((batch, lat, own_rows, share), F32)
    for s in range(sections):
        if s == 0:
            piece = latent_all[..., :share]
        else:
            piece = lax.ppermute(
                latent_all[..., s * share : (s + 1) * share],
                "segment",
                [(q, (q + s) % sections) for q in range(sections)],
            )
        latent_out = jnp.where(section == s, piece, latent_out)
    return (latent_out, features_out)


def solution(mesh):
    placed = (
        P("segment", None, None, "patch", None),
        P(None, None, "patch", None),
        P(),
        P("segment"),
        P("segment", None, None, None, None),
        P("segment", None, None, None, None),
        P("segment", None, None, None),
        P("segment", None, None, None),
        P(),
        P(),
        P(),
        P(),
    )
    return jax.shard_map(
        per_device,
        mesh=mesh,
        in_specs=placed,
        out_specs=(P(None, None, "patch", "segment"), P("segment", None, None, "patch", None)),
        check_vma=False,
    )
```

```python
import functools

import jax
import jax.numpy as jnp
from jax import lax
from jax.experimental import pallas as pl
from jax.experimental.pallas import tpu as pltpu
from jax.sharding import PartitionSpec as P

GROUPS = 32
STEPS = 2
SCHED = 12
CORES = 2

epsilon = 1e-05
sigma_top = 3.0
sigma_low = 0.1
rho_power = 7.0

F32 = jnp.float32
BF16 = jnp.bfloat16
VMEM_LIMIT = 24 * 1024 * 1024


def sigma_at(position):
    fraction = position.astype(F32) / (SCHED - 1)
    top_root = sigma_top ** (1.0 / rho_power)
    low_root = sigma_low ** (1.0 / rho_power)
    return (top_root + fraction * (low_root - top_root)) ** rho_power


def dot(a, b):
    return lax.dot_general(a, b, (((1,), (0,)), ((), ())), preferred_element_type=F32)


def split3(x):
    hi = x.astype(BF16)
    rest = x - hi.astype(F32)
    mid = rest.astype(BF16)
    lo = (rest - mid.astype(F32)).astype(BF16)
    return hi, mid, lo


def group_sum(x, gather):
    parts = jnp.concatenate(split3(x), axis=0)
    return jnp.sum(dot(gather, parts), axis=1, keepdims=True)


def expand(x, spread):
    return dot(spread, jnp.concatenate(split3(x), axis=0))


def tile_sum(tiles):
    total = tiles[0]
    for tile in tiles[1:]:
        total = total + tile
    return total


def pivot_of(tiles, gather, spread, count):
    mean = group_sum(tile_sum(tiles), gather) / (count * len(tiles))
    return mean, expand(jnp.broadcast_to(mean, (GROUPS, 128)), spread)


def add_deviations(sums, tiles, center):
    first, second = sums
    for tile in tiles:
        dev = tile - center
        first = dev if first is None else first + dev
        second = dev * dev if second is None else second + dev * dev
    return first, second


def finish_stats(pivot, sums, gather, count):
    wide = dot(gather, jnp.concatenate(split3(jnp.concatenate(sums, axis=1)), axis=0))
    first = jnp.sum(wide[:, :128], axis=1, keepdims=True)
    second = jnp.sum(wide[:, 128:], axis=1, keepdims=True)
    return pivot + first / count, jnp.maximum(second - first * first / count, 0.0)


def encode_stats(mean, square):
    lane = lax.broadcasted_iota(jnp.int32, (GROUPS, 128), 1) // 16
    out = jnp.zeros((GROUPS, 128), F32)
    for slot, part in enumerate(split3(mean) + split3(square)):
        out = jnp.where(lane == slot, part.astype(F32), out)
    return out.astype(BF16)


def decode_stats(message):
    wide = message.astype(F32)
    take = [wide[:, 16 * k : 16 * k + 1] for k in range(6)]
    return take[0] + take[1] + take[2], take[3] + take[4] + take[5]


def combine_stats(messages, count):
    pairs = [decode_stats(m) for m in messages]
    mean = sum(p[0] for p in pairs) / len(pairs)
    square = sum(p[1] for p in pairs)
    for p in pairs:
        square = square + count * (p[0] - mean) * (p[0] - mean)
    return mean, lax.rsqrt(square / (count * len(pairs)) + epsilon)


def channel_moments(mean, scale, spread):
    both = jnp.concatenate(
        [jnp.broadcast_to(mean, (GROUPS, 128)), jnp.broadcast_to(scale, (GROUPS, 128))], axis=1
    )
    wide = expand(both, spread)
    return wide[:, :128], wide[:, 128:]


def silu(v):
    half = 0.5 * v
    return half + half * jnp.tanh(half)


def shift_cols(t):
    lane = lax.broadcasted_iota(jnp.int32, t.shape, 1)
    before = jnp.where(lane == 0, 0.0, pltpu.roll(t, 1, 1))
    after = jnp.where(lane == 127, 0.0, pltpu.roll(t, 127, 1))
    return before, after


def fill_row(r, last, tile, moments, flags, patches):
    center, scale, shift = moments
    chans = center.shape[0]
    main = chans // 128 * 128
    tail = chans - main
    t = silu((tile - center) * scale + shift)
    if r == 0:
        t = jnp.where(flags[0] > 0, t, 0.0)
    if r == last:
        t = jnp.where(flags[1] > 0, t, 0.0)
    before, after = shift_cols(t)
    lanes = pl.ds(r * 128, 128)
    for j, piece in enumerate((before, t, after)):
        piece = piece.astype(BF16)
        patches[pl.ds(j * main, main), lanes] = piece[:main]
        patches[pl.ds(3 * main + j * tail, tail), lanes] = piece[main:]


def conv_rows(patches, weight, start, rows):
    depth = weight.shape[1] // 9
    main = depth // 128 * 128
    parts = ((0, 3 * main), (3 * main, 3 * (depth - main)))
    pieces = [
        patches[pl.ds(low, size), pl.ds((start + i) * 128, rows * 128)]
        for low, size in parts
        for i in range(3)
    ]
    return dot(weight[...], jnp.concatenate(pieces, axis=0))


CHUNK = 4


def conv_all(tiles, moments, flags, patches, weight, store, gather, spread):
    rows = len(tiles) - 2
    chans = weight.shape[0]
    filled = 0
    per_row = count_of(chans, 128)
    sums = (None, None)
    for start in range(0, rows, CHUNK):
        while filled < start + CHUNK + 2:
            fill_row(filled, rows + 1, tiles[filled](), moments, flags, patches)
            filled += 1
        kept = store(start, CHUNK, conv_rows(patches, weight, start, CHUNK))
        kept = [kept[:, r * 128 : (r + 1) * 128] for r in range(CHUNK)]
        if start == 0:
            pivot, center = pivot_of(kept, gather, spread, per_row)
        sums = add_deviations(sums, kept, center)
    return encode_stats(*finish_stats(pivot, sums, gather, per_row * rows))


def write_messages(out, stats, top_msg, bot_msg, st_msg):
    chans, cells = out.shape
    st_msg[...] = stats
    for ref, start in ((top_msg, 0), (bot_msg, cells - 128)):
        ref[pl.ds(0, chans), :] = out[:, pl.ds(start, 128)].astype(BF16)
        ref[pl.ds(chans, GROUPS), :] = stats


def pack_kernel(first, second, *outs):
    chans = first.shape[3]
    main = chans // 128 * 128
    tail = chans - main
    for n in range(4):
        pieces = []
        for t in range(9):
            tap = (first, second)[n % 2][0, n // 2, t]
            outs[n][:, pl.ds(t * main, main)] = tap[:, :main]
            pieces.append(tap[:, main:])
        outs[n][:, pl.ds(9 * main, 9 * tail)] = jnp.concatenate(pieces, axis=1)


def count_of(chans, cells):
    return float(chans // GROUPS * cells)


def row_tile(ref, r):
    return lambda: ref[:, pl.ds(r * 128, 128)].astype(F32)


def enter_kernel(own, gather, spread, top_msg, bot_msg, st_msg):
    chans, cells = own.shape
    tiles = [own[:, pl.ds(start, 128)].astype(F32) for start in range(0, cells, 128)]
    per_row = count_of(chans, 128)
    pivot, center = pivot_of(tiles[:2], gather[...], spread[...], per_row)
    sums = add_deviations((None, None), tiles, center)
    stats = encode_stats(*finish_stats(pivot, sums, gather[...], per_row * len(tiles)))
    write_messages(own, stats, top_msg, bot_msg, st_msg)


def pair_kernel(ints, kept, other, out):
    lat = kept.shape[0]
    first = ints[5] == 0
    out[0:lat, :] = jnp.where(first, kept[...], other[...])
    out[lat:, :] = jnp.where(first, other[...], kept[...])


def column(params, k):
    return params[:, k : k + 1]


def gathered(up, down, others, count):
    chans = up.shape[0] - GROUPS
    messages = [up[pl.ds(chans, GROUPS), :], down[pl.ds(chans, GROUPS), :]]
    return combine_stats(messages + [ref[...] for ref in others], count)


def head_kernel(params, own, up, down, weight, spread, *rest):
    others, (out, forward) = rest[:-2], rest[-2:]
    latent = None
    if out.shape[0] == 8:
        others, latent = others[:-1], others[-1]
    chans, cells = own.shape
    rows = cells // 128
    mean, root = gathered(up, down, others, count_of(chans, cells))
    stats = encode_stats(mean, root)
    for ref, low in ((up, 0), (down, 128)):
        forward[pl.ds(0, chans), pl.ds(low, 128)] = ref[pl.ds(0, chans), :]
        forward[pl.ds(chans, GROUPS), pl.ds(low, 128)] = stats
    center, scale = channel_moments(mean, root, spread[...])
    scale = scale * column(params, 8)
    shift = column(params, 9)
    tiles = [row_tile(own, r) for r in range(rows)]
    sums = []
    for tile in tiles:
        act = silu((tile() - center) * scale + shift).astype(BF16)
        y = dot(weight[...], act)
        before, _ = shift_cols(y[0:24])
        _, after = shift_cols(y[48:72])
        sums.append(before + y[24:48] + after)
    for r in range(-1, rows + 1):
        acc = jnp.zeros((8, 128), F32)
        for i in range(3):
            if 0 <= r + i - 1 < rows:
                acc = acc + sums[r + i - 1][8 * i : 8 * i + 8]
        if latent is not None and 0 <= r < rows:
            acc = acc + latent[:, pl.ds(r * 128, 128)]
        out[:, pl.ds((r + 1) * 128, 128)] = acc[: out.shape[0]]


def first_kernel(first_step, chips, ints, floats, params, *rest):
    parts, rest = rest[:chips], rest[chips:]
    if not first_step:
        latent_in, rest = rest[0], rest[1:]
    in_weight, own, forward, weight, gather, spread = rest[:6]
    out, source, latent_out, lat_keep, lat_send, top_msg, bot_msg, st_msg = rest[6:14]
    patches, wide, moments, noise, field, entry = rest[14:]
    chans, cells = own.shape
    rows = cells // 128
    full = chips * rows
    flags = (ints[0], ints[1])
    section, place = ints[2], ints[3]

    @pl.when(section == 0)
    def _():
        noise[...] = jnp.zeros_like(noise)
        for d in range(chips):
            owner = lax.rem(place - d + chips, chips)
            lanes = pl.ds(pl.multiple_of(owner * cells, 128), cells + 256)
            height = parts[d].shape[0]
            noise[:height, lanes] = noise[:height, lanes] + parts[d][...]
        change, root = floats[0], floats[1]
        field[...] = jnp.zeros_like(field)
        for r in range(full):
            piece = noise[:, pl.ds((r + 1) * 128, 128)]
            if first_step:
                old = pltpu.roll(piece, 4, 0)
            else:
                old = latent_in[:, pl.ds(r * 128, 128)]
            new = old + change * piece
            latent_out[:, pl.ds(r * 128, 128)] = new
            scaled = (new / root).astype(BF16).astype(F32)
            before, after = shift_cols(scaled)
            lanes = pl.ds((r + 1) * 128, 128)
            field[pl.ds(0, 8), lanes] = before
            field[pl.ds(8, 8), lanes] = scaled
            field[pl.ds(16, 8), lanes] = after
        half = cells // CORES
        for ref, which in ((lat_keep, ints[5]), (lat_send, 1 - ints[5])):
            begin = pl.multiple_of(place * cells + which * half, 128)
            ref[...] = latent_out[: ref.shape[0], pl.ds(begin, half)]
        sums = (None, None)
        per_row = count_of(chans, 128)
        for z in range(chips):
            taps = [field[:, pl.ds((z * rows + i) * 128, cells)] for i in range(3)]
            rows_out = dot(in_weight[...], jnp.concatenate(taps, axis=0).astype(BF16)).astype(BF16)
            entry[:, pl.ds(z * cells + 128, cells)] = rows_out
            kept = [rows_out[:, r * 128 : (r + 1) * 128].astype(F32) for r in range(rows)]
            if z == 0:
                pivot, center = pivot_of(kept, gather[...], spread[...], per_row)
            sums = add_deviations(sums, kept, center)
        entry[:, pl.ds(0, 128)] = jnp.zeros((chans, 128), BF16)
        entry[:, pl.ds(full * 128 + 128, 128)] = jnp.zeros((chans, 128), BF16)
        count = per_row * full
        mean, square = finish_stats(pivot, sums, gather[...], count)
        scale = lax.rsqrt(square / count + epsilon)
        moments[:, 0:128], moments[:, 128:256] = channel_moments(mean, scale, spread[...])
        wide[...] = entry[:, pl.ds(pl.multiple_of(place * cells, 128), cells + 256)]

    @pl.when(section != 0)
    def _():
        latent_out[...] = jnp.zeros_like(latent_out)
        lat_keep[...] = jnp.zeros_like(lat_keep)
        lat_send[...] = jnp.zeros_like(lat_send)
        mean, scale = decode_stats(forward[pl.ds(chans, GROUPS), pl.ds(0, 128)])
        moments[:, 0:128], moments[:, 128:256] = channel_moments(mean, scale, spread[...])
        wide[:, pl.ds(0, 128)] = forward[pl.ds(0, chans), pl.ds(0, 128)]
        wide[:, pl.ds(128, cells)] = own[...]
        wide[:, pl.ds(cells + 128, 128)] = forward[pl.ds(0, chans), pl.ds(128, 128)]

    source[...] = wide[:, pl.ds(128, cells)]
    tiles = [row_tile(wide, r) for r in range(rows + 2)]
    known = (moments[:, 0:128], moments[:, 128:256] * column(params, 0), column(params, 1))

    def store(start, count, acc):
        out[:, pl.ds(start * 128, count * 128)] = acc
        return acc

    stats_out = conv_all(tiles, known, flags, patches, weight, store, gather[...], spread[...])
    write_messages(out, stats_out, top_msg, bot_msg, st_msg)


def conv_kernel(index, residual, last, ints, params, own, up, down, weight, gather, spread, *rest):
    rest = list(rest)
    base = rest.pop(0) if residual else None
    patches = rest.pop()
    others, (out, top_msg, bot_msg, st_msg) = rest[:-4], rest[-4:]
    chans, cells = own.shape
    rows = cells // 128
    mean, root = gathered(up, down, others, count_of(chans, cells))
    center, scale = channel_moments(mean, root, spread[...])
    tiles = [lambda: up[pl.ds(0, chans), :].astype(F32)]
    tiles += [row_tile(own, r) for r in range(rows)]
    tiles += [lambda: down[pl.ds(0, chans), :].astype(F32)]
    known = (center, scale * column(params, 2 * index), column(params, 2 * index + 1))

    def store(start, count, acc):
        lanes = pl.ds(start * 128, count * 128)
        if residual:
            old = base[:, lanes].astype(F32)
            acc = (old + acc).astype(BF16).astype(F32)
        if last:
            acc = jnp.where(ints[4] >= 2, acc, old)
        out[:, lanes] = acc.astype(out.dtype)
        return acc

    stats_out = conv_all(
        tiles, known, (ints[0], ints[1]), patches, weight, store, gather[...], spread[...]
    )
    write_messages(out, stats_out, top_msg, bot_msg, st_msg)


VM = pl.BlockSpec(memory_space=pltpu.VMEM)
SM = pl.BlockSpec(memory_space=pltpu.SMEM)
HB = pl.BlockSpec(memory_space=pl.ANY)


def call(kernel, outs, in_specs, scratch, flops):
    return pl.pallas_call(
        kernel,
        out_shape=outs,
        in_specs=in_specs,
        out_specs=jax.tree.map(lambda _: VM, outs),
        scratch_shapes=scratch,
        compiler_params=pltpu.CompilerParams(vmem_limit_bytes=VMEM_LIMIT),
        cost_estimate=pl.CostEstimate(flops=flops, bytes_accessed=4_000_000, transcendentals=0),
    )


def sds(shape, dtype):
    return jax.ShapeDtypeStruct(shape, dtype)


def per_device(
    features,
    latent,
    plan_pos,
    blocks_used,
    conv1_w,
    conv2_w,
    norm_gain,
    norm_shift,
    in_w,
    head_w,
    head_gain,
    head_shift,
):
    sections = lax.axis_size("segment")
    patches = lax.axis_size("patch")
    chips = patches // CORES
    section = lax.axis_index("segment")
    core = lax.rem(lax.axis_index("patch"), CORES)
    place = lax.axis_index("patch") // CORES
    _, batch, chans, own_rows, cols = features.shape
    rows = CORES * own_rows
    half = own_rows * cols
    cells = rows * cols
    joint = ("segment", "patch")

    swap_pairs = [(p, p ^ 1) for p in range(patches)]

    def swap(x):
        return lax.ppermute(x, "patch", swap_pairs)

    def around(x, by):
        pairs = [
            (CORES * z + c, CORES * ((z + by) % chips) + c)
            for z in range(chips)
            for c in range(CORES)
        ]
        return lax.ppermute(x, "patch", pairs)

    def device(s, z, c):
        return s * patches + CORES * (z % chips) + c

    def every(shift_section):
        return [
            (s, z, c) for s in shift_section for z in range(chips) for c in range(CORES)
        ]

    def onward(x):
        pairs = [(device(s, z, c), device(s + 1, z, c)) for s, z, c in every(range(sections - 1))]
        return lax.ppermute(x, joint, pairs)

    def to_first(x, by):
        pairs = [
            (device(s, z, c), device((s + 1) % sections, z + by, c))
            for s, z, c in every(range(sections))
        ]
        return lax.ppermute(x, joint, pairs)

    group_of = jnp.arange(chans) // (chans // GROUPS)
    member = (jnp.arange(GROUPS)[:, None] == group_of[None, :]).astype(BF16)
    gather = jnp.tile(member, (1, 3))
    spread = jnp.tile(member.T, (1, 3))

    lat = latent.shape[1]
    ints = jnp.stack(
        [
            (place > 0).astype(jnp.int32),
            (place < chips - 1).astype(jnp.int32),
            section.astype(jnp.int32),
            place.astype(jnp.int32),
            blocks_used[0],
            core.astype(jnp.int32),
        ]
    )

    def pick(x, which):
        return lax.dynamic_index_in_dim(x, which, 0, keepdims=False)

    stats_shape = sds((GROUPS, 128), BF16)
    rows_shape = sds((chans + GROUPS, 128), BF16)
    wide_shape = sds((chans, cells), F32)
    half_shape = sds((chans, cells), BF16)
    conv_flops = 2 * 9 * chans * chans * cells
    conv_scratch = [pltpu.VMEM((3 * chans, cells + 256), BF16)]

    first_core = core == 0
    mine = pick(features[0], core)
    other = swap(pick(features[0], 1 - core))
    own = jnp.concatenate(
        [jnp.where(first_core, mine, other), jnp.where(first_core, other, mine)], axis=1
    ).reshape(chans, cells)
    messages = call(
        enter_kernel, (rows_shape, rows_shape, stats_shape), [VM] * 3, [], 10_000_000
    )(own, gather, spread)

    conv1_w, conv2_w, norm_gain, norm_shift, in_w, head_w, latent, _ = lax.optimization_barrier(
        (conv1_w, conv2_w, norm_gain, norm_shift, in_w, head_w, latent, messages[2])
    )
    params = jnp.stack(
        [x[0, k, q] for k in range(2) for q in range(2) for x in (norm_gain, norm_shift)]
        + [head_gain, head_shift]
        + [jnp.zeros((chans,), F32)] * 6
    ).T
    kernels = call(
        pack_kernel, (sds((chans, 9 * chans), BF16),) * 4, [VM, VM], [], 10_000_000
    )(conv1_w, conv2_w)
    head_packed = jnp.zeros((3, 3, 8, chans), BF16)
    head_packed = head_packed.at[:, :, :lat].set(
        jnp.transpose(head_w.reshape(3, 3, lat, chans), (1, 0, 2, 3))
    ).reshape(72, chans)
    in_packed = jnp.zeros((chans, 3, 3, 8), BF16)
    in_packed = in_packed.at[:, :, :, :lat].set(
        jnp.transpose(in_w.reshape(3, 3, chans, lat), (2, 0, 1, 3))
    ).reshape(chans, 72)
    mine = pick(latent, core)
    other = swap(pick(latent, 1 - core))
    latent_rows = jnp.concatenate(
        [jnp.where(core == 0, mine, other), jnp.where(core == 0, other, mine)], axis=1
    ).reshape(lat, cells)
    latent_rows = jnp.concatenate([jnp.zeros((8 - lat, cells), F32), latent_rows], axis=0)
    position = pick(plan_pos, core)
    sigmas = [sigma_at(position + step) for step in range(STEPS + 1)]
    floats = [
        jnp.stack([sigmas[step + 1] - sigmas[step], jnp.sqrt(sigmas[step + 1] ** 2 + 1.0)])
        for step in range(STEPS)
    ]
    full_latent = None

    def exchange(top_msg, bot_msg, st_msg):
        up = around(bot_msg, 1)
        down = around(top_msg, chips - 1)
        return up, down, [st_msg] + [around(st_msg, d) for d in range(2, chips - 1)]

    for step in range(STEPS):
        first_step = step == 0
        own_next = onward(own)
        up, down, others = exchange(*messages)
        height = 8 if first_step else lat
        extra = [latent_rows] if first_step else []
        noise, forward = call(
            head_kernel,
            (sds((height, cells + 256), F32), sds((chans + GROUPS, 256), BF16)),
            [VM] * (6 + len(others) + len(extra)),
            [],
            300_000_000,
        )(params, own, up, down, head_packed, spread, *others, *extra)
        parts = [to_first(noise, d) for d in range(chips)]
        forward_next = onward(forward)
        extra = [] if first_step else [full_latent]
        middle, source, full_latent, lat_keep, lat_send, *messages = call(
            functools.partial(first_kernel, first_step, chips),
            (
                wide_shape,
                half_shape,
                sds((8, chips * cells), F32),
                sds((lat, half), F32),
                sds((lat, half), F32),
                rows_shape,
                rows_shape,
                stats_shape,
            ),
            [SM, SM] + [VM] * (7 + chips + len(extra)),
            conv_scratch
            + [
                pltpu.VMEM((chans, cells + 256), BF16),
                pltpu.VMEM((chans, 256), F32),
                pltpu.VMEM((8, chips * cells + 256), F32),
                pltpu.VMEM((24, chips * cells + 256), F32),
                pltpu.VMEM((chans, chips * cells + 256), BF16),
            ],
            conv_flops,
        )(
            ints,
            floats[step],
            params,
            *parts,
            *extra,
            in_packed,
            own_next,
            forward_next,
            kernels[0],
            gather,
            spread,
        )

        if step == STEPS - 1:
            latents = call(
                pair_kernel, sds((CORES * lat, half), F32), [SM, VM, VM], [], 100_000
            )(ints, lat_keep, swap(lat_send))
            shares = [latents] + [
                lax.ppermute(
                    latents, "segment", [(q, (q + s) % sections) for q in range(sections)]
                )
                for s in range(1, sections)
            ]

        def conv(index, own, messages, base, last=False):
            up, down, others = exchange(*messages)
            extra = [] if base is None else [base]
            return call(
                functools.partial(conv_kernel, index, base is not None, last),
                (wide_shape if base is None else half_shape, rows_shape, rows_shape, stats_shape),
                [SM] + [VM] * (7 + len(extra) + len(others)),
                conv_scratch,
                conv_flops,
            )(ints, params, own, up, down, kernels[index], gather, spread, *extra, *others)

        one, *messages = conv(1, middle, messages, source)
        middle, *messages = conv(2, one, messages, None)
        own, *messages = conv(3, middle, messages, one, True)

    own, *shares = lax.optimization_barrier((own, *shares))
    low, high = own[:, :half], own[:, half:]
    mine = jnp.where(first_core, low, high)
    other = swap(jnp.where(first_core, high, low))
    pair = jnp.where(first_core, jnp.stack([mine, other]), jnp.stack([other, mine]))
    features_out = pair.reshape(1, batch, chans, own_rows, cols)
    share = cols // sections
    latent_out = None
    for s, piece in enumerate(shares):
        piece = piece.reshape(batch, lat, own_rows, cols)[..., s * share : (s + 1) * share]
        latent_out = piece if latent_out is None else jnp.where(section == s, piece, latent_out)
    return (latent_out, features_out)


def solution(mesh):
    placed = (
        P("segment", None, None, "patch", None),
        P(None, None, "patch", None),
        P(),
        P("segment"),
        P("segment", None, None, None, None),
        P("segment", None, None, None, None),
        P("segment", None, None, None),
        P("segment", None, None, None),
        P(),
        P(),
        P(),
        P(),
    )
    return jax.shard_map(
        per_device,
        mesh=mesh,
        in_specs=placed,
        out_specs=(P(None, None, "patch", "segment"), P("segment", None, None, "patch", None)),
        check_vma=False,
    )
```

```python
import functools

import jax
import jax.numpy as jnp
import numpy as np
from jax import lax
from jax.experimental import pallas as pl
from jax.experimental.pallas import tpu as pltpu
from jax.sharding import PartitionSpec as P

GROUPS = 32
STEPS = 2
SCHED = 12
CORES = 2

epsilon = 1e-05
sigma_top = 3.0
sigma_low = 0.1
rho_power = 7.0

F32 = jnp.float32
BF16 = jnp.bfloat16
VMEM_LIMIT = 24 * 1024 * 1024


def sigma_at(position):
    fraction = position.astype(F32) / (SCHED - 1)
    top_root = sigma_top ** (1.0 / rho_power)
    low_root = sigma_low ** (1.0 / rho_power)
    return (top_root + fraction * (low_root - top_root)) ** rho_power


def dot(a, b):
    return lax.dot_general(a, b, (((1,), (0,)), ((), ())), preferred_element_type=F32)


def split3(x):
    hi = x.astype(BF16)
    rest = x - hi.astype(F32)
    mid = rest.astype(BF16)
    lo = (rest - mid.astype(F32)).astype(BF16)
    return hi, mid, lo


def group_lanes(x, gather):
    return dot(gather, jnp.concatenate(split3(x)[:2], axis=0))


def group_sum(x, gather):
    return jnp.sum(group_lanes(x, gather), axis=1, keepdims=True)


def expand(x, spread):
    return dot(spread, jnp.concatenate(split3(x), axis=0))


def tile_sum(tiles):
    total = tiles[0]
    for tile in tiles[1:]:
        total = total + tile
    return total


def pivot_of(tiles, gather, spread, count):
    mean = group_sum(tile_sum(tiles), gather) / (count * len(tiles))
    return mean, expand(jnp.broadcast_to(mean, (GROUPS, 128)), spread)


def add_deviations(sums, tiles, center):
    first, second = sums
    for tile in tiles:
        dev = tile - center
        first = dev if first is None else first + dev
        second = dev * dev if second is None else second + dev * dev
    return first, second


def finish_stats(pivot, sums, gather, count):
    wide = group_lanes(jnp.concatenate(sums, axis=1), gather)
    first = jnp.sum(wide[:, :128], axis=1, keepdims=True)
    second = jnp.sum(wide[:, 128:], axis=1, keepdims=True)
    return pivot + first / count, jnp.maximum(second - first * first / count, 0.0)


def encode_stats(mean, square):
    lane = lax.broadcasted_iota(jnp.int32, (GROUPS, 128), 1) // 16
    out = jnp.zeros((GROUPS, 128), F32)
    for slot, part in enumerate(split3(mean) + split3(square)):
        out = jnp.where(lane == slot, part.astype(F32), out)
    return out.astype(BF16)


def decode_stats(message):
    wide = message.astype(F32)
    take = [wide[:, 16 * k : 16 * k + 1] for k in range(6)]
    return take[0] + take[1] + take[2], take[3] + take[4] + take[5]


def combine_stats(messages, count):
    pairs = [decode_stats(m) for m in messages]
    mean = sum(p[0] for p in pairs) / len(pairs)
    square = sum(p[1] for p in pairs)
    for p in pairs:
        square = square + count * (p[0] - mean) * (p[0] - mean)
    return mean, lax.rsqrt(square / (count * len(pairs)) + epsilon)


def channel_moments(mean, scale, spread):
    both = jnp.concatenate(
        [jnp.broadcast_to(mean, (GROUPS, 128)), jnp.broadcast_to(scale, (GROUPS, 128))], axis=1
    )
    wide = expand(both, spread)
    return wide[:, :128], wide[:, 128:]


def silu(v):
    half = 0.5 * v
    return half + half * jnp.tanh(half)


def shift_cols(t):
    lane = lax.broadcasted_iota(jnp.int32, t.shape, 1)
    before = jnp.where(lane == 0, 0.0, pltpu.roll(t, 1, 1))
    after = jnp.where(lane == 127, 0.0, pltpu.roll(t, 127, 1))
    return before, after


def fill_row(r, last, tile, moments, flags, patches):
    center, scale, shift = moments
    chans = center.shape[0]
    main = chans // 128 * 128
    tail = chans - main
    t = silu((tile - center) * scale + shift)
    if r == 0:
        t = jnp.where(flags[0] > 0, t, 0.0)
    if r == last:
        t = jnp.where(flags[1] > 0, t, 0.0)
    before, after = shift_cols(t)
    lanes = pl.ds(r * 128, 128)
    for j, piece in enumerate((before, t, after)):
        piece = piece.astype(BF16)
        patches[pl.ds(j * main, main), lanes] = piece[:main]
        patches[pl.ds(3 * main + j * tail, tail), lanes] = piece[main:]


def conv_rows(patches, weight, start, rows):
    depth = weight.shape[1] // 9
    main = depth // 128 * 128
    parts = ((0, 3 * main), (3 * main, 3 * (depth - main)))
    pieces = [
        patches[pl.ds(low, size), pl.ds((start + i) * 128, rows * 128)]
        for low, size in parts
        for i in range(3)
    ]
    return dot(weight[...], jnp.concatenate(pieces, axis=0))


CHUNK = 4


def conv_all(tiles, moments, flags, patches, weight, store, gather=None, spread=None):
    rows = len(tiles) - 2
    chans = weight.shape[0]
    filled = 0
    per_row = count_of(chans, 128)
    sums = (None, None)
    for start in range(0, rows, CHUNK):
        while filled < start + CHUNK + 2:
            fill_row(filled, rows + 1, tiles[filled](), moments, flags, patches)
            filled += 1
        kept = store(start, CHUNK, conv_rows(patches, weight, start, CHUNK))
        if gather is None:
            continue
        kept = [kept[:, r * 128 : (r + 1) * 128] for r in range(CHUNK)]
        if start == 0:
            pivot, center = pivot_of(kept, gather, spread, per_row)
        sums = add_deviations(sums, kept, center)
    if gather is None:
        return None
    return encode_stats(*finish_stats(pivot, sums, gather, per_row * rows))


def write_messages(out, stats, top_msg, bot_msg, st_msg):
    chans, cells = out.shape
    st_msg[...] = stats
    for ref, start in ((top_msg, 0), (bot_msg, cells - 128)):
        ref[pl.ds(0, chans), :] = out[:, pl.ds(start, 128)].astype(BF16)
        ref[pl.ds(chans, GROUPS), :] = stats


def pack_kernel(block, taps_in, out, taps, sem):
    copy = pltpu.make_async_copy(taps_in.at[0, block], taps, sem)
    copy.start()
    copy.wait()
    chans = taps.shape[1]
    main = chans // 128 * 128
    tail = chans - main
    pieces = []
    for t in range(9):
        tap = taps[t]
        out[:, pl.ds(t * main, main)] = tap[:, :main]
        pieces.append(tap[:, main:])
    out[:, pl.ds(9 * main, 9 * tail)] = jnp.concatenate(pieces, axis=1)


def count_of(chans, cells):
    return float(chans // GROUPS * cells)


def row_tile(ref, r):
    return lambda: ref[:, pl.ds(r * 128, 128)].astype(F32)


def enter_kernel(own, gather, spread, top_msg, bot_msg, st_msg):
    chans, cells = own.shape
    tiles = [own[:, pl.ds(start, 128)].astype(F32) for start in range(0, cells, 128)]
    per_row = count_of(chans, 128)
    pivot, center = pivot_of(tiles[:2], gather[...], spread[...], per_row)
    sums = add_deviations((None, None), tiles, center)
    stats = encode_stats(*finish_stats(pivot, sums, gather[...], per_row * len(tiles)))
    write_messages(own, stats, top_msg, bot_msg, st_msg)


def pair_kernel(ints, kept, other, out):
    lat = kept.shape[0]
    first = ints[5] == 0
    out[0:lat, :] = jnp.where(first, kept[...], other[...])
    out[lat:, :] = jnp.where(first, other[...], kept[...])


def column(params, k):
    return params[:, k : k + 1]


def gathered(up, down, others, count):
    chans = up.shape[0] - GROUPS
    messages = [up[pl.ds(chans, GROUPS), :], down[pl.ds(chans, GROUPS), :]]
    return combine_stats(messages + [ref[...] for ref in others], count)


def head_kernel(early, params, own, up, down, weight, spread, *rest):
    others, (out, forward) = rest[: len(rest) - 2 - early], rest[-2:]
    latent = None
    if out.shape[0] == 8:
        others, latent = others[:-1], others[-1]
    chans, cells = own.shape
    rows = cells // 128
    mean, root = gathered(up, down, others, count_of(chans, cells))
    stats = encode_stats(mean, root)
    for ref, low in ((up, 0), (down, 128)):
        forward[pl.ds(0, chans), pl.ds(low, 128)] = ref[pl.ds(0, chans), :]
        forward[pl.ds(chans, GROUPS), pl.ds(low, 128)] = stats
    center, scale = channel_moments(mean, root, spread[...])
    scale = scale * column(params, 8)
    shift = column(params, 9)
    tiles = [row_tile(own, r) for r in range(rows)]
    sums = []
    for tile in tiles:
        act = silu((tile() - center) * scale + shift).astype(BF16)
        y = dot(weight[...], act)
        before, _ = shift_cols(y[0:24])
        _, after = shift_cols(y[48:72])
        sums.append(before + y[24:48] + after)
    for r in range(-1, rows + 1):
        acc = jnp.zeros((8, 128), F32)
        for i in range(3):
            if 0 <= r + i - 1 < rows:
                acc = acc + sums[r + i - 1][8 * i : 8 * i + 8]
        if latent is not None and 0 <= r < rows:
            acc = acc + latent[:, pl.ds(r * 128, 128)]
        out[:, pl.ds((r + 1) * 128, 128)] = acc[: out.shape[0]]


def first_kernel(first_step, chips, ints, floats, params, *rest):
    parts, rest = rest[:chips], rest[chips:]
    if not first_step:
        latent_in, rest = rest[0], rest[1:]
    in_weight, own, forward, weight, gather, spread = rest[:6]
    out, source, latent_out, lat_keep, lat_send, top_msg, bot_msg, st_msg = rest[6:14]
    patches, wide, moments, noise, field, entry = rest[14:]
    chans, cells = own.shape
    rows = cells // 128
    full = chips * rows
    flags = (ints[0], ints[1])
    section, place = ints[2], ints[3]

    @pl.when(section == 0)
    def _():
        noise[...] = jnp.zeros_like(noise)
        for d in range(chips):
            owner = lax.rem(place - d + chips, chips)
            lanes = pl.ds(pl.multiple_of(owner * cells, 128), cells + 256)
            height = parts[d].shape[0]
            noise[:height, lanes] = noise[:height, lanes] + parts[d][...]
        change, root = floats[0], floats[1]
        field[...] = jnp.zeros_like(field)
        for r in range(full):
            piece = noise[:, pl.ds((r + 1) * 128, 128)]
            if first_step:
                old = pltpu.roll(piece, 4, 0)
            else:
                old = latent_in[:, pl.ds(r * 128, 128)]
            new = old + change * piece
            latent_out[:, pl.ds(r * 128, 128)] = new
            scaled = (new / root).astype(BF16).astype(F32)
            before, after = shift_cols(scaled)
            lanes = pl.ds((r + 1) * 128, 128)
            field[pl.ds(0, 8), lanes] = before
            field[pl.ds(8, 8), lanes] = scaled
            field[pl.ds(16, 8), lanes] = after
        half = cells // CORES
        for ref, which in ((lat_keep, ints[5]), (lat_send, 1 - ints[5])):
            begin = pl.multiple_of(place * cells + which * half, 128)
            ref[...] = latent_out[: ref.shape[0], pl.ds(begin, half)]
        sums = (None, None)
        per_row = count_of(chans, 128)
        for z in range(chips):
            taps = [field[:, pl.ds((z * rows + i) * 128, cells)] for i in range(3)]
            rows_out = dot(in_weight[...], jnp.concatenate(taps, axis=0).astype(BF16)).astype(BF16)
            entry[:, pl.ds(z * cells + 128, cells)] = rows_out
            kept = [rows_out[:, r * 128 : (r + 1) * 128].astype(F32) for r in range(rows)]
            if z == 0:
                pivot, center = pivot_of(kept, gather[...], spread[...], per_row)
            sums = add_deviations(sums, kept, center)
        entry[:, pl.ds(0, 128)] = jnp.zeros((chans, 128), BF16)
        entry[:, pl.ds(full * 128 + 128, 128)] = jnp.zeros((chans, 128), BF16)
        count = per_row * full
        mean, square = finish_stats(pivot, sums, gather[...], count)
        scale = lax.rsqrt(square / count + epsilon)
        moments[:, 0:128], moments[:, 128:256] = channel_moments(mean, scale, spread[...])
        wide[...] = entry[:, pl.ds(pl.multiple_of(place * cells, 128), cells + 256)]

    @pl.when(section != 0)
    def _():
        latent_out[...] = jnp.zeros_like(latent_out)
        lat_keep[...] = jnp.zeros_like(lat_keep)
        lat_send[...] = jnp.zeros_like(lat_send)
        mean, scale = decode_stats(forward[pl.ds(chans, GROUPS), pl.ds(0, 128)])
        moments[:, 0:128], moments[:, 128:256] = channel_moments(mean, scale, spread[...])
        wide[:, pl.ds(0, 128)] = forward[pl.ds(0, chans), pl.ds(0, 128)]
        wide[:, pl.ds(128, cells)] = own[...]
        wide[:, pl.ds(cells + 128, 128)] = forward[pl.ds(0, chans), pl.ds(128, 128)]

    source[...] = wide[:, pl.ds(128, cells)]
    tiles = [row_tile(wide, r) for r in range(rows + 2)]
    known = (moments[:, 0:128], moments[:, 128:256] * column(params, 0), column(params, 1))

    def store(start, count, acc):
        out[:, pl.ds(start * 128, count * 128)] = acc
        return acc

    stats_out = conv_all(tiles, known, flags, patches, weight, store, gather[...], spread[...])
    write_messages(out, stats_out, top_msg, bot_msg, st_msg)


def conv_kernel(index, residual, last, ints, params, own, up, down, weight, gather, spread, *rest):
    rest = list(rest)
    base = rest.pop(0) if residual else None
    patches = rest.pop()
    final = last == "final"
    given = 1 if final else 4
    others, outs = rest[:-given], rest[-given:]
    out = outs[0]
    chans, cells = own.shape
    rows = cells // 128
    mean, root = gathered(up, down, others, count_of(chans, cells))
    center, scale = channel_moments(mean, root, spread[...])
    tiles = [lambda: up[pl.ds(0, chans), :].astype(F32)]
    tiles += [row_tile(own, r) for r in range(rows)]
    tiles += [lambda: down[pl.ds(0, chans), :].astype(F32)]
    known = (center, scale * column(params, 2 * index), column(params, 2 * index + 1))

    def store(start, count, acc):
        lanes = pl.ds(start * 128, count * 128)
        if residual:
            old = base[:, lanes].astype(F32)
            acc = (old + acc).astype(BF16).astype(F32)
        if last:
            acc = jnp.where(ints[4] >= 2, acc, old)
        out[:, lanes] = acc.astype(out.dtype)
        return acc

    sums = () if final else (gather[...], spread[...])
    stats_out = conv_all(tiles, known, (ints[0], ints[1]), patches, weight, store, *sums)
    if not final:
        write_messages(out, stats_out, *outs[1:])


VM = pl.BlockSpec(memory_space=pltpu.VMEM)
SM = pl.BlockSpec(memory_space=pltpu.SMEM)
HB = pl.BlockSpec(memory_space=pl.ANY)


def call(kernel, outs, in_specs, scratch, flops):
    return pl.pallas_call(
        kernel,
        out_shape=outs,
        in_specs=in_specs,
        out_specs=jax.tree.map(lambda _: VM, outs),
        scratch_shapes=scratch,
        compiler_params=pltpu.CompilerParams(vmem_limit_bytes=VMEM_LIMIT),
        cost_estimate=pl.CostEstimate(flops=flops, bytes_accessed=4_000_000, transcendentals=0),
    )


def sds(shape, dtype):
    return jax.ShapeDtypeStruct(shape, dtype)


def per_device(
    features,
    latent,
    plan_pos,
    blocks_used,
    conv1_w,
    conv2_w,
    norm_gain,
    norm_shift,
    in_w,
    head_w,
    head_gain,
    head_shift,
):
    sections = lax.axis_size("segment")
    patches = lax.axis_size("patch")
    chips = patches // CORES
    section = lax.axis_index("segment")
    core = lax.rem(lax.axis_index("patch"), CORES)
    place = lax.axis_index("patch") // CORES
    _, batch, chans, own_rows, cols = features.shape
    rows = CORES * own_rows
    half = own_rows * cols
    cells = rows * cols
    joint = ("segment", "patch")

    swap_pairs = [(p, p ^ 1) for p in range(patches)]

    def swap(x):
        return lax.ppermute(x, "patch", swap_pairs)

    def by_core(m, l):
        return CORES * (l % chips) + m

    def by_chips(m, l):
        return m * chips + ((l % chips) ^ ((l % chips) >> 1))

    blocks = [(m, l) for m in range(CORES) for l in range(chips)]

    def around(layout, x, by):
        return lax.ppermute(x, "patch", [(layout(m, l), layout(m, l + by)) for m, l in blocks])

    def onward(source, target, x):
        pairs = [
            (s * patches + source(m, l), (s + 1) % sections * patches + target(m, l))
            for s in range(sections)
            for m, l in blocks
        ]
        return lax.ppermute(x, joint, pairs)

    def to_first(source, target, x, by):
        pairs = [
            (s * patches + source(m, l), (s + 1) % sections * patches + target(m, l + by))
            for s in range(sections)
            for m, l in blocks
        ]
        return lax.ppermute(x, joint, pairs)

    group_of = np.arange(chans) // (chans // GROUPS)
    member = (np.arange(GROUPS)[:, None] == group_of[None, :]).astype(np.float32)
    gather = jnp.asarray(np.tile(member, (1, 2)), BF16)
    spread = jnp.asarray(np.tile(member.T, (1, 3)), BF16)

    lat = latent.shape[1]
    group, rank = lax.axis_index("patch") // chips, lax.rem(lax.axis_index("patch"), chips)
    turn = 1
    while turn < chips:
        rank = rank ^ (rank >> turn)
        turn *= 2

    def describe(row_block):
        return jnp.stack(
            [
                (row_block > 0).astype(jnp.int32),
                (row_block < chips - 1).astype(jnp.int32),
                section.astype(jnp.int32),
                row_block.astype(jnp.int32),
                blocks_used[0],
                core.astype(jnp.int32),
            ]
        )

    def pick(x, which):
        return lax.dynamic_index_in_dim(x, which, 0, keepdims=False)

    stats_shape = sds((GROUPS, 128), BF16)
    rows_shape = sds((chans + GROUPS, 128), BF16)
    wide_shape = sds((chans, cells), F32)
    half_shape = sds((chans, cells), BF16)
    conv_flops = 2 * 9 * chans * chans * cells
    conv_scratch = [pltpu.VMEM((3 * chans, cells + 256), BF16)]

    first_core = core == 0
    mine = pick(features[0], core)
    other = swap(pick(features[0], 1 - core))
    own = jnp.concatenate(
        [jnp.where(first_core, mine, other), jnp.where(first_core, other, mine)], axis=1
    ).reshape(chans, cells)
    messages = call(
        enter_kernel, (rows_shape, rows_shape, stats_shape), [VM] * 3, [], 10_000_000
    )(own, gather, spread)

    given = (conv1_w, conv2_w, norm_gain, norm_shift, in_w, head_w, head_gain, head_shift)
    *given, latent, plan_pos, _ = lax.optimization_barrier((*given, latent, plan_pos, messages[2]))
    conv1_w, conv2_w, norm_gain, norm_shift, in_w, head_w, head_gain, head_shift = given
    params = jnp.stack(
        [x[0, k, q] for k in range(2) for q in range(2) for x in (norm_gain, norm_shift)]
        + [head_gain, head_shift]
        + [jnp.zeros((chans,), F32)] * 6
    ).T
    kernels = [
        call(
            functools.partial(pack_kernel, block),
            sds((chans, 9 * chans), BF16),
            [HB],
            [pltpu.VMEM(taps.shape[2:], BF16), pltpu.SemaphoreType.DMA(())],
            10_000_000,
        )(taps)
        for block in range(2)
        for taps in (conv1_w, conv2_w)
    ]
    head_packed = jnp.zeros((3, 3, 8, chans), BF16)
    head_packed = head_packed.at[:, :, :lat].set(
        jnp.transpose(head_w.reshape(3, 3, lat, chans), (1, 0, 2, 3))
    ).reshape(72, chans)
    in_packed = jnp.zeros((chans, 3, 3, 8), BF16)
    in_packed = in_packed.at[:, :, :, :lat].set(
        jnp.transpose(in_w.reshape(3, 3, chans, lat), (2, 0, 1, 3))
    ).reshape(chans, 72)
    mine = pick(latent, core)
    other = swap(pick(latent, 1 - core))
    latent_rows = jnp.concatenate(
        [jnp.where(core == 0, mine, other), jnp.where(core == 0, other, mine)], axis=1
    ).reshape(lat, cells)
    latent_rows = jnp.concatenate([jnp.zeros((8 - lat, cells), F32), latent_rows], axis=0)
    layouts = (by_core,) * (STEPS + 1)
    described = {by_core: describe(place), by_chips: describe(rank)}
    floats = []
    for step in range(STEPS):
        position = pick(plan_pos, core if layouts[step + 1] is by_core else group) + step
        now, later = sigma_at(position), sigma_at(position + 1)
        floats.append(jnp.stack([later - now, jnp.sqrt(later * later + 1.0)]))
    full_latent = None

    def exchange(layout, top_msg, bot_msg, st_msg):
        up = around(layout, bot_msg, 1)
        down = around(layout, top_msg, chips - 1)
        return up, down, [st_msg] + [around(layout, st_msg, d) for d in range(2, chips - 1)]

    for step in range(STEPS):
        first_step = step == 0
        before, layout = layouts[step], layouts[step + 1]
        ints = described[layout]
        own_next = onward(before, layout, own)
        up, down, others = exchange(before, *messages)
        height = 8 if first_step else lat
        extra = [latent_rows] if first_step else []
        early = []
        noise, forward = call(
            functools.partial(head_kernel, len(early)),
            (sds((height, cells + 256), F32), sds((chans + GROUPS, 256), BF16)),
            [VM] * (6 + len(others) + len(extra)) + [HB] * len(early),
            [],
            300_000_000,
        )(params, own, up, down, head_packed, spread, *others, *extra, *early)
        parts = [to_first(before, layout, noise, d) for d in range(chips)]
        forward_next = onward(before, layout, forward)
        extra = []
        if not first_step:
            extra = [full_latent]
            if before is not layout:
                moves = [(before(m, l), layout(m, l)) for m, l in blocks]
                extra = [lax.ppermute(full_latent, "patch", moves)]
        middle, source, full_latent, lat_keep, lat_send, *messages = call(
            functools.partial(first_kernel, first_step, chips),
            (
                wide_shape,
                half_shape,
                sds((8, chips * cells), F32),
                sds((lat, half), F32),
                sds((lat, half), F32),
                rows_shape,
                rows_shape,
                stats_shape,
            ),
            [SM, SM] + [VM] * (7 + chips + len(extra)),
            conv_scratch
            + [
                pltpu.VMEM((chans, cells + 256), BF16),
                pltpu.VMEM((chans, 256), F32),
                pltpu.VMEM((8, chips * cells + 256), F32),
                pltpu.VMEM((24, chips * cells + 256), F32),
                pltpu.VMEM((chans, chips * cells + 256), BF16),
            ],
            conv_flops,
        )(
            ints,
            floats[step],
            params,
            *parts,
            *extra,
            in_packed,
            own_next,
            forward_next,
            kernels[0],
            gather,
            spread,
        )

        if step == STEPS - 1:
            latents = call(
                pair_kernel, sds((CORES * lat, half), F32), [SM, VM, VM], [], 100_000
            )(ints, lat_keep, swap(lat_send))
            shares = [latents] + [
                lax.ppermute(
                    latents, "segment", [(q, (q + s) % sections) for q in range(sections)]
                )
                for s in range(1, sections)
            ]

        def conv(index, own, messages, base, last=False):
            up, down, others = exchange(layout, *messages)
            extra = [] if base is None else [base]
            return call(
                functools.partial(conv_kernel, index, base is not None, last),
                (
                    (half_shape,)
                    if last == "final"
                    else (wide_shape if base is None else half_shape, rows_shape, rows_shape, stats_shape)
                ),
                [SM] + [VM] * (7 + len(extra) + len(others)),
                conv_scratch,
                conv_flops,
            )(ints, params, own, up, down, kernels[index], gather, spread, *extra, *others)

        one, *messages = conv(1, middle, messages, source)
        middle, *messages = conv(2, one, messages, None)
        own, *messages = conv(
            3, middle, messages, one, "final" if step == STEPS - 1 else "last"
        )

    own, *shares = lax.optimization_barrier((own, *shares))
    low, high = own[:, :half], own[:, half:]
    mine = jnp.where(first_core, low, high)
    other = swap(jnp.where(first_core, high, low))
    pair = jnp.where(first_core, jnp.stack([mine, other]), jnp.stack([other, mine]))
    features_out = pair.reshape(1, batch, chans, own_rows, cols)
    share = cols // sections
    latent_out = None
    for s, piece in enumerate(shares):
        piece = piece.reshape(batch, lat, own_rows, cols)[..., s * share : (s + 1) * share]
        latent_out = piece if latent_out is None else jnp.where(section == s, piece, latent_out)
    return (latent_out, features_out)


def solution(mesh):
    placed = (
        P("segment", None, None, "patch", None),
        P(None, None, "patch", None),
        P(),
        P("segment"),
        P("segment", None, None, None, None),
        P("segment", None, None, None, None),
        P("segment", None, None, None),
        P("segment", None, None, None),
        P(),
        P(),
        P(),
        P(),
    )
    return jax.shard_map(
        per_device,
        mesh=mesh,
        in_specs=placed,
        out_specs=(P(None, None, "patch", "segment"), P("segment", None, None, "patch", None)),
        check_vma=False,
    )
```

```python
import functools

import jax
import jax.numpy as jnp
import numpy as np
from jax import lax
from jax.experimental import pallas as pl
from jax.experimental.pallas import tpu as pltpu
from jax.sharding import PartitionSpec as P

GROUPS = 32
STEPS = 2
SCHED = 12
CORES = 2

epsilon = 1e-05
sigma_top = 3.0
sigma_low = 0.1
rho_power = 7.0

F32 = jnp.float32
BF16 = jnp.bfloat16
VMEM_LIMIT = 24 * 1024 * 1024


def sigma_at(position):
    fraction = position / (SCHED - 1)
    top_root = sigma_top ** (1.0 / rho_power)
    low_root = sigma_low ** (1.0 / rho_power)
    base = top_root + fraction * (low_root - top_root)
    square = base * base
    return base * square * (square * square)


def dot(a, b):
    return lax.dot_general(a, b, (((1,), (0,)), ((), ())), preferred_element_type=F32)


def split3(x):
    hi = x.astype(BF16)
    rest = x - hi.astype(F32)
    mid = rest.astype(BF16)
    lo = (rest - mid.astype(F32)).astype(BF16)
    return hi, mid, lo


def group_lanes(x, gather):
    return dot(gather, jnp.concatenate(split3(x)[:2], axis=0))


def group_sum(x, gather):
    return jnp.sum(group_lanes(x, gather), axis=1, keepdims=True)


def expand(x, spread):
    return dot(spread, jnp.concatenate(split3(x), axis=0))


def tile_sum(tiles):
    total = tiles[0]
    for tile in tiles[1:]:
        total = total + tile
    return total


def pivot_of(tiles, gather, spread, count):
    mean = group_sum(tile_sum(tiles), gather) / (count * len(tiles))
    return mean, expand(jnp.broadcast_to(mean, (GROUPS, 128)), spread)


def add_deviations(sums, tiles, center):
    first, second = sums
    for tile in tiles:
        dev = tile - center
        first = dev if first is None else first + dev
        second = dev * dev if second is None else second + dev * dev
    return first, second


def finish_stats(pivot, sums, gather, count):
    wide = group_lanes(jnp.concatenate(sums, axis=1), gather)
    first = jnp.sum(wide[:, :128], axis=1, keepdims=True)
    second = jnp.sum(wide[:, 128:], axis=1, keepdims=True)
    return pivot + first / count, jnp.maximum(second - first * first / count, 0.0)


def encode_stats(mean, square):
    lane = lax.broadcasted_iota(jnp.int32, (GROUPS, 128), 1) // 16
    out = jnp.zeros((GROUPS, 128), F32)
    for slot, part in enumerate(split3(mean) + split3(square)):
        out = jnp.where(lane == slot, part.astype(F32), out)
    return out.astype(BF16)


def decode_stats(message):
    wide = message.astype(F32)
    take = [wide[:, 16 * k : 16 * k + 1] for k in range(6)]
    return take[0] + take[1] + take[2], take[3] + take[4] + take[5]


def combine_stats(messages, count):
    pairs = [decode_stats(m) for m in messages]
    mean = sum(p[0] for p in pairs) / len(pairs)
    square = sum(p[1] for p in pairs)
    for p in pairs:
        square = square + count * (p[0] - mean) * (p[0] - mean)
    return mean, lax.rsqrt(square / (count * len(pairs)) + epsilon)


def channel_moments(mean, scale, spread):
    both = jnp.concatenate(
        [jnp.broadcast_to(mean, (GROUPS, 128)), jnp.broadcast_to(scale, (GROUPS, 128))], axis=1
    )
    wide = expand(both, spread)
    return wide[:, :128], wide[:, 128:]


def silu(v):
    half = 0.5 * v
    return half + half * jnp.tanh(half)


def shift_cols(t):
    lane = lax.broadcasted_iota(jnp.int32, t.shape, 1)
    before = jnp.where(lane == 0, 0.0, pltpu.roll(t, 1, 1))
    after = jnp.where(lane == 127, 0.0, pltpu.roll(t, 127, 1))
    return before, after


def fill_row(r, last, tile, moments, flags, patches):
    center, scale, shift = moments
    chans = center.shape[0]
    main = chans // 128 * 128
    tail = chans - main
    t = silu((tile - center) * scale + shift)
    if r == 0:
        t = jnp.where(flags[0] > 0, t, 0.0)
    if r == last:
        t = jnp.where(flags[1] > 0, t, 0.0)
    before, after = shift_cols(t)
    lanes = pl.ds(r * 128, 128)
    for j, piece in enumerate((before, t, after)):
        piece = piece.astype(BF16)
        patches[pl.ds(j * main, main), lanes] = piece[:main]
        patches[pl.ds(3 * main + j * tail, tail), lanes] = piece[main:]


def conv_rows(patches, weight, start, rows):
    depth = weight.shape[1] // 9
    main = depth // 128 * 128
    parts = ((0, 3 * main), (3 * main, 3 * (depth - main)))
    pieces = [
        patches[pl.ds(low, size), pl.ds((start + i) * 128, rows * 128)]
        for low, size in parts
        for i in range(3)
    ]
    return dot(weight[...], jnp.concatenate(pieces, axis=0))


CHUNK = 4


def conv_all(tiles, moments, flags, patches, weight, store, gather=None, spread=None):
    rows = len(tiles) - 2
    chans = weight.shape[0]
    filled = 0
    per_row = count_of(chans, 128)
    sums = (None, None)
    for start in range(0, rows, CHUNK):
        while filled < start + CHUNK + 2:
            fill_row(filled, rows + 1, tiles[filled](), moments, flags, patches)
            filled += 1
        kept = store(start, CHUNK, conv_rows(patches, weight, start, CHUNK))
        if gather is None:
            continue
        kept = [kept[:, r * 128 : (r + 1) * 128] for r in range(CHUNK)]
        if start == 0:
            pivot, center = pivot_of(kept, gather, spread, per_row)
        sums = add_deviations(sums, kept, center)
    if gather is None:
        return None
    return encode_stats(*finish_stats(pivot, sums, gather, per_row * rows))


def write_messages(out, stats, top_msg, bot_msg, st_msg):
    chans, cells = out.shape
    st_msg[...] = stats
    for ref, start in ((top_msg, 0), (bot_msg, cells - 128)):
        ref[pl.ds(0, chans), :] = out[:, pl.ds(start, 128)].astype(BF16)
        ref[pl.ds(chans, GROUPS), :] = stats


def pack_kernel(block, taps_in, out, taps, sem):
    copy = pltpu.make_async_copy(taps_in.at[0, block], taps, sem)
    copy.start()
    copy.wait()
    chans = taps.shape[1]
    main = chans // 128 * 128
    tail = chans - main
    pieces = []
    for t in range(9):
        tap = taps[t]
        out[:, pl.ds(t * main, main)] = tap[:, :main]
        pieces.append(tap[:, main:])
    out[:, pl.ds(9 * main, 9 * tail)] = jnp.concatenate(pieces, axis=1)


def count_of(chans, cells):
    return float(chans // GROUPS * cells)


def row_tile(ref, r):
    return lambda: ref[:, pl.ds(r * 128, 128)].astype(F32)


def enter_kernel(own, gather, spread, top_msg, bot_msg, st_msg):
    chans, cells = own.shape
    tiles = [own[:, pl.ds(start, 128)].astype(F32) for start in range(0, cells, 128)]
    per_row = count_of(chans, 128)
    pivot, center = pivot_of(tiles[:2], gather[...], spread[...], per_row)
    sums = add_deviations((None, None), tiles, center)
    stats = encode_stats(*finish_stats(pivot, sums, gather[...], per_row * len(tiles)))
    write_messages(own, stats, top_msg, bot_msg, st_msg)


def pair_kernel(ints, kept, other, out):
    lat = kept.shape[0]
    first = ints[5] == 0
    out[0:lat, :] = jnp.where(first, kept[...], other[...])
    out[lat:, :] = jnp.where(first, other[...], kept[...])


def column(params, k):
    return params[:, k : k + 1]


def gathered(up, down, others, count):
    chans = up.shape[0] - GROUPS
    messages = [up[pl.ds(chans, GROUPS), :], down[pl.ds(chans, GROUPS), :]]
    return combine_stats(messages + [ref[...] for ref in others], count)


def head_kernel(early, params, own, up, down, weight, spread, *rest):
    others, (out, forward) = rest[: len(rest) - 2 - early], rest[-2:]
    latent = None
    if out.shape[0] == 8:
        others, latent = others[:-1], others[-1]
    chans, cells = own.shape
    rows = cells // 128
    mean, root = gathered(up, down, others, count_of(chans, cells))
    stats = encode_stats(mean, root)
    for ref, low in ((up, 0), (down, 128)):
        forward[pl.ds(0, chans), pl.ds(low, 128)] = ref[pl.ds(0, chans), :]
        forward[pl.ds(chans, GROUPS), pl.ds(low, 128)] = stats
    center, scale = channel_moments(mean, root, spread[...])
    scale = scale * column(params, 8)
    shift = column(params, 9)
    tiles = [row_tile(own, r) for r in range(rows)]
    sums = []
    for tile in tiles:
        act = silu((tile() - center) * scale + shift).astype(BF16)
        y = dot(weight[...], act)
        before, _ = shift_cols(y[0:24])
        _, after = shift_cols(y[48:72])
        sums.append(before + y[24:48] + after)
    for r in range(-1, rows + 1):
        acc = jnp.zeros((8, 128), F32)
        for i in range(3):
            if 0 <= r + i - 1 < rows:
                acc = acc + sums[r + i - 1][8 * i : 8 * i + 8]
        if latent is not None and 0 <= r < rows:
            acc = acc + latent[:, pl.ds(r * 128, 128)]
        out[:, pl.ds((r + 1) * 128, 128)] = acc[: out.shape[0]]
        coded = [part.astype(F32) for part in split3(acc)] + [jnp.zeros((8, 128), F32)]
        begin = chans + GROUPS + (r + 1) // 2 * 32
        forward[pl.ds(begin, 32), pl.ds((r + 1) % 2 * 128, 128)] = jnp.concatenate(
            coded, axis=0
        ).astype(BF16)


def first_kernel(step, chips, ints, plan, params, *rest):
    first_step = step == 0
    parts, rest = rest[: chips - 1], rest[chips - 1 :]
    if not first_step:
        latent_in, rest = rest[0], rest[1:]
    in_weight, own, forward, weight, gather, spread = rest[:6]
    out, source, latent_out, lat_keep, lat_send, top_msg, bot_msg, st_msg = rest[6:14]
    patches, wide, moments, noise, field, entry = rest[14:]
    chans, cells = own.shape
    rows = cells // 128
    full = chips * rows
    flags = (ints[0], ints[1])
    section, place = ints[2], ints[3]

    @pl.when(section == 0)
    def _():
        noise[...] = jnp.zeros_like(noise)
        for d in range(chips):
            owner = lax.rem(place - d + chips, chips)
            lanes = pl.ds(pl.multiple_of(owner * cells, 128), cells + 256)
            if d > 0:
                height = parts[d - 1].shape[0]
                noise[:height, lanes] = noise[:height, lanes] + parts[d - 1][...]
                continue
            for r in range(rows + 2):
                begin = chans + GROUPS + r // 2 * 32
                coded = forward[pl.ds(begin, 32), pl.ds(r % 2 * 128, 128)].astype(F32)
                spot = pl.ds(pl.multiple_of(owner * cells + r * 128, 128), 128)
                noise[:, spot] = noise[:, spot] + coded[0:8] + coded[8:16] + coded[16:24]
        position = jnp.broadcast_to(plan[ints[6]] + step, (8, 128)).astype(F32)
        later = sigma_at(position + 1.0)
        change = later - sigma_at(position)
        shrink = lax.rsqrt(later * later + 1.0)
        field[...] = jnp.zeros_like(field)
        for r in range(full):
            piece = noise[:, pl.ds((r + 1) * 128, 128)]
            if first_step:
                old = pltpu.roll(piece, 4, 0)
            else:
                old = latent_in[:, pl.ds(r * 128, 128)]
            new = old + change * piece
            latent_out[:, pl.ds(r * 128, 128)] = new
            scaled = (new * shrink).astype(BF16).astype(F32)
            before, after = shift_cols(scaled)
            lanes = pl.ds((r + 1) * 128, 128)
            field[pl.ds(0, 8), lanes] = before
            field[pl.ds(8, 8), lanes] = scaled
            field[pl.ds(16, 8), lanes] = after
        half = cells // CORES
        for ref, which in ((lat_keep, ints[5]), (lat_send, 1 - ints[5])):
            begin = pl.multiple_of(place * cells + which * half, 128)
            ref[...] = latent_out[: ref.shape[0], pl.ds(begin, half)]
        sums = (None, None)
        per_row = count_of(chans, 128)
        for z in range(chips):
            taps = [field[:, pl.ds((z * rows + i) * 128, cells)] for i in range(3)]
            rows_out = dot(in_weight[...], jnp.concatenate(taps, axis=0).astype(BF16)).astype(BF16)
            entry[:, pl.ds(z * cells + 128, cells)] = rows_out
            kept = [rows_out[:, r * 128 : (r + 1) * 128].astype(F32) for r in range(rows)]
            if z == 0:
                pivot, center = pivot_of(kept, gather[...], spread[...], per_row)
            sums = add_deviations(sums, kept, center)
        entry[:, pl.ds(0, 128)] = jnp.zeros((chans, 128), BF16)
        entry[:, pl.ds(full * 128 + 128, 128)] = jnp.zeros((chans, 128), BF16)
        count = per_row * full
        mean, square = finish_stats(pivot, sums, gather[...], count)
        scale = lax.rsqrt(square / count + epsilon)
        moments[:, 0:128], moments[:, 128:256] = channel_moments(mean, scale, spread[...])
        wide[...] = entry[:, pl.ds(pl.multiple_of(place * cells, 128), cells + 256)]

    @pl.when(section != 0)
    def _():
        latent_out[...] = jnp.zeros_like(latent_out)
        lat_keep[...] = jnp.zeros_like(lat_keep)
        lat_send[...] = jnp.zeros_like(lat_send)
        mean, scale = decode_stats(forward[pl.ds(chans, GROUPS), pl.ds(0, 128)])
        moments[:, 0:128], moments[:, 128:256] = channel_moments(mean, scale, spread[...])
        wide[:, pl.ds(0, 128)] = forward[pl.ds(0, chans), pl.ds(0, 128)]
        wide[:, pl.ds(128, cells)] = own[...]
        wide[:, pl.ds(cells + 128, 128)] = forward[pl.ds(0, chans), pl.ds(128, 128)]

    source[...] = wide[:, pl.ds(128, cells)]
    tiles = [row_tile(wide, r) for r in range(rows + 2)]
    known = (moments[:, 0:128], moments[:, 128:256] * column(params, 0), column(params, 1))

    def store(start, count, acc):
        out[:, pl.ds(start * 128, count * 128)] = acc
        return acc

    stats_out = conv_all(tiles, known, flags, patches, weight, store, gather[...], spread[...])
    write_messages(out, stats_out, top_msg, bot_msg, st_msg)


def conv_kernel(index, residual, last, ints, params, own, up, down, weight, gather, spread, *rest):
    rest = list(rest)
    base = rest.pop(0) if residual else None
    patches = rest.pop()
    final = last == "final"
    given = 1 if final else 4
    others, outs = rest[:-given], rest[-given:]
    out = outs[0]
    chans, cells = own.shape
    rows = cells // 128
    mean, root = gathered(up, down, others, count_of(chans, cells))
    center, scale = channel_moments(mean, root, spread[...])
    tiles = [lambda: up[pl.ds(0, chans), :].astype(F32)]
    tiles += [row_tile(own, r) for r in range(rows)]
    tiles += [lambda: down[pl.ds(0, chans), :].astype(F32)]
    known = (center, scale * column(params, 2 * index), column(params, 2 * index + 1))

    def store(start, count, acc):
        lanes = pl.ds(start * 128, count * 128)
        if residual:
            old = base[:, lanes].astype(F32)
            acc = (old + acc).astype(BF16).astype(F32)
        if last:
            acc = jnp.where(ints[4] >= 2, acc, old)
        out[:, lanes] = acc.astype(out.dtype)
        return acc

    sums = () if final else (gather[...], spread[...])
    stats_out = conv_all(tiles, known, (ints[0], ints[1]), patches, weight, store, *sums)
    if not final:
        write_messages(out, stats_out, *outs[1:])


VM = pl.BlockSpec(memory_space=pltpu.VMEM)
SM = pl.BlockSpec(memory_space=pltpu.SMEM)
HB = pl.BlockSpec(memory_space=pl.ANY)


def call(kernel, outs, in_specs, scratch, flops):
    return pl.pallas_call(
        kernel,
        out_shape=outs,
        in_specs=in_specs,
        out_specs=jax.tree.map(lambda _: VM, outs),
        scratch_shapes=scratch,
        compiler_params=pltpu.CompilerParams(vmem_limit_bytes=VMEM_LIMIT),
        cost_estimate=pl.CostEstimate(flops=flops, bytes_accessed=4_000_000, transcendentals=0),
    )


def sds(shape, dtype):
    return jax.ShapeDtypeStruct(shape, dtype)


def per_device(
    features,
    latent,
    plan_pos,
    blocks_used,
    conv1_w,
    conv2_w,
    norm_gain,
    norm_shift,
    in_w,
    head_w,
    head_gain,
    head_shift,
):
    sections = lax.axis_size("segment")
    patches = lax.axis_size("patch")
    chips = patches // CORES
    section = lax.axis_index("segment")
    core = lax.rem(lax.axis_index("patch"), CORES)
    place = lax.axis_index("patch") // CORES
    _, batch, chans, own_rows, cols = features.shape
    rows = CORES * own_rows
    half = own_rows * cols
    cells = rows * cols
    joint = ("segment", "patch")

    swap_pairs = [(p, p ^ 1) for p in range(patches)]

    def swap(x):
        return lax.ppermute(x, "patch", swap_pairs)

    def by_core(m, l):
        return CORES * (l % chips) + m

    def by_chips(m, l):
        return m * chips + ((l % chips) ^ ((l % chips) >> 1))

    blocks = [(m, l) for m in range(CORES) for l in range(chips)]

    def around(layout, x, by):
        return lax.ppermute(x, "patch", [(layout(m, l), layout(m, l + by)) for m, l in blocks])

    def onward(source, target, x):
        pairs = [
            (s * patches + source(m, l), (s + 1) % sections * patches + target(m, l))
            for s in range(sections)
            for m, l in blocks
        ]
        return lax.ppermute(x, joint, pairs)

    def to_first(source, target, x, by):
        pairs = [
            (s * patches + source(m, l), (s + 1) % sections * patches + target(m, l + by))
            for s in range(sections)
            for m, l in blocks
        ]
        return lax.ppermute(x, joint, pairs)

    group_of = np.arange(chans) // (chans // GROUPS)
    member = (np.arange(GROUPS)[:, None] == group_of[None, :]).astype(np.float32)
    gather = jnp.asarray(np.tile(member, (1, 2)), BF16)
    spread = jnp.asarray(np.tile(member.T, (1, 3)), BF16)

    lat = latent.shape[1]
    group, rank = lax.axis_index("patch") // chips, lax.rem(lax.axis_index("patch"), chips)
    turn = 1
    while turn < chips:
        rank = rank ^ (rank >> turn)
        turn *= 2

    def describe(row_block, which):
        return jnp.stack(
            [
                (row_block > 0).astype(jnp.int32),
                (row_block < chips - 1).astype(jnp.int32),
                section.astype(jnp.int32),
                row_block.astype(jnp.int32),
                blocks_used[0],
                core.astype(jnp.int32),
                which.astype(jnp.int32),
            ]
        )

    def pick(x, which):
        return lax.dynamic_index_in_dim(x, which, 0, keepdims=False)

    stats_shape = sds((GROUPS, 128), BF16)
    rows_shape = sds((chans + GROUPS, 128), BF16)
    wide_shape = sds((chans, cells), F32)
    half_shape = sds((chans, cells), BF16)
    conv_flops = 2 * 9 * chans * chans * cells
    conv_scratch = [pltpu.VMEM((3 * chans, cells + 256), BF16)]

    first_core = core == 0
    mine = pick(features[0], core)
    other = swap(pick(features[0], 1 - core))
    own = jnp.concatenate(
        [jnp.where(first_core, mine, other), jnp.where(first_core, other, mine)], axis=1
    ).reshape(chans, cells)
    messages = call(
        enter_kernel, (rows_shape, rows_shape, stats_shape), [VM] * 3, [], 10_000_000
    )(own, gather, spread)

    given = (conv1_w, conv2_w, norm_gain, norm_shift, in_w, head_w, head_gain, head_shift)
    *given, latent, plan_pos, _ = lax.optimization_barrier((*given, latent, plan_pos, messages[2]))
    conv1_w, conv2_w, norm_gain, norm_shift, in_w, head_w, head_gain, head_shift = given
    params = jnp.stack(
        [x[0, k, q] for k in range(2) for q in range(2) for x in (norm_gain, norm_shift)]
        + [head_gain, head_shift]
        + [jnp.zeros((chans,), F32)] * 6
    ).T
    kernels = [
        call(
            functools.partial(pack_kernel, block),
            sds((chans, 9 * chans), BF16),
            [HB],
            [pltpu.VMEM(taps.shape[2:], BF16), pltpu.SemaphoreType.DMA(())],
            10_000_000,
        )(taps)
        for block in range(2)
        for taps in (conv1_w, conv2_w)
    ]
    head_packed = jnp.zeros((3, 3, 8, chans), BF16)
    head_packed = head_packed.at[:, :, :lat].set(
        jnp.transpose(head_w.reshape(3, 3, lat, chans), (1, 0, 2, 3))
    ).reshape(72, chans)
    in_packed = jnp.zeros((chans, 3, 3, 8), BF16)
    in_packed = in_packed.at[:, :, :, :lat].set(
        jnp.transpose(in_w.reshape(3, 3, chans, lat), (2, 0, 1, 3))
    ).reshape(chans, 72)
    mine = pick(latent, core)
    other = swap(pick(latent, 1 - core))
    latent_rows = jnp.concatenate(
        [jnp.where(core == 0, mine, other), jnp.where(core == 0, other, mine)], axis=1
    ).reshape(lat, cells)
    latent_rows = jnp.concatenate([jnp.zeros((8 - lat, cells), F32), latent_rows], axis=0)
    layouts = (by_core,) * (STEPS + 1)
    described = {by_core: describe(place, core), by_chips: describe(rank, group)}
    full_latent = None

    def exchange(layout, top_msg, bot_msg, st_msg):
        up = around(layout, bot_msg, 1)
        down = around(layout, top_msg, chips - 1)
        return up, down, [st_msg] + [around(layout, st_msg, d) for d in range(2, chips - 1)]

    for step in range(STEPS):
        first_step = step == 0
        before, layout = layouts[step], layouts[step + 1]
        ints = described[layout]
        own_next = onward(before, layout, own)
        up, down, others = exchange(before, *messages)
        height = 8 if first_step else lat
        extra = [latent_rows] if first_step else []
        early = []
        noise, forward = call(
            functools.partial(head_kernel, len(early)),
            (sds((height, cells + 256), F32), sds((chans + GROUPS + (rows + 2) // 2 * 32, 256), BF16)),
            [VM] * (6 + len(others) + len(extra)) + [HB] * len(early),
            [],
            300_000_000,
        )(params, own, up, down, head_packed, spread, *others, *extra, *early)
        parts = [to_first(before, layout, noise, d) for d in range(1, chips)]
        forward_next = onward(before, layout, forward)
        extra = []
        if not first_step:
            extra = [full_latent]
            if before is not layout:
                moves = [(before(m, l), layout(m, l)) for m, l in blocks]
                extra = [lax.ppermute(full_latent, "patch", moves)]
        middle, source, full_latent, lat_keep, lat_send, *messages = call(
            functools.partial(first_kernel, step, chips),
            (
                wide_shape,
                half_shape,
                sds((8, chips * cells), F32),
                sds((lat, half), F32),
                sds((lat, half), F32),
                rows_shape,
                rows_shape,
                stats_shape,
            ),
            [SM, SM] + [VM] * (6 + chips + len(extra)),
            conv_scratch
            + [
                pltpu.VMEM((chans, cells + 256), BF16),
                pltpu.VMEM((chans, 256), F32),
                pltpu.VMEM((8, chips * cells + 256), F32),
                pltpu.VMEM((24, chips * cells + 256), F32),
                pltpu.VMEM((chans, chips * cells + 256), BF16),
            ],
            conv_flops,
        )(
            ints,
            plan_pos,
            params,
            *parts,
            *extra,
            in_packed,
            own_next,
            forward_next,
            kernels[0],
            gather,
            spread,
        )

        if step == STEPS - 1:
            latents = call(
                pair_kernel, sds((CORES * lat, half), F32), [SM, VM, VM], [], 100_000
            )(ints, lat_keep, swap(lat_send))
            shares = [latents] + [
                lax.ppermute(
                    latents, "segment", [(q, (q + s) % sections) for q in range(sections)]
                )
                for s in range(1, sections)
            ]

        def conv(index, own, messages, base, last=False):
            up, down, others = exchange(layout, *messages)
            extra = [] if base is None else [base]
            return call(
                functools.partial(conv_kernel, index, base is not None, last),
                (
                    (half_shape,)
                    if last == "final"
                    else (wide_shape if base is None else half_shape, rows_shape, rows_shape, stats_shape)
                ),
                [SM] + [VM] * (7 + len(extra) + len(others)),
                conv_scratch,
                conv_flops,
            )(ints, params, own, up, down, kernels[index], gather, spread, *extra, *others)

        one, *messages = conv(1, middle, messages, source)
        middle, *messages = conv(2, one, messages, None)
        own, *messages = conv(
            3, middle, messages, one, "final" if step == STEPS - 1 else "last"
        )

    own, *shares = lax.optimization_barrier((own, *shares))
    low, high = own[:, :half], own[:, half:]
    mine = jnp.where(first_core, low, high)
    other = swap(jnp.where(first_core, high, low))
    pair = jnp.where(first_core, jnp.stack([mine, other]), jnp.stack([other, mine]))
    features_out = pair.reshape(1, batch, chans, own_rows, cols)
    share = cols // sections
    latent_out = None
    for s, piece in enumerate(shares):
        piece = piece.reshape(batch, lat, own_rows, cols)[..., s * share : (s + 1) * share]
        latent_out = piece if latent_out is None else jnp.where(section == s, piece, latent_out)
    return (latent_out, features_out)


def solution(mesh):
    placed = (
        P("segment", None, None, "patch", None),
        P(None, None, "patch", None),
        P(),
        P("segment"),
        P("segment", None, None, None, None),
        P("segment", None, None, None, None),
        P("segment", None, None, None),
        P("segment", None, None, None),
        P(),
        P(),
        P(),
        P(),
    )
    return jax.shard_map(
        per_device,
        mesh=mesh,
        in_specs=placed,
        out_specs=(P(None, None, "patch", "segment"), P("segment", None, None, "patch", None)),
        check_vma=False,
    )
```

```python
import functools

import jax
import jax.numpy as jnp
import numpy as np
from jax import lax
from jax.experimental import pallas as pl
from jax.experimental.pallas import tpu as pltpu
from jax.sharding import PartitionSpec as P

GROUPS = 32
STEPS = 2
SCHED = 12
CORES = 2

epsilon = 1e-05
sigma_top = 3.0
sigma_low = 0.1
rho_power = 7.0

F32 = jnp.float32
BF16 = jnp.bfloat16
VMEM_LIMIT = 24 * 1024 * 1024


def sigma_at(position):
    fraction = position / (SCHED - 1)
    top_root = sigma_top ** (1.0 / rho_power)
    low_root = sigma_low ** (1.0 / rho_power)
    base = top_root + fraction * (low_root - top_root)
    square = base * base
    return base * square * (square * square)


def dot(a, b):
    return lax.dot_general(a, b, (((1,), (0,)), ((), ())), preferred_element_type=F32)


def split3(x):
    hi = x.astype(BF16)
    rest = x - hi.astype(F32)
    mid = rest.astype(BF16)
    lo = (rest - mid.astype(F32)).astype(BF16)
    return hi, mid, lo


def group_lanes(x, gather):
    return dot(gather, jnp.concatenate(split3(x)[:2], axis=0))


def group_sum(x, gather):
    return jnp.sum(group_lanes(x, gather), axis=1, keepdims=True)


def expand(x, spread):
    return dot(spread, jnp.concatenate(split3(x), axis=0))


def tile_sum(tiles):
    total = tiles[0]
    for tile in tiles[1:]:
        total = total + tile
    return total


def pivot_of(tiles, gather, spread, count):
    mean = group_sum(tile_sum(tiles), gather) / (count * len(tiles))
    return mean, expand(jnp.broadcast_to(mean, (GROUPS, 128)), spread)


def add_deviations(sums, tiles, center):
    first, second = sums
    for tile in tiles:
        dev = tile - center
        first = dev if first is None else first + dev
        second = dev * dev if second is None else second + dev * dev
    return first, second


def finish_stats(pivot, sums, gather, count):
    wide = group_lanes(jnp.concatenate(sums, axis=1), gather)
    first = jnp.sum(wide[:, :128], axis=1, keepdims=True)
    second = jnp.sum(wide[:, 128:], axis=1, keepdims=True)
    return pivot + first / count, jnp.maximum(second - first * first / count, 0.0)


def encode_stats(mean, square):
    lane = lax.broadcasted_iota(jnp.int32, (GROUPS, 128), 1) // 16
    out = jnp.zeros((GROUPS, 128), F32)
    for slot, part in enumerate(split3(mean) + split3(square)):
        out = jnp.where(lane == slot, part.astype(F32), out)
    return out.astype(BF16)


def decode_stats(message):
    wide = message.astype(F32)
    take = [wide[:, 16 * k : 16 * k + 1] for k in range(6)]
    return take[0] + take[1] + take[2], take[3] + take[4] + take[5]


def combine_stats(messages, count):
    pairs = [decode_stats(m) for m in messages]
    mean = sum(p[0] for p in pairs) / len(pairs)
    square = sum(p[1] for p in pairs)
    for p in pairs:
        square = square + count * (p[0] - mean) * (p[0] - mean)
    return mean, lax.rsqrt(square / (count * len(pairs)) + epsilon)


def channel_moments(mean, scale, spread):
    both = jnp.concatenate(
        [jnp.broadcast_to(mean, (GROUPS, 128)), jnp.broadcast_to(scale, (GROUPS, 128))], axis=1
    )
    wide = expand(both, spread)
    return wide[:, :128], wide[:, 128:]


def silu(v):
    half = 0.5 * v
    return half + half * jnp.tanh(half)


def shift_cols(t):
    lane = lax.broadcasted_iota(jnp.int32, t.shape, 1)
    before = jnp.where(lane == 0, 0.0, pltpu.roll(t, 1, 1))
    after = jnp.where(lane == 127, 0.0, pltpu.roll(t, 127, 1))
    return before, after


def fill_row(r, last, tile, moments, flags, patches):
    center, scale, shift = moments
    chans = center.shape[0]
    main = chans // 128 * 128
    tail = chans - main
    t = silu((tile - center) * scale + shift)
    if r == 0:
        t = jnp.where(flags[0] > 0, t, 0.0)
    if r == last:
        t = jnp.where(flags[1] > 0, t, 0.0)
    before, after = shift_cols(t)
    lanes = pl.ds(r * 128, 128)
    for j, piece in enumerate((before, t, after)):
        piece = piece.astype(BF16)
        patches[pl.ds(j * main, main), lanes] = piece[:main]
        patches[pl.ds(3 * main + j * tail, tail), lanes] = piece[main:]


def conv_rows(patches, weight, start, rows):
    depth = weight.shape[1] // 9
    main = depth // 128 * 128
    parts = ((0, 3 * main), (3 * main, 3 * (depth - main)))
    pieces = [
        patches[pl.ds(low, size), pl.ds((start + i) * 128, rows * 128)]
        for low, size in parts
        for i in range(3)
    ]
    return dot(weight[...], jnp.concatenate(pieces, axis=0))


CHUNK = 4


def conv_all(tiles, moments, flags, patches, weight, store, gather=None, spread=None):
    rows = len(tiles) - 2
    chans = weight.shape[0]
    filled = 0
    per_row = count_of(chans, 128)
    sums = (None, None)
    for start in range(0, rows, CHUNK):
        while filled < start + CHUNK + 2:
            fill_row(filled, rows + 1, tiles[filled](), moments, flags, patches)
            filled += 1
        kept = store(start, CHUNK, conv_rows(patches, weight, start, CHUNK))
        if gather is None:
            continue
        kept = [kept[:, r * 128 : (r + 1) * 128] for r in range(CHUNK)]
        if start == 0:
            pivot, center = pivot_of(kept, gather, spread, per_row)
        sums = add_deviations(sums, kept, center)
    if gather is None:
        return None
    return encode_stats(*finish_stats(pivot, sums, gather, per_row * rows))


def write_messages(out, stats, top_msg, bot_msg, st_msg):
    chans, cells = out.shape
    st_msg[...] = stats
    for ref, start in ((top_msg, 0), (bot_msg, cells - 128)):
        ref[pl.ds(0, chans), :] = out[:, pl.ds(start, 128)].astype(BF16)
        ref[pl.ds(chans, GROUPS), :] = stats


def pack_kernel(block, taps_in, out, taps, sem):
    copy = pltpu.make_async_copy(taps_in.at[0, block], taps, sem)
    copy.start()
    copy.wait()
    chans = taps.shape[1]
    main = chans // 128 * 128
    tail = chans - main
    pieces = []
    for t in range(9):
        tap = taps[t]
        out[:, pl.ds(t * main, main)] = tap[:, :main]
        pieces.append(tap[:, main:])
    out[:, pl.ds(9 * main, 9 * tail)] = jnp.concatenate(pieces, axis=1)


def count_of(chans, cells):
    return float(chans // GROUPS * cells)


def row_tile(ref, r):
    return lambda: ref[:, pl.ds(r * 128, 128)].astype(F32)


def enter_kernel(own, gather, spread, top_msg, bot_msg, st_msg):
    chans, cells = own.shape
    tiles = [own[:, pl.ds(start, 128)].astype(F32) for start in range(0, cells, 128)]
    per_row = count_of(chans, 128)
    pivot, center = pivot_of(tiles[:2], gather[...], spread[...], per_row)
    sums = add_deviations((None, None), tiles, center)
    stats = encode_stats(*finish_stats(pivot, sums, gather[...], per_row * len(tiles)))
    write_messages(own, stats, top_msg, bot_msg, st_msg)


def pair_kernel(ints, kept, other, out):
    lat = kept.shape[0]
    first = ints[5] == 0
    out[0:lat, :] = jnp.where(first, kept[...], other[...])
    out[lat:, :] = jnp.where(first, other[...], kept[...])


def column(params, k):
    return params[:, k : k + 1]


def gathered(up, down, others, count):
    chans = up.shape[0] - GROUPS
    messages = [up[pl.ds(chans, GROUPS), :], down[pl.ds(chans, GROUPS), :]]
    return combine_stats(messages + [ref[...] for ref in others], count)


def head_kernel(early, params, own, up, down, weight, spread, *rest):
    others, (out, forward) = rest[: len(rest) - 2 - early], rest[-2:]
    latent = None
    if out.shape[0] == 8:
        others, latent = others[:-1], others[-1]
    chans, cells = own.shape
    rows = cells // 128
    mean, root = gathered(up, down, others, count_of(chans, cells))
    stats = encode_stats(mean, root)
    for ref, low in ((up, 0), (down, 128)):
        forward[pl.ds(0, chans), pl.ds(low, 128)] = ref[pl.ds(0, chans), :]
        forward[pl.ds(chans, GROUPS), pl.ds(low, 128)] = stats
    center, scale = channel_moments(mean, root, spread[...])
    scale = scale * column(params, 8)
    shift = column(params, 9)
    tiles = [row_tile(own, r) for r in range(rows)]
    sums = []
    for tile in tiles:
        act = silu((tile() - center) * scale + shift).astype(BF16)
        y = dot(weight[...], act)
        before, _ = shift_cols(y[0:24])
        _, after = shift_cols(y[48:72])
        sums.append(before + y[24:48] + after)
    for r in range(-1, rows + 1):
        acc = jnp.zeros((8, 128), F32)
        for i in range(3):
            if 0 <= r + i - 1 < rows:
                acc = acc + sums[r + i - 1][8 * i : 8 * i + 8]
        if latent is not None and 0 <= r < rows:
            acc = acc + latent[:, pl.ds(r * 128, 128)]
        out[:, pl.ds((r + 1) * 128, 128)] = acc[: out.shape[0]]
        coded = [part.astype(F32) for part in split3(acc)] + [jnp.zeros((8, 128), F32)]
        begin = chans + GROUPS + (r + 1) // 2 * 32
        forward[pl.ds(begin, 32), pl.ds((r + 1) % 2 * 128, 128)] = jnp.concatenate(
            coded, axis=0
        ).astype(BF16)


def first_kernel(step, chips, ints, plan, params, *rest):
    first_step = step == 0
    parts, rest = rest[: chips - 1], rest[chips - 1 :]
    if not first_step:
        latent_in, rest = rest[0], rest[1:]
    in_weight, own, forward, weight, gather, spread = rest[:6]
    out, source, latent_out, lat_keep, lat_send, top_msg, bot_msg, st_msg = rest[6:14]
    patches, wide, moments, noise, field, entry = rest[14:]
    chans, cells = own.shape
    rows = cells // 128
    full = chips * rows
    flags = (ints[0], ints[1])
    section, place = ints[2], ints[3]

    @pl.when(section == 0)
    def _():
        noise[...] = jnp.zeros_like(noise)
        for d in range(chips):
            owner = lax.rem(place - d + chips, chips)
            lanes = pl.ds(pl.multiple_of(owner * cells, 128), cells + 256)
            if d > 0:
                height = parts[d - 1].shape[0]
                noise[:height, lanes] = noise[:height, lanes] + parts[d - 1][...]
                continue
            for r in range(rows + 2):
                begin = chans + GROUPS + r // 2 * 32
                coded = forward[pl.ds(begin, 32), pl.ds(r % 2 * 128, 128)].astype(F32)
                spot = pl.ds(pl.multiple_of(owner * cells + r * 128, 128), 128)
                noise[:, spot] = noise[:, spot] + coded[0:8] + coded[8:16] + coded[16:24]
        position = jnp.broadcast_to(plan[ints[6]] + step, (8, 128)).astype(F32)
        later = sigma_at(position + 1.0)
        change = later - sigma_at(position)
        shrink = lax.rsqrt(later * later + 1.0)
        for edge in (0, (full + 1) * 128):
            field[:, pl.ds(edge, 128)] = jnp.zeros((24, 128), F32)
        for r in range(full):
            piece = noise[:, pl.ds((r + 1) * 128, 128)]
            if first_step:
                old = pltpu.roll(piece, 4, 0)
            else:
                old = latent_in[:, pl.ds(r * 128, 128)]
            new = old + change * piece
            latent_out[:, pl.ds(r * 128, 128)] = new
            scaled = (new * shrink).astype(BF16).astype(F32)
            before, after = shift_cols(scaled)
            lanes = pl.ds((r + 1) * 128, 128)
            field[pl.ds(0, 8), lanes] = before
            field[pl.ds(8, 8), lanes] = scaled
            field[pl.ds(16, 8), lanes] = after
        half = cells // CORES
        for ref, which in ((lat_keep, ints[5]), (lat_send, 1 - ints[5])):
            begin = pl.multiple_of(place * cells + which * half, 128)
            ref[...] = latent_out[: ref.shape[0], pl.ds(begin, half)]
        sums = (None, None)
        per_row = count_of(chans, 128)
        for z in range(chips):
            taps = [field[:, pl.ds((z * rows + i) * 128, cells)] for i in range(3)]
            rows_out = dot(in_weight[...], jnp.concatenate(taps, axis=0).astype(BF16)).astype(BF16)
            entry[:, pl.ds(z * cells + 128, cells)] = rows_out
            kept = [rows_out[:, r * 128 : (r + 1) * 128].astype(F32) for r in range(rows)]
            if z == 0:
                pivot, center = pivot_of(kept[:2], gather[...], spread[...], per_row)
            sums = add_deviations(sums, kept, center)
        entry[:, pl.ds(0, 128)] = jnp.zeros((chans, 128), BF16)
        entry[:, pl.ds(full * 128 + 128, 128)] = jnp.zeros((chans, 128), BF16)
        count = per_row * full
        mean, square = finish_stats(pivot, sums, gather[...], count)
        scale = lax.rsqrt(square / count + epsilon)
        moments[:, 0:128], moments[:, 128:256] = channel_moments(mean, scale, spread[...])
        wide[...] = entry[:, pl.ds(pl.multiple_of(place * cells, 128), cells + 256)]

    @pl.when(section != 0)
    def _():
        latent_out[...] = jnp.zeros_like(latent_out)
        lat_keep[...] = jnp.zeros_like(lat_keep)
        lat_send[...] = jnp.zeros_like(lat_send)
        mean, scale = decode_stats(forward[pl.ds(chans, GROUPS), pl.ds(0, 128)])
        moments[:, 0:128], moments[:, 128:256] = channel_moments(mean, scale, spread[...])
        wide[:, pl.ds(0, 128)] = forward[pl.ds(0, chans), pl.ds(0, 128)]
        wide[:, pl.ds(128, cells)] = own[...]
        wide[:, pl.ds(cells + 128, 128)] = forward[pl.ds(0, chans), pl.ds(128, 128)]

    source[...] = wide[:, pl.ds(128, cells)]
    tiles = [row_tile(wide, r) for r in range(rows + 2)]
    known = (moments[:, 0:128], moments[:, 128:256] * column(params, 0), column(params, 1))

    def store(start, count, acc):
        out[:, pl.ds(start * 128, count * 128)] = acc
        return acc

    stats_out = conv_all(tiles, known, flags, patches, weight, store, gather[...], spread[...])
    write_messages(out, stats_out, top_msg, bot_msg, st_msg)


def conv_kernel(index, residual, last, ints, params, own, up, down, weight, gather, spread, *rest):
    rest = list(rest)
    base = rest.pop(0) if residual else None
    patches = rest.pop()
    final = last == "final"
    given = 1 if final else 4
    others, outs = rest[:-given], rest[-given:]
    out = outs[0]
    chans, cells = own.shape
    rows = cells // 128
    mean, root = gathered(up, down, others, count_of(chans, cells))
    center, scale = channel_moments(mean, root, spread[...])
    tiles = [lambda: up[pl.ds(0, chans), :].astype(F32)]
    tiles += [row_tile(own, r) for r in range(rows)]
    tiles += [lambda: down[pl.ds(0, chans), :].astype(F32)]
    known = (center, scale * column(params, 2 * index), column(params, 2 * index + 1))

    def store(start, count, acc):
        lanes = pl.ds(start * 128, count * 128)
        if residual:
            old = base[:, lanes].astype(F32)
            acc = (old + acc).astype(BF16).astype(F32)
        if last:
            acc = jnp.where(ints[4] >= 2, acc, old)
        out[:, lanes] = acc.astype(out.dtype)
        return acc

    sums = () if final else (gather[...], spread[...])
    stats_out = conv_all(tiles, known, (ints[0], ints[1]), patches, weight, store, *sums)
    if not final:
        write_messages(out, stats_out, *outs[1:])


VM = pl.BlockSpec(memory_space=pltpu.VMEM)
SM = pl.BlockSpec(memory_space=pltpu.SMEM)
HB = pl.BlockSpec(memory_space=pl.ANY)


def call(kernel, outs, in_specs, scratch, flops):
    return pl.pallas_call(
        kernel,
        out_shape=outs,
        in_specs=in_specs,
        out_specs=jax.tree.map(lambda _: VM, outs),
        scratch_shapes=scratch,
        compiler_params=pltpu.CompilerParams(vmem_limit_bytes=VMEM_LIMIT),
        cost_estimate=pl.CostEstimate(flops=flops, bytes_accessed=4_000_000, transcendentals=0),
    )


def sds(shape, dtype):
    return jax.ShapeDtypeStruct(shape, dtype)


def per_device(
    features,
    latent,
    plan_pos,
    blocks_used,
    conv1_w,
    conv2_w,
    norm_gain,
    norm_shift,
    in_w,
    head_w,
    head_gain,
    head_shift,
):
    sections = lax.axis_size("segment")
    patches = lax.axis_size("patch")
    chips = patches // CORES
    section = lax.axis_index("segment")
    core = lax.rem(lax.axis_index("patch"), CORES)
    place = lax.axis_index("patch") // CORES
    _, batch, chans, own_rows, cols = features.shape
    rows = CORES * own_rows
    half = own_rows * cols
    cells = rows * cols
    joint = ("segment", "patch")

    swap_pairs = [(p, p ^ 1) for p in range(patches)]

    def swap(x):
        return lax.ppermute(x, "patch", swap_pairs)

    def by_core(m, l):
        return CORES * (l % chips) + m

    def by_chips(m, l):
        return m * chips + ((l % chips) ^ ((l % chips) >> 1))

    blocks = [(m, l) for m in range(CORES) for l in range(chips)]

    def around(layout, x, by):
        return lax.ppermute(x, "patch", [(layout(m, l), layout(m, l + by)) for m, l in blocks])

    def onward(source, target, x):
        pairs = [
            (s * patches + source(m, l), (s + 1) % sections * patches + target(m, l))
            for s in range(sections)
            for m, l in blocks
        ]
        return lax.ppermute(x, joint, pairs)

    def to_first(source, target, x, by):
        pairs = [
            (s * patches + source(m, l), (s + 1) % sections * patches + target(m, l + by))
            for s in range(sections)
            for m, l in blocks
        ]
        return lax.ppermute(x, joint, pairs)

    group_of = np.arange(chans) // (chans // GROUPS)
    member = (np.arange(GROUPS)[:, None] == group_of[None, :]).astype(np.float32)
    gather = jnp.asarray(np.tile(member, (1, 2)), BF16)
    spread = jnp.asarray(np.tile(member.T, (1, 3)), BF16)

    lat = latent.shape[1]
    group, rank = lax.axis_index("patch") // chips, lax.rem(lax.axis_index("patch"), chips)
    turn = 1
    while turn < chips:
        rank = rank ^ (rank >> turn)
        turn *= 2

    def describe(row_block, which):
        return jnp.stack(
            [
                (row_block > 0).astype(jnp.int32),
                (row_block < chips - 1).astype(jnp.int32),
                section.astype(jnp.int32),
                row_block.astype(jnp.int32),
                blocks_used[0],
                core.astype(jnp.int32),
                which.astype(jnp.int32),
            ]
        )

    def pick(x, which):
        return lax.dynamic_index_in_dim(x, which, 0, keepdims=False)

    stats_shape = sds((GROUPS, 128), BF16)
    rows_shape = sds((chans + GROUPS, 128), BF16)
    wide_shape = sds((chans, cells), F32)
    half_shape = sds((chans, cells), BF16)
    conv_flops = 2 * 9 * chans * chans * cells
    conv_scratch = [pltpu.VMEM((3 * chans, cells + 256), BF16)]

    first_core = core == 0
    mine, other = features[0], swap(features[0])
    own = jnp.concatenate(
        [
            jnp.where(first_core, mine[0], other[1]),
            jnp.where(first_core, other[0], mine[1]),
        ],
        axis=1,
    ).reshape(chans, cells)
    messages = call(
        enter_kernel, (rows_shape, rows_shape, stats_shape), [VM] * 3, [], 10_000_000
    )(own, gather, spread)

    given = (conv1_w, conv2_w, norm_gain, norm_shift, in_w, head_w, head_gain, head_shift)
    *given, latent, plan_pos, _ = lax.optimization_barrier((*given, latent, plan_pos, messages[2]))
    conv1_w, conv2_w, norm_gain, norm_shift, in_w, head_w, head_gain, head_shift = given
    params = jnp.stack(
        [x[0, k, q] for k in range(2) for q in range(2) for x in (norm_gain, norm_shift)]
        + [head_gain, head_shift]
        + [jnp.zeros((chans,), F32)] * 6
    ).T
    kernels = [
        call(
            functools.partial(pack_kernel, block),
            sds((chans, 9 * chans), BF16),
            [HB],
            [pltpu.VMEM(taps.shape[2:], BF16), pltpu.SemaphoreType.DMA(())],
            10_000_000,
        )(taps)
        for block in range(2)
        for taps in (conv1_w, conv2_w)
    ]
    head_packed = jnp.zeros((3, 3, 8, chans), BF16)
    head_packed = head_packed.at[:, :, :lat].set(
        jnp.transpose(head_w.reshape(3, 3, lat, chans), (1, 0, 2, 3))
    ).reshape(72, chans)
    in_packed = jnp.zeros((chans, 3, 3, 8), BF16)
    in_packed = in_packed.at[:, :, :, :lat].set(
        jnp.transpose(in_w.reshape(3, 3, chans, lat), (2, 0, 1, 3))
    ).reshape(chans, 72)
    mine = pick(latent, core)
    other = swap(pick(latent, 1 - core))
    latent_rows = jnp.concatenate(
        [jnp.where(core == 0, mine, other), jnp.where(core == 0, other, mine)], axis=1
    ).reshape(lat, cells)
    latent_rows = jnp.concatenate([jnp.zeros((8 - lat, cells), F32), latent_rows], axis=0)
    layouts = (by_core,) * (STEPS + 1)
    described = {by_core: describe(place, core), by_chips: describe(rank, group)}
    full_latent = None

    def exchange(layout, top_msg, bot_msg, st_msg):
        up = around(layout, bot_msg, 1)
        down = around(layout, top_msg, chips - 1)
        return up, down, [st_msg] + [around(layout, st_msg, d) for d in range(2, chips - 1)]

    for step in range(STEPS):
        first_step = step == 0
        before, layout = layouts[step], layouts[step + 1]
        ints = described[layout]
        own_next = onward(before, layout, own)
        up, down, others = exchange(before, *messages)
        height = 8 if first_step else lat
        extra = [latent_rows] if first_step else []
        early = []
        noise, forward = call(
            functools.partial(head_kernel, len(early)),
            (sds((height, cells + 256), F32), sds((chans + GROUPS + (rows + 2) // 2 * 32, 256), BF16)),
            [VM] * (6 + len(others) + len(extra)) + [HB] * len(early),
            [],
            300_000_000,
        )(params, own, up, down, head_packed, spread, *others, *extra, *early)
        parts = [to_first(before, layout, noise, d) for d in range(1, chips)]
        forward_next = onward(before, layout, forward)
        extra = []
        if not first_step:
            extra = [full_latent]
            if before is not layout:
                moves = [(before(m, l), layout(m, l)) for m, l in blocks]
                extra = [lax.ppermute(full_latent, "patch", moves)]
        middle, source, full_latent, lat_keep, lat_send, *messages = call(
            functools.partial(first_kernel, step, chips),
            (
                wide_shape,
                half_shape,
                sds((8, chips * cells), F32),
                sds((lat, half), F32),
                sds((lat, half), F32),
                rows_shape,
                rows_shape,
                stats_shape,
            ),
            [SM, SM] + [VM] * (6 + chips + len(extra)),
            conv_scratch
            + [
                pltpu.VMEM((chans, cells + 256), BF16),
                pltpu.VMEM((chans, 256), F32),
                pltpu.VMEM((8, chips * cells + 256), F32),
                pltpu.VMEM((24, chips * cells + 256), F32),
                pltpu.VMEM((chans, chips * cells + 256), BF16),
            ],
            conv_flops,
        )(
            ints,
            plan_pos,
            params,
            *parts,
            *extra,
            in_packed,
            own_next,
            forward_next,
            kernels[0],
            gather,
            spread,
        )

        if step == STEPS - 1:
            latents = call(
                pair_kernel, sds((CORES * lat, half), F32), [SM, VM, VM], [], 100_000
            )(ints, lat_keep, swap(lat_send))
            shares = [latents] + [
                lax.ppermute(
                    latents, "segment", [(q, (q + s) % sections) for q in range(sections)]
                )
                for s in range(1, sections)
            ]

        def conv(index, own, messages, base, last=False):
            up, down, others = exchange(layout, *messages)
            extra = [] if base is None else [base]
            return call(
                functools.partial(conv_kernel, index, base is not None, last),
                (
                    (half_shape,)
                    if last == "final"
                    else (wide_shape if base is None else half_shape, rows_shape, rows_shape, stats_shape)
                ),
                [SM] + [VM] * (7 + len(extra) + len(others)),
                conv_scratch,
                conv_flops,
            )(ints, params, own, up, down, kernels[index], gather, spread, *extra, *others)

        one, *messages = conv(1, middle, messages, source)
        middle, *messages = conv(2, one, messages, None)
        own, *messages = conv(
            3, middle, messages, one, "final" if step == STEPS - 1 else "last"
        )

    own, *shares = lax.optimization_barrier((own, *shares))
    low, high = own[:, :half], own[:, half:]
    mine = jnp.where(first_core, low, high)
    other = swap(jnp.where(first_core, high, low))
    pair = jnp.where(first_core, jnp.stack([mine, other]), jnp.stack([other, mine]))
    features_out = pair.reshape(1, batch, chans, own_rows, cols)
    share = cols // sections
    latent_out = None
    for s, piece in enumerate(shares):
        piece = piece.reshape(batch, lat, own_rows, cols)[..., s * share : (s + 1) * share]
        latent_out = piece if latent_out is None else jnp.where(section == s, piece, latent_out)
    return (latent_out, features_out)


def solution(mesh):
    placed = (
        P("segment", None, None, "patch", None),
        P(None, None, "patch", None),
        P(),
        P("segment"),
        P("segment", None, None, None, None),
        P("segment", None, None, None, None),
        P("segment", None, None, None),
        P("segment", None, None, None),
        P(),
        P(),
        P(),
        P(),
    )
    return jax.shard_map(
        per_device,
        mesh=mesh,
        in_specs=placed,
        out_specs=(P(None, None, "patch", "segment"), P("segment", None, None, "patch", None)),
        check_vma=False,
    )
```

```python
import functools

import jax
import jax.numpy as jnp
import numpy as np
from jax import lax
from jax.experimental import pallas as pl
from jax.experimental.pallas import tpu as pltpu
from jax.sharding import PartitionSpec as P

GROUPS = 32
STEPS = 2
SCHED = 12
CORES = 2

epsilon = 1e-05
sigma_top = 3.0
sigma_low = 0.1
rho_power = 7.0

F32 = jnp.float32
BF16 = jnp.bfloat16
VMEM_LIMIT = 24 * 1024 * 1024


def sigma_at(position):
    fraction = position / (SCHED - 1)
    top_root = sigma_top ** (1.0 / rho_power)
    low_root = sigma_low ** (1.0 / rho_power)
    base = top_root + fraction * (low_root - top_root)
    square = base * base
    return base * square * (square * square)


def dot(a, b):
    return lax.dot_general(a, b, (((1,), (0,)), ((), ())), preferred_element_type=F32)


def split3(x):
    hi = x.astype(BF16)
    rest = x - hi.astype(F32)
    mid = rest.astype(BF16)
    lo = (rest - mid.astype(F32)).astype(BF16)
    return hi, mid, lo


def group_lanes(x, gather):
    return dot(gather, jnp.concatenate(split3(x)[:2], axis=0))


def group_sum(x, gather):
    return jnp.sum(group_lanes(x, gather), axis=1, keepdims=True)


def expand(x, spread):
    return dot(spread, jnp.concatenate(split3(x), axis=0))


def tile_sum(tiles):
    total = tiles[0]
    for tile in tiles[1:]:
        total = total + tile
    return total


def pivot_of(tiles, gather, spread, count):
    mean = group_sum(tile_sum(tiles), gather) / (count * len(tiles))
    return mean, expand(jnp.broadcast_to(mean, (GROUPS, 128)), spread)


def add_deviations(sums, tiles, center):
    first, second = sums
    for tile in tiles:
        dev = tile - center
        first = dev if first is None else first + dev
        second = dev * dev if second is None else second + dev * dev
    return first, second


def finish_stats(pivot, sums, gather, count):
    wide = group_lanes(jnp.concatenate(sums, axis=1), gather)
    first = jnp.sum(wide[:, :128], axis=1, keepdims=True)
    second = jnp.sum(wide[:, 128:], axis=1, keepdims=True)
    return pivot + first / count, jnp.maximum(second - first * first / count, 0.0)


def encode_stats(mean, square):
    lane = lax.broadcasted_iota(jnp.int32, (GROUPS, 128), 1) // 16
    out = jnp.zeros((GROUPS, 128), F32)
    for slot, part in enumerate(split3(mean) + split3(square)):
        out = jnp.where(lane == slot, part.astype(F32), out)
    return out.astype(BF16)


def decode_stats(message):
    wide = message.astype(F32)
    take = [wide[:, 16 * k : 16 * k + 1] for k in range(6)]
    return take[0] + take[1] + take[2], take[3] + take[4] + take[5]


def combine_stats(messages, count):
    pairs = [decode_stats(m) for m in messages]
    mean = sum(p[0] for p in pairs) / len(pairs)
    square = sum(p[1] for p in pairs)
    for p in pairs:
        square = square + count * (p[0] - mean) * (p[0] - mean)
    return mean, lax.rsqrt(square / (count * len(pairs)) + epsilon)


def channel_moments(mean, scale, spread):
    both = jnp.concatenate(
        [jnp.broadcast_to(mean, (GROUPS, 128)), jnp.broadcast_to(scale, (GROUPS, 128))], axis=1
    )
    wide = expand(both, spread)
    return wide[:, :128], wide[:, 128:]


def silu(v):
    half = 0.5 * v
    return half + half * jnp.tanh(half)


def shift_cols(t):
    lane = lax.broadcasted_iota(jnp.int32, t.shape, 1)
    before = jnp.where(lane == 0, 0.0, pltpu.roll(t, 1, 1))
    after = jnp.where(lane == 127, 0.0, pltpu.roll(t, 127, 1))
    return before, after


def fill_row(r, last, tile, moments, flags, patches):
    center, scale, shift = moments
    chans = center.shape[0]
    main = chans // 128 * 128
    tail = chans - main
    t = silu((tile - center) * scale + shift)
    if r == 0:
        t = jnp.where(flags[0] > 0, t, 0.0)
    if r == last:
        t = jnp.where(flags[1] > 0, t, 0.0)
    before, after = shift_cols(t)
    lanes = pl.ds(r * 128, 128)
    for j, piece in enumerate((before, t, after)):
        piece = piece.astype(BF16)
        patches[pl.ds(j * main, main), lanes] = piece[:main]
        patches[pl.ds(3 * main + j * tail, tail), lanes] = piece[main:]


def conv_rows(patches, weight, start, rows):
    depth = weight.shape[1] // 9
    main = depth // 128 * 128
    parts = ((0, 3 * main), (3 * main, 3 * (depth - main)))
    pieces = [
        patches[pl.ds(low, size), pl.ds((start + i) * 128, rows * 128)]
        for low, size in parts
        for i in range(3)
    ]
    return dot(weight[...], jnp.concatenate(pieces, axis=0))


CHUNK = 4


def conv_all(tiles, moments, flags, patches, weight, store, gather=None, spread=None):
    rows = len(tiles) - 2
    chans = weight.shape[0]
    filled = 0
    per_row = count_of(chans, 128)
    sums = (None, None)
    for start in range(0, rows, CHUNK):
        while filled < start + CHUNK + 2:
            fill_row(filled, rows + 1, tiles[filled](), moments, flags, patches)
            filled += 1
        kept = store(start, CHUNK, conv_rows(patches, weight, start, CHUNK))
        if gather is None:
            continue
        kept = [kept[:, r * 128 : (r + 1) * 128] for r in range(CHUNK)]
        if start == 0:
            pivot, center = pivot_of(kept, gather, spread, per_row)
        sums = add_deviations(sums, kept, center)
    if gather is None:
        return None
    return encode_stats(*finish_stats(pivot, sums, gather, per_row * rows))


def write_messages(out, stats, top_msg, bot_msg, st_msg):
    chans, cells = out.shape
    st_msg[...] = stats
    for ref, start in ((top_msg, 0), (bot_msg, cells - 128)):
        ref[pl.ds(0, chans), :] = out[:, pl.ds(start, 128)].astype(BF16)
        ref[pl.ds(chans, GROUPS), :] = stats


def pack_kernel(block, taps_in, out, taps, sem):
    copy = pltpu.make_async_copy(taps_in.at[0, block], taps, sem)
    copy.start()
    copy.wait()
    chans = taps.shape[1]
    main = chans // 128 * 128
    tail = chans - main
    pieces = []
    for t in range(9):
        tap = taps[t]
        out[:, pl.ds(t * main, main)] = tap[:, :main]
        pieces.append(tap[:, main:])
    out[:, pl.ds(9 * main, 9 * tail)] = jnp.concatenate(pieces, axis=1)


def count_of(chans, cells):
    return float(chans // GROUPS * cells)


def row_tile(ref, r):
    return lambda: ref[:, pl.ds(r * 128, 128)].astype(F32)


def enter_kernel(own, gather, spread, top_msg, bot_msg, st_msg):
    chans, cells = own.shape
    tiles = [own[:, pl.ds(start, 128)].astype(F32) for start in range(0, cells, 128)]
    per_row = count_of(chans, 128)
    pivot, center = pivot_of(tiles[:2], gather[...], spread[...], per_row)
    sums = add_deviations((None, None), tiles, center)
    stats = encode_stats(*finish_stats(pivot, sums, gather[...], per_row * len(tiles)))
    write_messages(own, stats, top_msg, bot_msg, st_msg)


def pair_kernel(ints, kept, other, out):
    lat = kept.shape[0]
    first = ints[5] == 0
    out[0:lat, :] = jnp.where(first, kept[...], other[...])
    out[lat:, :] = jnp.where(first, other[...], kept[...])


def column(params, k):
    return params[:, k : k + 1]


def gathered(up, down, others, count):
    chans = up.shape[0] - GROUPS
    messages = [up[pl.ds(chans, GROUPS), :], down[pl.ds(chans, GROUPS), :]]
    return combine_stats(messages + [ref[...] for ref in others], count)


def head_kernel(early, params, own, up, down, weight, spread, *rest):
    others, (out, forward) = rest[: len(rest) - 2 - early], rest[-2:]
    latent = None
    if out.shape[0] == 8:
        others, latent = others[:-1], others[-1]
    chans, cells = own.shape
    rows = cells // 128
    mean, root = gathered(up, down, others, count_of(chans, cells))
    stats = encode_stats(mean, root)
    for ref, low in ((up, 0), (down, 128)):
        forward[pl.ds(0, chans), pl.ds(low, 128)] = ref[pl.ds(0, chans), :]
        forward[pl.ds(chans, GROUPS), pl.ds(low, 128)] = stats
    center, scale = channel_moments(mean, root, spread[...])
    scale = scale * column(params, 8)
    shift = column(params, 9)
    tiles = [row_tile(own, r) for r in range(rows)]
    sums = []
    for tile in tiles:
        act = silu((tile() - center) * scale + shift).astype(BF16)
        y = dot(weight[...], act)
        before, _ = shift_cols(y[0:24])
        _, after = shift_cols(y[48:72])
        sums.append(before + y[24:48] + after)
    for r in range(-1, rows + 1):
        acc = jnp.zeros((8, 128), F32)
        for i in range(3):
            if 0 <= r + i - 1 < rows:
                acc = acc + sums[r + i - 1][8 * i : 8 * i + 8]
        if latent is not None and 0 <= r < rows:
            acc = acc + latent[:, pl.ds(r * 128, 128)]
        out[:, pl.ds((r + 1) * 128, 128)] = acc[: out.shape[0]]
        coded = [part.astype(F32) for part in split3(acc)] + [jnp.zeros((8, 128), F32)]
        begin = chans + GROUPS + (r + 1) // 2 * 32
        forward[pl.ds(begin, 32), pl.ds((r + 1) % 2 * 128, 128)] = jnp.concatenate(
            coded, axis=0
        ).astype(BF16)


def first_kernel(step, chips, ints, plan, params, *rest):
    first_step = step == 0
    parts, rest = rest[: chips - 1], rest[chips - 1 :]
    if not first_step:
        latent_in, rest = rest[0], rest[1:]
    in_weight, own, forward, weight, gather, spread = rest[:6]
    out, source, latent_out, lat_keep, lat_send, top_msg, bot_msg, st_msg = rest[6:14]
    patches, wide, moments, noise, field, entry = rest[14:]
    chans, cells = own.shape
    rows = cells // 128
    full = chips * rows
    flags = (ints[0], ints[1])
    section, place = ints[2], ints[3]

    @pl.when(section == 0)
    def _():
        noise[...] = jnp.zeros_like(noise)
        for d in range(chips):
            owner = lax.rem(place - d + chips, chips)
            lanes = pl.ds(pl.multiple_of(owner * cells, 128), cells + 256)
            if d > 0:
                height = parts[d - 1].shape[0]
                noise[:height, lanes] = noise[:height, lanes] + parts[d - 1][...]
                continue
            for r in range(rows + 2):
                begin = chans + GROUPS + r // 2 * 32
                coded = forward[pl.ds(begin, 32), pl.ds(r % 2 * 128, 128)].astype(F32)
                spot = pl.ds(pl.multiple_of(owner * cells + r * 128, 128), 128)
                noise[:, spot] = noise[:, spot] + coded[0:8] + coded[8:16] + coded[16:24]
        position = jnp.broadcast_to(plan[ints[6]] + step, (8, 128)).astype(F32)
        later = sigma_at(position + 1.0)
        change = later - sigma_at(position)
        shrink = lax.rsqrt(later * later + 1.0)
        for edge in (0, (full + 1) * 128):
            field[:, pl.ds(edge, 128)] = jnp.zeros((24, 128), F32)
        for r in range(full):
            piece = noise[:, pl.ds((r + 1) * 128, 128)]
            if first_step:
                old = pltpu.roll(piece, 4, 0)
            else:
                old = latent_in[:, pl.ds(r * 128, 128)]
            new = old + change * piece
            latent_out[:, pl.ds(r * 128, 128)] = new
            scaled = (new * shrink).astype(BF16).astype(F32)
            before, after = shift_cols(scaled)
            lanes = pl.ds((r + 1) * 128, 128)
            field[pl.ds(0, 8), lanes] = before
            field[pl.ds(8, 8), lanes] = scaled
            field[pl.ds(16, 8), lanes] = after
        half = cells // CORES
        for ref, which in ((lat_keep, ints[5]), (lat_send, 1 - ints[5])):
            begin = pl.multiple_of(place * cells + which * half, 128)
            ref[...] = latent_out[: ref.shape[0], pl.ds(begin, half)]
        sums = (None, None)
        per_row = count_of(chans, 128)
        for z in range(chips):
            taps = [field[:, pl.ds((z * rows + i) * 128, cells)] for i in range(3)]
            rows_out = dot(in_weight[...], jnp.concatenate(taps, axis=0).astype(BF16)).astype(BF16)
            entry[:, pl.ds(z * cells + 128, cells)] = rows_out
            kept = [rows_out[:, r * 128 : (r + 1) * 128].astype(F32) for r in range(rows)]
            if z == 0:
                pivot, center = pivot_of(kept[:2], gather[...], spread[...], per_row)
            sums = add_deviations(sums, kept, center)
        entry[:, pl.ds(0, 128)] = jnp.zeros((chans, 128), BF16)
        entry[:, pl.ds(full * 128 + 128, 128)] = jnp.zeros((chans, 128), BF16)
        count = per_row * full
        mean, square = finish_stats(pivot, sums, gather[...], count)
        scale = lax.rsqrt(square / count + epsilon)
        moments[:, 0:128], moments[:, 128:256] = channel_moments(mean, scale, spread[...])
        wide[...] = entry[:, pl.ds(pl.multiple_of(place * cells, 128), cells + 256)]

    @pl.when(section != 0)
    def _():
        latent_out[...] = jnp.zeros_like(latent_out)
        lat_keep[...] = jnp.zeros_like(lat_keep)
        lat_send[...] = jnp.zeros_like(lat_send)
        mean, scale = decode_stats(forward[pl.ds(chans, GROUPS), pl.ds(0, 128)])
        moments[:, 0:128], moments[:, 128:256] = channel_moments(mean, scale, spread[...])
        wide[:, pl.ds(0, 128)] = forward[pl.ds(0, chans), pl.ds(0, 128)]
        wide[:, pl.ds(128, cells)] = own[...]
        wide[:, pl.ds(cells + 128, 128)] = forward[pl.ds(0, chans), pl.ds(128, 128)]

    source[...] = wide[:, pl.ds(128, cells)]
    tiles = [row_tile(wide, r) for r in range(rows + 2)]
    known = (moments[:, 0:128], moments[:, 128:256] * column(params, 0), column(params, 1))

    def store(start, count, acc):
        out[:, pl.ds(start * 128, count * 128)] = acc
        return acc

    stats_out = conv_all(tiles, known, flags, patches, weight, store, gather[...], spread[...])
    write_messages(out, stats_out, top_msg, bot_msg, st_msg)


def conv_kernel(index, residual, last, ints, params, own, up, down, weight, gather, spread, *rest):
    rest = list(rest)
    base = rest.pop(0) if residual else None
    patches = rest.pop()
    final = last == "final"
    given = 1 if final else 4
    others, outs = rest[:-given], rest[-given:]
    out = outs[0]
    chans, cells = own.shape
    rows = cells // 128
    mean, root = gathered(up, down, others, count_of(chans, cells))
    center, scale = channel_moments(mean, root, spread[...])
    tiles = [lambda: up[pl.ds(0, chans), :].astype(F32)]
    tiles += [row_tile(own, r) for r in range(rows)]
    tiles += [lambda: down[pl.ds(0, chans), :].astype(F32)]
    known = (center, scale * column(params, 2 * index), column(params, 2 * index + 1))

    def store(start, count, acc):
        lanes = pl.ds(start * 128, count * 128)
        if residual:
            old = base[:, lanes].astype(F32)
            acc = (old + acc).astype(BF16).astype(F32)
        if last:
            acc = jnp.where(ints[4] >= 2, acc, old)
        out[:, lanes] = acc.astype(out.dtype)
        return acc

    sums = () if final else (gather[...], spread[...])
    stats_out = conv_all(tiles, known, (ints[0], ints[1]), patches, weight, store, *sums)
    if not final:
        write_messages(out, stats_out, *outs[1:])


VM = pl.BlockSpec(memory_space=pltpu.VMEM)
SM = pl.BlockSpec(memory_space=pltpu.SMEM)
HB = pl.BlockSpec(memory_space=pl.ANY)


def call(kernel, outs, in_specs, scratch, flops):
    return pl.pallas_call(
        kernel,
        out_shape=outs,
        in_specs=in_specs,
        out_specs=jax.tree.map(lambda _: VM, outs),
        scratch_shapes=scratch,
        compiler_params=pltpu.CompilerParams(vmem_limit_bytes=VMEM_LIMIT),
        cost_estimate=pl.CostEstimate(flops=flops, bytes_accessed=4_000_000, transcendentals=0),
    )


def sds(shape, dtype):
    return jax.ShapeDtypeStruct(shape, dtype)


def per_device(
    features,
    latent,
    plan_pos,
    blocks_used,
    conv1_w,
    conv2_w,
    norm_gain,
    norm_shift,
    in_w,
    head_w,
    head_gain,
    head_shift,
):
    sections = lax.axis_size("segment")
    patches = lax.axis_size("patch")
    chips = patches // CORES
    section = lax.axis_index("segment")
    core = lax.rem(lax.axis_index("patch"), CORES)
    place = lax.axis_index("patch") // CORES
    _, batch, chans, own_rows, cols = features.shape
    rows = CORES * own_rows
    half = own_rows * cols
    cells = rows * cols
    joint = ("segment", "patch")

    swap_pairs = [(p, p ^ 1) for p in range(patches)]

    def swap(x):
        return lax.ppermute(x, "patch", swap_pairs)

    def by_core(m, l):
        return CORES * (l % chips) + m

    def by_chips(m, l):
        return m * chips + ((l % chips) ^ ((l % chips) >> 1))

    blocks = [(m, l) for m in range(CORES) for l in range(chips)]

    def around(layout, x, by):
        return lax.ppermute(x, "patch", [(layout(m, l), layout(m, l + by)) for m, l in blocks])

    def onward(source, target, x):
        pairs = [
            (s * patches + source(m, l), (s + 1) % sections * patches + target(m, l))
            for s in range(sections)
            for m, l in blocks
        ]
        return lax.ppermute(x, joint, pairs)

    def to_first(source, target, x, by):
        pairs = [
            (s * patches + source(m, l), (s + 1) % sections * patches + target(m, l + by))
            for s in range(sections)
            for m, l in blocks
        ]
        return lax.ppermute(x, joint, pairs)

    group_of = np.arange(chans) // (chans // GROUPS)
    member = (np.arange(GROUPS)[:, None] == group_of[None, :]).astype(np.float32)
    gather = jnp.asarray(np.tile(member, (1, 2)), BF16)
    spread = jnp.asarray(np.tile(member.T, (1, 3)), BF16)

    lat = latent.shape[1]
    group, rank = lax.axis_index("patch") // chips, lax.rem(lax.axis_index("patch"), chips)
    turn = 1
    while turn < chips:
        rank = rank ^ (rank >> turn)
        turn *= 2

    def describe(row_block, which):
        return jnp.stack(
            [
                (row_block > 0).astype(jnp.int32),
                (row_block < chips - 1).astype(jnp.int32),
                section.astype(jnp.int32),
                row_block.astype(jnp.int32),
                blocks_used[0],
                core.astype(jnp.int32),
                which.astype(jnp.int32),
            ]
        )

    def pick(x, which):
        return lax.dynamic_index_in_dim(x, which, 0, keepdims=False)

    stats_shape = sds((GROUPS, 128), BF16)
    rows_shape = sds((chans + GROUPS, 128), BF16)
    wide_shape = sds((chans, cells), F32)
    half_shape = sds((chans, cells), BF16)
    conv_flops = 2 * 9 * chans * chans * cells
    conv_scratch = [pltpu.VMEM((3 * chans, cells + 256), BF16)]

    first_core = core == 0
    mine, other = features[0], swap(features[0])
    own = jnp.concatenate(
        [
            jnp.where(first_core, mine[0], other[1]),
            jnp.where(first_core, other[0], mine[1]),
        ],
        axis=1,
    ).reshape(chans, cells)
    messages = call(
        enter_kernel, (rows_shape, rows_shape, stats_shape), [VM] * 3, [], 10_000_000
    )(own, gather, spread)

    given = (conv1_w, conv2_w, norm_gain, norm_shift, in_w, head_w, head_gain, head_shift)
    *given, latent, plan_pos, _ = lax.optimization_barrier((*given, latent, plan_pos, messages[2]))
    conv1_w, conv2_w, norm_gain, norm_shift, in_w, head_w, head_gain, head_shift = given
    params = jnp.stack(
        [x[0, k, q] for k in range(2) for q in range(2) for x in (norm_gain, norm_shift)]
        + [head_gain, head_shift]
        + [jnp.zeros((chans,), F32)] * 6
    ).T
    kernels = [
        call(
            functools.partial(pack_kernel, block),
            sds((chans, 9 * chans), BF16),
            [HB],
            [pltpu.VMEM(taps.shape[2:], BF16), pltpu.SemaphoreType.DMA(())],
            10_000_000,
        )(taps)
        for block in range(2)
        for taps in (conv1_w, conv2_w)
    ]
    head_packed = jnp.zeros((3, 3, 8, chans), BF16)
    head_packed = head_packed.at[:, :, :lat].set(
        jnp.transpose(head_w.reshape(3, 3, lat, chans), (1, 0, 2, 3))
    ).reshape(72, chans)
    in_packed = jnp.zeros((chans, 3, 3, 8), BF16)
    in_packed = in_packed.at[:, :, :, :lat].set(
        jnp.transpose(in_w.reshape(3, 3, chans, lat), (2, 0, 1, 3))
    ).reshape(chans, 72)
    mine = pick(latent, core)
    other = swap(pick(latent, 1 - core))
    latent_rows = jnp.concatenate(
        [jnp.where(core == 0, mine, other), jnp.where(core == 0, other, mine)], axis=1
    ).reshape(lat, cells)
    latent_rows = jnp.concatenate([jnp.zeros((8 - lat, cells), F32), latent_rows], axis=0)
    layouts = (by_core,) * (STEPS + 1)
    described = {by_core: describe(place, core), by_chips: describe(rank, group)}
    full_latent = None

    def exchange(layout, top_msg, bot_msg, st_msg):
        up = around(layout, bot_msg, 1)
        down = around(layout, top_msg, chips - 1)
        return up, down, [st_msg] + [around(layout, st_msg, d) for d in range(2, chips - 1)]

    for step in range(STEPS):
        first_step = step == 0
        before, layout = layouts[step], layouts[step + 1]
        ints = described[layout]
        own_next = onward(before, layout, own)
        up, down, others = exchange(before, *messages)
        height = 8 if first_step else lat
        extra = [latent_rows] if first_step else []
        early = []
        noise, forward = call(
            functools.partial(head_kernel, len(early)),
            (sds((height, cells + 256), F32), sds((chans + GROUPS + (rows + 2) // 2 * 32, 256), BF16)),
            [VM] * (6 + len(others) + len(extra)) + [HB] * len(early),
            [],
            300_000_000,
        )(params, own, up, down, head_packed, spread, *others, *extra, *early)
        parts = [to_first(before, layout, noise, d) for d in range(1, chips)]
        forward_next = onward(before, layout, forward)
        extra = []
        if not first_step:
            extra = [full_latent]
            if before is not layout:
                moves = [(before(m, l), layout(m, l)) for m, l in blocks]
                extra = [lax.ppermute(full_latent, "patch", moves)]
        middle, source, full_latent, lat_keep, lat_send, *messages = call(
            functools.partial(first_kernel, step, chips),
            (
                wide_shape,
                half_shape,
                sds((8, chips * cells), F32),
                sds((lat, half), F32),
                sds((lat, half), F32),
                rows_shape,
                rows_shape,
                stats_shape,
            ),
            [SM, SM] + [VM] * (6 + chips + len(extra)),
            conv_scratch
            + [
                pltpu.VMEM((chans, cells + 256), BF16),
                pltpu.VMEM((chans, 256), F32),
                pltpu.VMEM((8, chips * cells + 256), F32),
                pltpu.VMEM((24, chips * cells + 256), F32),
                pltpu.VMEM((chans, chips * cells + 256), BF16),
            ],
            conv_flops,
        )(
            ints,
            plan_pos,
            params,
            *parts,
            *extra,
            in_packed,
            own_next,
            forward_next,
            kernels[0],
            gather,
            spread,
        )

        if step == STEPS - 1:
            latents = call(
                pair_kernel, sds((CORES * lat, half), F32), [SM, VM, VM], [], 100_000
            )(ints, lat_keep, swap(lat_send))
            shares = [latents] + [
                lax.ppermute(
                    latents, "segment", [(q, (q + s) % sections) for q in range(sections)]
                )
                for s in range(1, sections)
            ]

        def conv(index, own, messages, base, last=False):
            up, down, others = exchange(layout, *messages)
            extra = [] if base is None else [base]
            return call(
                functools.partial(conv_kernel, index, base is not None, last),
                (
                    (half_shape,)
                    if last == "final"
                    else (wide_shape if base is None else half_shape, rows_shape, rows_shape, stats_shape)
                ),
                [SM] + [VM] * (7 + len(extra) + len(others)),
                conv_scratch,
                conv_flops,
            )(ints, params, own, up, down, kernels[index], gather, spread, *extra, *others)

        one, *messages = conv(1, middle, messages, source)
        middle, *messages = conv(2, one, messages, None)
        own, *messages = conv(
            3, middle, messages, one, "final" if step == STEPS - 1 else "last"
        )

    own, *shares = lax.optimization_barrier((own, *shares))
    low, high = own[:, :half], own[:, half:]
    other = swap(own)
    pair = jnp.stack(
        [
            jnp.where(first_core, low, other[:, half:]),
            jnp.where(first_core, other[:, :half], high),
        ]
    )
    features_out = pair.reshape(1, batch, chans, own_rows, cols)
    share = cols // sections
    latent_out = None
    for s, piece in enumerate(shares):
        piece = piece.reshape(batch, lat, own_rows, cols)[..., s * share : (s + 1) * share]
        latent_out = piece if latent_out is None else jnp.where(section == s, piece, latent_out)
    return (latent_out, features_out)


def solution(mesh):
    placed = (
        P("segment", None, None, "patch", None),
        P(None, None, "patch", None),
        P(),
        P("segment"),
        P("segment", None, None, None, None),
        P("segment", None, None, None, None),
        P("segment", None, None, None),
        P("segment", None, None, None),
        P(),
        P(),
        P(),
        P(),
    )
    return jax.shard_map(
        per_device,
        mesh=mesh,
        in_specs=placed,
        out_specs=(P(None, None, "patch", "segment"), P("segment", None, None, "patch", None)),
        check_vma=False,
    )
```
